32 devices in a mesh: dp: 8 (over z, x), tensor: 4 (over y, core).
Axes of the slice: x: 2, y: 2, z: 4, core: 2. Of those that a mesh axis runs over, the one named last changes fastest.
Arguments:
- tokens: bfloat16 [16, 1024, 768], P('dp'), may hold values from -6 to 6
- segments: int32 [16, 1024], P('dp'), may hold values from 0 to 7, never falling along the last dimension, each value on 1 to 512 neighbouring positions
- cotangent: bfloat16 [16, 1024, 768], P('dp'), may hold values from -6 to 6
- block_owner_slots: int32 [4, 48], P('tensor'), may hold values from 0 to 47, as said below
- master_weights: float32 [4, 48, 192, 192], P('tensor', 'dp')
- statistics: float32 [4, 48, 2, 192, 192], P('tensor', 'dp')
- inverse_roots: float32 [4, 48, 2, 192, 192], P('tensor', 'dp')
- shared_vectors: float32 [6, 768], replicated
- shared_state: float32 [6, 768], replicated, may hold values from 1e-07 to 2e-06
- split_bias: float32 [4, 1344], P('tensor'), may hold values from -1.2 to 1.2
- split_state: float32 [4, 1344], P('tensor'), may hold values from 1e-07 to 2e-06
Outputs:
- output: float32 [16, 1024, 768], P('dp')
- input_grad: float32 [16, 1024, 768], P('dp')
- norm: float32 [], replicated
- clipped_grads: float32 [4, 48, 192, 192], P('tensor', 'dp')
- new_master: float32 [4, 48, 192, 192], P('tensor', 'dp')
- master_copy: bfloat16 [4, 48, 192, 192], P('tensor', 'dp')
- new_statistics: float32 [4, 48, 2, 192, 192], P('tensor', 'dp')
- shared_grad: float32 [6, 768], replicated
- shared_new_state: float32 [6, 768], replicated
- shared_new: float32 [6, 768], replicated
- split_grad: float32 [4, 1344], P('tensor')
- split_new_state: float32 [4, 1344], P('tensor')
- split_new: float32 [4, 1344], P('tensor')
The draws below stay inside these ranges and needn't reach their ends.
Inputs may be any that keep to these rules, and one draw needn't show every extreme that they name: `block_owner_slots`: row t gives each of the 48 blocks of tensor index t a distinct slot; slot s is held by data index s // 6; slots 0 and 47 are used in every row.
All inputs are finite; a program needn't handle non-finite values.
Results may differ from the reference program's by a relative error of at most 0.014.
Values may be sent and summed in bfloat16 or wider, within the bound.
A program may use at most 192 MiB of HBM per device.

```python
import math
from functools import partial
import jax
import jax.numpy as jnp
import numpy as np
from jax import lax

D = 768
HEAD = 64
FF = 3072
SEQ = 1024
SEQS = 16
BLOCK_ORDER = 192
TENSOR_BLOCKS = 48
BLOCK_SLOTS = 48
N_TENSOR = 4


def slot_table(key):
    keys = jax.random.split(key, N_TENSOR)

    def one_row(row_key):
        first_part, second = jax.random.split(row_key)
        middle_part = jax.random.permutation(first_part, BLOCK_SLOTS - 2).astype(jnp.int32) + 1
        chosen_items = jnp.concatenate([jnp.zeros((1,), jnp.int32), middle_part[:TENSOR_BLOCKS - 2], jnp.full((1,), BLOCK_SLOTS - 1, jnp.int32)])
        return chosen_items[jax.random.permutation(second, TENSOR_BLOCKS)]
    return jax.vmap(one_row)(keys)


def definite_draw(key, low_end, high_end, spread):
    first_part, second = jax.random.split(key)
    shape_tuple = (N_TENSOR, BLOCK_SLOTS, 2, BLOCK_ORDER, BLOCK_ORDER)
    diagonal = jnp.exp(jax.random.uniform(first_part, shape_tuple[:-1], jnp.float32, math.log(low_end), math.log(high_end)))
    noise_sample = spread * jax.random.truncated_normal(second, -4.0, 4.0, shape_tuple, jnp.float32)
    symmetric = (noise_sample + jnp.swapaxes(noise_sample, -1, -2)) * 0.5
    identity = jnp.eye(BLOCK_ORDER, dtype=jnp.float32)
    return symmetric * (1.0 - identity) + diagonal[..., None] * identity


def draw_block_owner_slots(key, part):
    return slot_table(key)


def draw_master_weights(key, part):
    lookup_table = slot_table(key)
    key = jax.random.fold_in(key, 5)
    rows = D // BLOCK_ORDER
    fold = FF // N_TENSOR // BLOCK_ORDER
    index = jnp.arange(TENSOR_BLOCKS)
    base_value = D ** (-0.5)
    scale_values = jnp.where(index < 3 * rows, base_value, jnp.where(index < 4 * rows, 6.0 * base_value, jnp.where(index < 4 * rows + rows * fold, base_value, FF ** (-0.5))))
    scale_per_slot = jax.vmap(lambda picked_items: jnp.full((BLOCK_SLOTS,), base_value, jnp.float32).at[picked_items].set(scale_values))(lookup_table)
    noise_sample = jax.random.truncated_normal(key, -4.0, 4.0, (N_TENSOR, BLOCK_SLOTS, BLOCK_ORDER, BLOCK_ORDER), jnp.float32)
    return noise_sample * scale_per_slot[:, :, None, None]


def draw_statistics(key, part):
    key = jax.random.fold_in(key, 3)
    return definite_draw(key, 8e-06, 3.2e-05, 2e-08)


def draw_inverse_roots(key, part):
    key = jax.random.fold_in(key, 4)
    return definite_draw(key, 10.0, 20.0, 5.3 * BLOCK_ORDER ** (-0.5))


def draw_shared_vectors(key, part):
    key = jax.random.fold_in(key, 7)
    gains = jax.random.uniform(key, (6, D), jnp.float32, 0.5, 1.5)
    shifts = 0.3 * jax.random.truncated_normal(jax.random.fold_in(key, 1), -3.0, 3.0, (6, D), jnp.float32)
    which = jnp.arange(6)[:, None]
    return jnp.where((which == 0) | (which == 2), gains, shifts)


def shard_levels(key, dims, cuts, smallest, top_value):
    def one(axis_at, blocks):
        heights = jax.random.uniform(jax.random.fold_in(jax.random.fold_in(key, 6), axis_at), (blocks,), jnp.float32, smallest / len(cuts), top_value / len(cuts))
        return jnp.repeat(jnp.exp(heights), dims[axis_at] // blocks).reshape((-1,) + (1,) * (len(dims) - axis_at - 1))

    level = one(*cuts[0])
    for cut in cuts[1:]:
        level = level * one(*cut)
    return level


def profile(number_of, total, limit, skew):
    portions = [(1 << 20) // math.isqrt(grade ** skew) + 1 for grade in range(2, number_of + 1)]
    spare, holding = total - limit - (number_of - 1), [1] * (number_of - 1)
    while spare > 0:
        free = [i for i in range(number_of - 1) if holding[i] < limit]
        whole, remaining = sum([portions[i] for i in free]), spare
        for i in free:
            more = min(limit - holding[i], max(1, remaining * portions[i] // whole), spare)
            holding[i] = holding[i] + more
            spare = spare - more
    return np.array([limit] + holding)


def ragged_sizes(rng, count, total, bound, lean):
    if count == 2:
        one = jax.random.randint(rng, (), max(1, total - bound), min(bound, total - 1) + 1)
        return jnp.stack([one, total - one])
    sizes = jnp.asarray(profile(count, total, bound, lean), jnp.int32)
    twos = (count - 1) // 2
    donor, taker = sizes[1:1 + 2 * twos:2], sizes[2:2 + 2 * twos:2]
    margin = jnp.minimum(donor - 1, bound - taker)
    shifted = jax.random.randint(jax.random.fold_in(rng, 1), (twos,), 0, 1 << 20) % (margin + 1)
    sizes = sizes.at[1:1 + 2 * twos:2].set(donor - shifted).at[2:2 + 2 * twos:2].set(taker + shifted)
    return sizes[jax.random.permutation(jax.random.fold_in(rng, 2), count)]


def normal_values(stream_key, extent, scale, most, pieces=(), kind=jnp.bfloat16):
    entries = jax.random.normal(stream_key, extent, jnp.float32) * scale
    if len(pieces) > 0:
        entries = shard_levels(stream_key, extent, pieces, -0.22, 0.18) * entries
    return jnp.clip(entries, min=-most, max=most).astype(kind)


def setup_inputs(seed: int = 0) -> dict:
    seeds = jax.random.split(jax.random.key(seed), 12)
    tokens = normal_values(seeds[0], (SEQS, SEQ, D), 1.0, 6.0, ((0, 8),))
    segments = jax.vmap(lambda own: jnp.searchsorted(jnp.cumsum(ragged_sizes(own, max(3, SEQ // 128), SEQ, SEQ // 2, 2)), jnp.arange(SEQ), side="right"))(jax.random.split(seeds[1], SEQS)).reshape((SEQS, SEQ)).astype(jnp.int32)
    cotangent = normal_values(seeds[2], (SEQS, SEQ, D), 1.0, 6.0, ((0, 8),))
    block_owner_slots = draw_block_owner_slots(jax.random.fold_in(seeds[11], 71), 0)
    master_weights = draw_master_weights(jax.random.fold_in(seeds[11], 71), 0)
    statistics = draw_statistics(jax.random.fold_in(seeds[11], 71), 0)
    inverse_roots = draw_inverse_roots(jax.random.fold_in(seeds[11], 71), 0)
    shared_vectors = draw_shared_vectors(jax.random.fold_in(seeds[11], 71), 0)
    shared_state = jnp.clip(jnp.exp(jax.random.uniform(seeds[8], (6, D), jnp.float32, math.log(1.0000000116860974e-07), math.log(1.9999999949504854e-06))), 1.0000000116860974e-07, 1.9999999949504854e-06)
    split_bias = normal_values(seeds[9], (N_TENSOR, 3 * BLOCK_ORDER + FF // N_TENSOR), 0.3, 1.2, ((0, 4),), jnp.float32)
    split_state = jnp.clip(jnp.exp(math.log(1.9999999949504854e-06) - 2.9957323 * jax.random.uniform(seeds[10], (N_TENSOR, 3 * BLOCK_ORDER + FF // N_TENSOR), jnp.float32) ** shard_levels(seeds[10], (N_TENSOR, 3 * BLOCK_ORDER + FF // N_TENSOR), ((0, 4),), -0.2, 0.2)), 1.0000000116860974e-07, 1.9999999949504854e-06)
    return dict(tokens=tokens, segments=segments, cotangent=cotangent, block_owner_slots=block_owner_slots, master_weights=master_weights, statistics=statistics, inverse_roots=inverse_roots, shared_vectors=shared_vectors, shared_state=shared_state, split_bias=split_bias, split_state=split_state)


EPS = 1e-05
NEG = -1000000000.0
DECAY = 0.5
RATE = 0.3
RATE_VECTOR = 0.2
HIGH = lax.Precision.HIGHEST

@jax.custom_vjp
def low(v):
    return lax.optimization_barrier(v.astype(jnp.bfloat16)).astype(jnp.float32)

@jax.custom_vjp
def low_back(v):
    return v

def low_keep(v):
    return (low(v), None)

def low_pass(kept, grad):
    return (grad,)

def back_keep(v):
    return (v, None)

def back_low(kept, grad):
    return (low(grad),)
low.defvjp(low_keep, low_pass)
low_back.defvjp(back_keep, back_low)

def layer_norm(value, gain, shift):
    mean = lax.optimization_barrier(jnp.mean(value, -1, keepdims=True))
    centred = value - mean
    spread = lax.optimization_barrier(jnp.mean(centred * centred, -1, keepdims=True))
    return centred * lax.rsqrt(spread + EPS) * gain + shift

def to_blocks(matrix, size):
    rows = matrix.shape[0] // size
    cols = matrix.shape[1] // size
    return matrix.reshape(rows, size, cols, size).transpose(0, 2, 1, 3).reshape(rows * cols, size, size)

def from_blocks(blocks, rows, cols):
    size = blocks.shape[-1]
    return blocks.reshape(rows, cols, size, size).transpose(0, 2, 1, 3).reshape(rows * size, cols * size)

def forward(seg, inputs, w_qkv, w_out, w_fc, w_proj, shared, split):
    heads = BLOCK_ORDER // HEAD
    gain1, shift1, gain2, shift2, out_bias, proj_bias = (shared[0], shared[1], shared[2], shared[3], shared[4], shared[5])
    qkv_bias = split[:, :3 * BLOCK_ORDER]
    fc_bias = split[:, 3 * BLOCK_ORDER:]
    h_one = low(layer_norm(inputs, gain1, shift1))
    qkv = jnp.einsum('sd,rdc->rsc', h_one, w_qkv, precision=HIGH) + qkv_bias[:, None, :]
    qkv = low(low_back(qkv)).reshape(N_TENSOR, SEQ, 3, heads, HEAD)
    query, keys, values = (qkv[:, :, 0], qkv[:, :, 1], qkv[:, :, 2])
    places = jnp.arange(SEQ)
    allowed = (seg[:, None] == seg[None, :]) & (places[None, :] <= places[:, None])
    scores = low_back(jnp.einsum('rqhe,rkhe->rhqk', query, keys, precision=HIGH) * HEAD ** (-0.5))
    scores = jnp.where(allowed, scores, NEG)
    top = lax.optimization_barrier(jnp.max(scores, -1, keepdims=True))
    expo = jnp.exp(scores - top)
    probs = low(expo / lax.optimization_barrier(jnp.sum(expo, -1, keepdims=True)))
    mixed = jnp.einsum('rhqk,rkhe->rqhe', probs, values, precision=HIGH)
    mixed = low(low_back(mixed)).reshape(N_TENSOR, SEQ, BLOCK_ORDER)
    attn = low_back(jnp.einsum('rsc,rcd->sd', mixed, w_out, precision=HIGH) + out_bias)
    second = inputs + attn
    h_two = low(layer_norm(second, gain2, shift2))
    hidden = low_back(jnp.einsum('sd,rdf->rsf', h_two, w_fc, precision=HIGH) + fc_bias[:, None, :])
    gelu_out = low(jax.nn.gelu(hidden, approximate=True))
    branch = low_back(jnp.einsum('rsf,rfd->sd', gelu_out, w_proj, precision=HIGH) + proj_bias)
    return second + branch

def reference(tokens, segments, cotangent, block_owner_slots, master_weights, statistics, inverse_roots, shared_vectors, shared_state, split_bias, split_state):
    copies = master_weights.astype(jnp.bfloat16).astype(jnp.float32)
    blocks = jax.vmap(lambda mats, picked_items: mats[picked_items])(copies, block_owner_slots)
    rows = D // BLOCK_ORDER
    fold = FF // N_TENSOR // BLOCK_ORDER
    cut_a = 3 * rows
    cut_b = cut_a + rows
    cut_c = cut_b + rows * fold
    w_qkv = jax.vmap(lambda piece_list: from_blocks(piece_list[:cut_a], rows, 3))(blocks)
    w_out = jax.vmap(lambda piece_list: from_blocks(piece_list[cut_a:cut_b], 1, rows))(blocks)
    w_fc = jax.vmap(lambda piece_list: from_blocks(piece_list[cut_b:cut_c], rows, fold))(blocks)
    w_proj = jax.vmap(lambda piece_list: from_blocks(piece_list[cut_c:], fold, rows))(blocks)
    params = (w_qkv, w_out, w_fc, w_proj, shared_vectors, split_bias)

    def one_sequence(carry, item):
        inputs, seg, cot = item
        result, back = jax.vjp(partial(forward, seg), inputs.astype(jnp.float32), *params)
        grads = back(cot.astype(jnp.float32))
        carry = tuple((total + extra for total, extra in zip(carry, grads[1:])))
        return (carry, (result, grads[0]))
    start = tuple((jnp.zeros_like(param) for param in params))
    totals, (output, input_grad) = lax.scan(one_sequence, start, (tokens, segments, cotangent))
    d_qkv, d_out, d_fc, d_proj, shared_raw, split_raw = totals
    cutter = jax.vmap(partial(to_blocks, size=BLOCK_ORDER))
    gradient_blocks = jnp.concatenate([cutter(d_qkv), cutter(d_out), cutter(d_fc), cutter(d_proj)], 1)
    laid_out = jax.vmap(lambda picked_items, piece_list: jnp.zeros((BLOCK_SLOTS, BLOCK_ORDER, BLOCK_ORDER), piece_list.dtype).at[picked_items].set(piece_list))(block_owner_slots, gradient_blocks)
    square = jnp.sum(laid_out * laid_out) + jnp.sum(shared_raw * shared_raw) + jnp.sum(split_raw * split_raw)
    norm = jnp.sqrt(square)
    factor = 1.0 / jnp.maximum(norm, 1.0)
    clipped = laid_out * factor
    left = DECAY * statistics[:, :, 0] + (1.0 - DECAY) * jnp.einsum('tsij,tskj->tsik', clipped, clipped, precision=HIGH)
    right = DECAY * statistics[:, :, 1] + (1.0 - DECAY) * jnp.einsum('tsji,tsjk->tsik', clipped, clipped, precision=HIGH)
    step = jnp.einsum('tsij,tsjk->tsik', inverse_roots[:, :, 0], clipped, precision=HIGH)
    step = jnp.einsum('tsij,tsjk->tsik', step, inverse_roots[:, :, 1], precision=HIGH)
    new_master = master_weights - RATE * step
    shared_grad = shared_raw * factor
    shared_new_state = DECAY * shared_state + (1.0 - DECAY) * shared_grad * shared_grad
    shared_new = shared_vectors - RATE_VECTOR * shared_grad * lax.rsqrt(shared_new_state)
    split_grad = split_raw * factor
    split_new_state = DECAY * split_state + (1.0 - DECAY) * split_grad * split_grad
    split_new = split_bias - RATE_VECTOR * split_grad * lax.rsqrt(split_new_state)
    return (output, input_grad, norm, clipped, new_master, new_master.astype(jnp.bfloat16), jnp.stack([left, right], 2), shared_grad, shared_new_state, shared_new, split_grad, split_new_state, split_new)
```

```python
import functools
import math

import jax
import jax.numpy as jnp
from jax import lax
from jax.sharding import PartitionSpec as P
import jax.experimental.pallas as pl
import jax.experimental.pallas.tpu as pltpu

MESH = pl.DeviceIdType.MESH
PAIR = 2
CORES = 2
LANES = 128
MIB = 2**20


def packed_rows(size):
    return size * size // LANES


def pack_block(block, size):
    half = size // 2
    left = block[:, :LANES]
    right = jnp.concatenate([block[:half, LANES:], block[half:, LANES:]], 1)
    return left, right


def place():
    d = lax.axis_index("dp")
    t = lax.axis_index("tensor")
    return d // PAIR, lax.rem(d, PAIR), t // CORES, lax.rem(t, CORES)


def device(a, b, y, c):
    return (a * PAIR + b, y * CORES + c)


def gather_kernel(line, size, w_ref, out_ref, own, sem_own, s_zr, s_zl, s_x, s_y, s_xy, s_yx, r_z, r_x, r_y, r_xy, r_yx):
    a, b, y, c = place()
    other_b, other_y = 1 - b, 1 - y
    slots = w_ref.shape[0]
    block_rows = packed_rows(size)
    rows = slots * block_rows
    half = rows // 2
    barrier = pltpu.get_barrier_semaphore()
    x_dev = device(a, other_b, y, c)
    y_dev = device(a, b, other_y, c)
    right = device(jnp.minimum(a + 1, line - 1), b, y, c)
    left = device(jnp.maximum(a - 1, 0), b, y, c)
    pl.semaphore_signal(barrier, inc=1, device_id=x_dev, device_id_type=MESH)
    pl.semaphore_signal(barrier, inc=1, device_id=y_dev, device_id_type=MESH)

    @pl.when(a < line - 1)
    def _():
        pl.semaphore_signal(barrier, inc=1, device_id=right, device_id_type=MESH)

    @pl.when(a > 0)
    def _():
        pl.semaphore_signal(barrier, inc=1, device_id=left, device_id_type=MESH)

    def pack(s, carry):
        left_part, right_part = pack_block(w_ref[s].astype(jnp.bfloat16), size)
        start = pl.multiple_of(s * block_rows, 32)
        own[pl.ds(start, size), :] = left_part
        own[pl.ds(pl.multiple_of(start + size, 32), size // 2), :] = right_part
        return carry

    lax.fori_loop(0, slots, pack, 0)
    pl.semaphore_wait(barrier, 2 + jnp.where(a < line - 1, 1, 0) + jnp.where(a > 0, 1, 0))

    def index(at, bb):
        return at * PAIR + bb

    def remote(src, dst, s, r, dev):
        return pltpu.make_async_remote_copy(src_ref=src, dst_ref=dst, send_sem=s, recv_sem=r, device_id=dev, device_id_type=MESH)

    def full(at, s, r, dev, src=None):
        ref = out_ref.at[y, index(at, b)]
        return remote(ref if src is None else src, ref, s, r, dev)

    def part(yy, at, bb, upper, s, r, dev):
        ref = out_ref.at[yy, index(at, bb), pl.ds(0 if upper else half, half)]
        return remote(ref, ref, s, r, dev)

    keep = pltpu.make_async_copy(own, out_ref.at[y, index(a, b)], sem_own)
    keep.start()

    def spread(at, src=None):
        full(at, s_x.at[at], r_x.at[at], x_dev, src).start()
        full(at, s_y.at[at], r_y.at[at], y_dev, src).start()

    def second(at):
        pltpu.make_async_remote_copy(
            src_ref=own, dst_ref=out_ref.at[y, index(at, other_b)], send_sem=s_x.at[at], recv_sem=r_x.at[at], device_id=x_dev, device_id_type=MESH
        ).wait_recv()
        part(y, at, other_b, True, s_yx.at[at], r_yx.at[at], y_dev).start()
        pltpu.make_async_remote_copy(
            src_ref=own, dst_ref=out_ref.at[other_y, index(at, b)], send_sem=s_y.at[at], recv_sem=r_y.at[at], device_id=y_dev, device_id_type=MESH
        ).wait_recv()
        part(other_y, at, b, False, s_xy.at[at], r_xy.at[at], x_dev).start()

    def each(j, do):
        if j == 0:
            do(a)
            return

        @pl.when(a - j >= 0)
        def _():
            do(a - j)

        @pl.when(a + j < line)
        def _():
            do(a + j)

    @pl.when(a < line - 1)
    def _():
        full(a, s_zr.at[a], r_z.at[a], right, own).start()

    @pl.when(a > 0)
    def _():
        full(a, s_zl.at[a], r_z.at[a], left, own).start()

    spread(a, own)
    for j in range(1, line):

        @pl.when(a - j >= 0)
        def _():
            at = a - j
            full(at, s_zr.at[at], r_z.at[at], right).wait_recv()

            @pl.when(a < line - 1)
            def _():
                full(at, s_zr.at[at], r_z.at[at], right).start()

        @pl.when(a + j < line)
        def _():
            at = a + j
            full(at, s_zl.at[at], r_z.at[at], left).wait_recv()

            @pl.when(a > 0)
            def _():
                full(at, s_zl.at[at], r_z.at[at], left).start()

        each(j, spread)
        each(j - 1, second)
    each(line - 1, second)

    def finish(at, carry):
        part(other_y, at, other_b, True, s_yx.at[at], r_yx.at[at], y_dev).wait_recv()
        part(other_y, at, other_b, False, s_xy.at[at], r_xy.at[at], x_dev).wait_recv()
        full(at, s_x.at[at], r_x.at[at], x_dev).wait_send()
        full(at, s_y.at[at], r_y.at[at], y_dev).wait_send()
        part(y, at, other_b, True, s_yx.at[at], r_yx.at[at], y_dev).wait_send()
        part(other_y, at, b, False, s_xy.at[at], r_xy.at[at], x_dev).wait_send()

        @pl.when((at <= a) & (a < line - 1))
        def _():
            full(at, s_zr.at[at], r_z.at[at], right).wait_send()

        @pl.when((at >= a) & (a > 0))
        def _():
            full(at, s_zl.at[at], r_z.at[at], left).wait_send()

        return carry

    lax.fori_loop(0, line, finish, 0)
    keep.wait()


def gather(master, line):
    slots, size, _ = master.shape
    rows = slots * packed_rows(size)
    sems = [pltpu.SemaphoreType.DMA((line,))] * 11
    return pl.pallas_call(
        functools.partial(gather_kernel, line, size),
        out_shape=jax.ShapeDtypeStruct((2, line * PAIR, rows, LANES), jnp.bfloat16),
        in_specs=[pl.BlockSpec(memory_space=pltpu.VMEM)],
        out_specs=pl.BlockSpec(memory_space=pl.ANY),
        scratch_shapes=[pltpu.VMEM((rows, LANES), jnp.bfloat16), pltpu.SemaphoreType.DMA] + sems,
        compiler_params=pltpu.CompilerParams(collective_id=1, has_side_effects=True, vmem_limit_bytes=40 * MIB),
        name="gather",
    )(master)


HEAD = 64
EPS = 1e-05
NEG = -1000000000.0
TOP = 3.0e38
QB = 256
MLP_ROWS = 512
LN_ROWS = 128
F32 = jnp.float32
BF16 = jnp.bfloat16


def dot(a, b):
    return lax.dot_general(a, b, (((1,), (0,)), ((), ())), preferred_element_type=F32)


def dot_nt(a, b):
    return lax.dot_general(a, b, (((1,), (1,)), ((), ())), preferred_element_type=F32)


def dot_tn(a, b):
    return lax.dot_general(a, b, (((0,), (0,)), ((), ())), preferred_element_type=F32)


def centre_of(value):
    mean = jnp.mean(value, -1, keepdims=True)
    centred = value - mean
    spread = jnp.mean(centred * centred, -1, keepdims=True)
    return centred, lax.rsqrt(spread + EPS)


def norm_back(value, d_out, gain):
    centred, scale = centre_of(value)
    hat = centred * scale
    d_hat = d_out * gain
    back = scale * (d_hat - jnp.mean(d_hat, -1, keepdims=True) - hat * jnp.mean(d_hat * hat, -1, keepdims=True))
    return back, hat


def rows_of(start, count):
    return pl.ds(pl.multiple_of(start, count), count)


def column_sum(value):
    return jnp.sum(value, 0, keepdims=True)


def layer_kernel(
    dims,
    table,
    tokens,
    segments,
    cotangent,
    pieces,
    shared,
    split,
    grad_blocks,
    out_pair,
    in_grad,
    vectors,
    x,
    dy,
    held,
    w_qkv,
    w_out,
    w_fc,
    w_proj,
    cap,
    seg_col,
    h_one,
    q_s,
    k_s,
    v_s,
    k_t,
    v_t,
    mixed,
    logsum,
    send_a,
    recv_a,
    send_b,
    recv_b,
    send_c,
    recv_c,
    recv_d,
    second,
    h_two,
    gelu_s,
    d_hid,
    d_mixed,
    d_keys,
    d_vals,
    d_qkv,
    bias_qkv,
    bias_fc,
    sem_in,
    sem_out,
    sa,
    ra,
    sb,
    rb,
    sc,
    rc,
    sd,
    rd,
    so,
    ro,
):
    size, width, count = dims
    a, b, y, c = place()
    partner = device(a, b, y, 1 - c)
    y_dev = device(a, b, 1 - y, c)
    barrier = pltpu.get_barrier_semaphore()
    for dev in (partner, y_dev):
        pl.semaphore_signal(barrier, inc=1, device_id=dev, device_id_type=MESH)

    grid = width // size
    hidden_t = split.shape[1] - 3 * size
    fold = hidden_t // size
    pair = 2 * size
    cut_a, cut_b = 3 * grid, 4 * grid
    cut_c = cut_b + grid * fold
    blocks = cut_c + grid * fold
    heads = pair // HEAD
    hidden = 2 * hidden_t
    steps = count // QB
    block_rows = packed_rows(size)
    half = size // 2

    load_x = pltpu.make_async_copy(tokens.at[y], x, sem_in.at[0])
    load_x.start()
    load_w = pltpu.make_async_copy(pieces, held, sem_in.at[1])
    load_w.start()
    load_dy = pltpu.make_async_copy(cotangent.at[y], dy, sem_in.at[2])
    load_dy.start()

    def remote(src, dst, s, r, dev):
        return pltpu.make_async_remote_copy(src_ref=src, dst_ref=dst, send_sem=s, recv_sem=r, device_id=dev, device_id_type=MESH)

    def swap(send, recv, s, r, at, rows):
        where = pl.ds(at * rows, rows) if isinstance(at, int) else rows_of(at * rows, rows)
        return remote(send.at[where], recv.at[where], s.at[at], r.at[at], partner)

    seg_row = segments[pl.ds(y, 1), :].astype(F32)
    seg_col[...] = jnp.transpose(jnp.broadcast_to(seg_row, (LANES, count)))
    reach = []
    at = 0
    for i in range(steps):
        first = max(0, i - 2) * QB
        wide = (i + 1) * QB - first
        reach.append((first, wide, at))
        key_seg = seg_col[first : first + wide, :]
        key_seg = jnp.concatenate([key_seg] * (QB // LANES), 1)
        key_at = lax.broadcasted_iota(jnp.int32, (wide, QB), 0) + first
        query_at = lax.broadcasted_iota(jnp.int32, (wide, QB), 1) + i * QB
        allowed = (key_seg == seg_row[:, i * QB : (i + 1) * QB]) & (key_at <= query_at)
        cap[at : at + wide, :] = jnp.where(allowed, TOP, NEG)
        at += wide

    bias_qkv[0:1, :] = jnp.concatenate([split[t : t + 1, g * size : (g + 1) * size] for g in range(3) for t in range(2)], 1)
    bias_fc[0:1, :] = jnp.concatenate([split[t : t + 1, 3 * size :] for t in range(2)], 1)
    vectors[...] = jnp.zeros_like(vectors)

    gain1, shift1 = shared[0:1, :], shared[1:2, :]
    gain2, shift2 = shared[2:3, :], shared[3:4, :]
    out_bias, proj_bias = shared[4:5, :], shared[5:6, :]

    load_x.wait()

    def norm_one(i, carry):
        where = rows_of(i * LN_ROWS, LN_ROWS)
        centred, scale = centre_of(x[where, :].astype(F32))
        h_one[where, :] = (centred * scale * gain1 + shift1).astype(BF16)
        return carry

    lax.fori_loop(0, count // LN_ROWS, norm_one, 0)
    load_w.wait()

    def block_at(t, block):
        packed = held[t, table[t, block]]
        tail = packed[size:, :]
        return packed[:size], jnp.concatenate([tail[:, : LANES // 2], tail[:, LANES // 2 :]], 0)

    def put_pair(ref, row, col, first, other):
        left0, right0 = first
        left1, right1 = other
        where = rows_of(row * size, size)
        for k, tile in enumerate(
            (
                left0,
                jnp.concatenate([right0, left1[:, : LANES // 2]], 1),
                jnp.concatenate([left1[:, LANES // 2 :], right1], 1),
            )
        ):
            ref[where, pl.ds(pl.multiple_of(col + k * LANES, LANES), LANES)] = tile

    def build_attention(r, carry):
        for g in range(3):
            put_pair(w_qkv, r, g * pair, block_at(0, r * 3 + g), block_at(1, r * 3 + g))
        return carry

    lax.fori_loop(0, grid, build_attention, 0)

    def build_out(n, carry):
        t, j = n // (grid // 2), lax.rem(n, grid // 2)
        put_pair(w_out, t, j * pair, block_at(t, cut_a + 2 * j), block_at(t, cut_a + 2 * j + 1))
        return carry

    lax.fori_loop(0, 2 * (grid // 2), build_out, 0)

    def build_fc(n, carry):
        t, r = n // grid, lax.rem(n, grid)
        for f in range(0, fold, 2):
            block = cut_b + r * fold + f
            put_pair(w_fc, r, t * hidden_t + f * size, block_at(t, block), block_at(t, block + 1))
        return carry

    lax.fori_loop(0, 2 * grid, build_fc, 0)

    def build_proj(n, carry):
        t, f = n // fold, lax.rem(n, fold)
        for r in range(0, grid, 2):
            block = cut_c + f * grid + r
            put_pair(w_proj, n, r * size, block_at(t, block), block_at(t, block + 1))
        return carry

    lax.fori_loop(0, 2 * fold, build_proj, 0)

    def make_qkv(i, carry):
        where = rows_of(i * QB, QB)
        qkv = dot(h_one[where, :], w_qkv[...]) + bias_qkv[0:1, :]
        q_s[where, :] = (qkv[:, :pair].astype(BF16).astype(F32) * HEAD ** (-0.5)).astype(BF16)
        keys, values = qkv[:, pair : 2 * pair], qkv[:, 2 * pair :]
        k_s[where, :] = keys.astype(BF16)
        v_s[where, :] = values.astype(BF16)
        k_t[:, where] = jnp.transpose(keys).astype(BF16)
        v_t[:, where] = jnp.transpose(values).astype(BF16)
        return carry

    lax.fori_loop(0, steps, make_qkv, 0)
    pl.semaphore_wait(barrier, 2)

    def head_of(value, h):
        lane = lax.broadcasted_iota(jnp.int32, value.shape, 1)
        return jnp.where((lane < HEAD) if h == 0 else (lane >= HEAD), value, jnp.zeros_like(value))

    for i in range(steps):
        first, wide, at = reach[i]
        query_rows = slice(i * QB, (i + 1) * QB)

        def attend(n, carry):
            lanes = pl.ds(pl.multiple_of(n * LANES, LANES), LANES)
            keys = k_s[first : first + wide, lanes]
            query = q_s[query_rows, lanes]
            parts = []
            for h in range(2):
                scores = jnp.minimum(dot_nt(keys, head_of(query, h)), cap[at : at + wide, :])
                top = jnp.max(scores, 0, keepdims=True)
                expo = jnp.exp(scores - top)
                total = jnp.sum(expo, 0, keepdims=True)
                probs = (expo * (1.0 / total)).astype(BF16)
                value_rows = pl.ds(pl.multiple_of(n * LANES + h * HEAD, HEAD), HEAD)
                parts.append(dot(v_t[value_rows, first : first + wide], probs))
                logsum[pl.ds(2 * n + h, 1), query_rows] = top + jnp.log(total)
            mixed[query_rows, lanes] = jnp.transpose(jnp.concatenate(parts, 0)).astype(BF16)
            return carry

        lax.fori_loop(0, heads // 2, attend, 0)
        send_a[query_rows, :] = dot(mixed[query_rows, :], w_out[...]).astype(BF16)
        swap(send_a, recv_a, sa, ra, i, QB).start()

    load_dy.wait()

    fc_cols = pair
    parts_of = hidden // fc_cols
    curve = math.sqrt(2.0 / math.pi)

    def mlp(m, carry):
        for i in range(MLP_ROWS // QB):
            swap(send_a, recv_a, sa, ra, m * (MLP_ROWS // QB) + i, QB).wait_recv()

        def norm_two(i, inner):
            where = rows_of(m * MLP_ROWS + i * LN_ROWS, LN_ROWS)
            total = send_a[where, :].astype(F32) + recv_a[where, :].astype(F32)
            value = x[where, :].astype(F32) + total + out_bias
            second[where, :] = value
            centred, scale = centre_of(value)
            h_two[where, :] = (centred * scale * gain2 + shift2).astype(BF16)
            return inner

        lax.fori_loop(0, MLP_ROWS // LN_ROWS, norm_two, 0)
        where = rows_of(m * MLP_ROWS, MLP_ROWS)

        def strip(n, inner):
            cols = pl.ds(pl.multiple_of(n * fc_cols, LANES), fc_cols)
            hid = dot(h_two[where, :], w_fc[:, cols]) + bias_fc[0:1, cols]
            square = hid * hid
            bend = jnp.tanh(curve * hid * (1.0 + 0.044715 * square))
            up = 0.5 * (1.0 + bend)
            gelu_s[where, cols] = (hid * up).astype(BF16)
            slope = up + 0.5 * hid * (1.0 - bend * bend) * (curve * (1.0 + 3 * 0.044715 * square))
            back = (dot_nt(dy[where, :], w_proj[cols, :]) * slope).astype(BF16)
            d_hid[where, cols] = back
            vectors_fc[0:1, cols] += column_sum(back.astype(F32))
            return inner

        lax.fori_loop(0, parts_of, strip, 0)
        send_b[where, :] = dot(gelu_s[where, :], w_proj[...]).astype(BF16)
        send_c[where, :] = dot_nt(d_hid[where, :], w_fc[...]).astype(BF16)
        swap(send_c, recv_c, sc, rc, m, MLP_ROWS).start()
        swap(send_b, recv_b, sb, rb, m, MLP_ROWS).start()
        return carry

    vectors_fc = bias_fc.at[8:16]
    vectors_fc[...] = jnp.zeros(vectors_fc.shape, F32)
    lax.fori_loop(0, count // MLP_ROWS, mlp, 0)

    def keep_pair(tile, spot0, spot1):
        tile = tile.astype(BF16)
        t0, t1, t2 = (tile[:, k * LANES : (k + 1) * LANES] for k in range(3))
        h = LANES // 2
        for (t, block), left, right in (
            (spot0, t0, t1[:, :h]),
            (spot1, jnp.concatenate([t1[:, h:], t2[:, :h]], 1), t2[:, h:]),
        ):
            held[t, block, :size, :] = left
            held[t, block, size:, :] = jnp.concatenate([right[:half], right[half:]], 1)

    def grad_proj(n, carry):
        got = dot_tn(gelu_s[:, pl.ds(pl.multiple_of(n * pair, LANES), pair)], dy[...])
        for s in range(2):
            t, f = (2 * n + s) // fold, lax.rem(2 * n + s, fold)
            for r in range(0, grid, 2):
                block = cut_c + f * grid + r
                keep_pair(got[s * size : (s + 1) * size, r * size : (r + 2) * size], (t, block), (t, block + 1))
        return carry

    lax.fori_loop(0, hidden // pair, grad_proj, 0)

    def grad_fc(n, carry):
        t, m = n // (width // pair), lax.rem(n, width // pair)
        got = dot_tn(h_two[:, pl.ds(pl.multiple_of(m * pair, LANES), pair)], d_hid[:, pl.ds(pl.multiple_of(t * hidden_t, LANES), hidden_t)])
        for s in range(2):
            for f in range(0, fold, 2):
                block = cut_b + (2 * m + s) * fold + f
                keep_pair(got[s * size : (s + 1) * size, f * size : (f + 2) * size], (t, block), (t, block + 1))
        return carry

    lax.fori_loop(0, 2 * (width // pair), grad_fc, 0)

    def store(first, last, sem):
        return pltpu.make_async_copy(held.at[:, pl.ds(first, last - first)], grad_blocks.at[:, pl.ds(first, last - first)], sem)

    store(cut_b, blocks, sem_out.at[0]).start()

    for m in range(count // MLP_ROWS):
        swap(send_b, recv_b, sb, rb, m, MLP_ROWS).wait_recv()
        swap(send_c, recv_c, sc, rc, m, MLP_ROWS).wait_recv()

    def norm_two_back(i, carry):
        d_gain, d_shift, d_bias, d_proj = carry
        where = rows_of(i * LN_ROWS, LN_ROWS)
        value = second[where, :]
        total = send_b[where, :].astype(F32) + recv_b[where, :].astype(F32)
        recv_b[where, :] = (value + total + proj_bias).astype(BF16)
        d_norm = send_c[where, :].astype(F32) + recv_c[where, :].astype(F32)
        d_out = dy[where, :].astype(F32)
        back, hat = norm_back(value, d_norm, gain2)
        d_second = d_out + back
        second[where, :] = d_second
        low = d_second.astype(BF16)
        recv_c[where, :] = low
        return (
            d_gain + column_sum(d_norm * hat),
            d_shift + column_sum(d_norm),
            d_bias + column_sum(low.astype(F32)),
            d_proj + column_sum(d_out),
        )

    zero = jnp.zeros((1, width), F32)
    sums = lax.fori_loop(0, count // LN_ROWS, norm_two_back, (zero,) * 4)
    for k, row in enumerate(sums):
        vectors[2 + k : 3 + k, :width] = row
    d_low = recv_c

    own_half = rows_of(c * (count // 2), count // 2)
    other_half = rows_of((1 - c) * (count // 2), count // 2)
    keep_out = pltpu.make_async_copy(recv_b, out_pair.at[y], sem_out.at[1])
    keep_out.start()
    cross = remote(recv_b.at[own_half], out_pair.at[y, own_half], so.at[0], ro.at[0], y_dev)
    cross.start()

    d_vals[...] = jnp.zeros_like(d_vals)
    d_keys[...] = jnp.zeros_like(d_keys)

    def make_d_mixed(i, carry):
        where = rows_of(i * QB, QB)
        d_mixed[where, :] = dot_nt(d_low[where, :], w_out[...]).astype(BF16)
        return carry

    lax.fori_loop(0, steps, make_d_mixed, 0)

    got = dot_tn(mixed[...], d_low[...])
    for t in range(2):
        for r in range(0, grid, 2):
            keep_pair(got[t * size : (t + 1) * size, r * size : (r + 2) * size], (t, cut_a + r), (t, cut_a + r + 1))

    for i in range(steps):
        first, wide, at = reach[i]
        query_rows = slice(i * QB, (i + 1) * QB)

        def attend_back(n, carry):
            lanes = pl.ds(pl.multiple_of(n * LANES, LANES), LANES)
            key_rows = slice(first, first + wide)
            keys = k_s[key_rows, lanes]
            values = v_s[key_rows, lanes]
            query = q_s[query_rows, lanes]
            d_out = d_mixed[query_rows, lanes]
            d_query = []
            d_value_sum = d_vals[key_rows, lanes]
            d_key_sum = d_keys[key_rows, lanes]
            for h in range(2):
                query_h, d_out_h = head_of(query, h), head_of(d_out, h)
                scores = jnp.minimum(dot_nt(keys, query_h), cap[at : at + wide, :])
                probs = jnp.exp(scores - logsum[pl.ds(2 * n + h, 1), query_rows])
                d_probs = dot_nt(values, d_out_h)
                centre = jnp.sum(probs * d_probs, 0, keepdims=True)
                d_scores = (probs * (d_probs - centre)).astype(BF16)
                d_value_sum += dot(probs.astype(BF16), d_out_h)
                d_key_sum += dot(d_scores, query_h)
                value_rows = pl.ds(pl.multiple_of(n * LANES + h * HEAD, HEAD), HEAD)
                d_query.append(dot(k_t[value_rows, key_rows], d_scores))
            d_vals[key_rows, lanes] = d_value_sum
            d_keys[key_rows, lanes] = d_key_sum
            d_qkv[query_rows, lanes] = (jnp.transpose(jnp.concatenate(d_query, 0)) * HEAD ** (-0.5)).astype(BF16)
            return carry

        lax.fori_loop(0, heads // 2, attend_back, 0)

    cross.wait_recv()
    forward = remote(out_pair.at[1 - y, own_half], out_pair.at[1 - y, own_half], so.at[1], ro.at[1], partner)
    forward.start()
    for i in range(steps):
        swap(send_a, recv_a, sa, ra, i, QB).wait_send()

    def make_d_one(i, carry):
        where = rows_of(i * QB, QB)
        d_qkv[where, pair : 2 * pair] = d_keys[where, :].astype(BF16)
        d_qkv[where, 2 * pair :] = d_vals[where, :].astype(BF16)
        send_a[where, :] = dot_nt(d_qkv[where, :], w_qkv[...]).astype(BF16)
        swap(send_a, recv_d, sd, rd, i, QB).start()
        return carry + column_sum(d_qkv[where, :].astype(F32))

    d_bias_qkv = lax.fori_loop(0, steps, make_d_one, jnp.zeros((1, 3 * pair), F32))
    for t in range(2):
        vectors[6 + t : 7 + t, : 3 * size] = jnp.concatenate(
            [d_bias_qkv[:, (2 * g + t) * size : (2 * g + t + 1) * size] for g in range(3)], 1
        )
        vectors[6 + t : 7 + t, 3 * size : 3 * size + hidden_t] = vectors_fc[0:1, t * hidden_t : (t + 1) * hidden_t]

    def grad_qkv(n, carry):
        m, g = n // 3, lax.rem(n, 3)
        got = dot_tn(h_one[:, pl.ds(pl.multiple_of(m * pair, LANES), pair)], d_qkv[:, pl.ds(pl.multiple_of(g * pair, LANES), pair)])
        for s in range(2):
            block = (2 * m + s) * 3 + g
            keep_pair(got[s * size : (s + 1) * size, :], (0, block), (1, block))
        return carry

    lax.fori_loop(0, 3 * (width // pair), grad_qkv, 0)
    if grad_blocks.shape[1] > blocks:
        held[:, blocks] = jnp.zeros(held.shape[:1] + held.shape[2:], BF16)
        store(blocks, blocks + 1, sem_out.at[3]).start()
    store(0, cut_b, sem_out.at[2]).start()

    def norm_one_back(i, carry):
        d_gain, d_shift = carry
        where = rows_of(i * LN_ROWS, LN_ROWS)
        d_norm = send_a[where, :].astype(F32) + recv_d[where, :].astype(F32)
        back, hat = norm_back(x[where, :].astype(F32), d_norm, gain1)
        in_grad[where, :] = (second[where, :] + back).astype(BF16)
        return d_gain + column_sum(d_norm * hat), d_shift + column_sum(d_norm)

    for i in range(steps):
        swap(send_a, recv_d, sd, rd, i, QB).wait_recv()
    sums = lax.fori_loop(0, count // LN_ROWS, norm_one_back, (zero,) * 2)
    for k, row in enumerate(sums):
        vectors[k : k + 1, :width] = row

    for m in range(count // MLP_ROWS):
        swap(send_b, recv_b, sb, rb, m, MLP_ROWS).wait_send()
        swap(send_c, recv_c, sc, rc, m, MLP_ROWS).wait_send()
    for i in range(steps):
        swap(send_a, recv_d, sd, rd, i, QB).wait_send()
    store(cut_b, blocks, sem_out.at[0]).wait()
    store(0, cut_b, sem_out.at[2]).wait()
    if grad_blocks.shape[1] > blocks:
        store(blocks, blocks + 1, sem_out.at[3]).wait()
    keep_out.wait()
    cross.wait_send()
    forward.wait_send()
    remote(out_pair.at[1 - y, other_half], out_pair.at[1 - y, other_half], so.at[1], ro.at[1], partner).wait_recv()


def layer(table, tokens, segments, cotangent, pieces, shared, split, collective_id=2):
    seqs, count, width = tokens.shape
    _, slots, block_rows, _ = pieces.shape
    size = int(round(math.sqrt(block_rows * LANES)))
    pair = 2 * size
    hidden = 2 * (split.shape[1] - 3 * size)
    blocks = table.shape[1]
    steps = count // QB
    halves = count // MLP_ROWS
    spans = sum((i + 1 - max(0, i - 2)) * QB for i in range(steps))
    wide_vec = -(-split.shape[1] // LANES) * LANES
    vm = lambda shape, kind=BF16: pltpu.VMEM(shape, kind)
    dma = lambda n: pltpu.SemaphoreType.DMA((n,))
    anywhere = pl.BlockSpec(memory_space=pl.ANY)
    inside = pl.BlockSpec(memory_space=pltpu.VMEM)
    act = (count, width)
    return pl.pallas_call(
        functools.partial(layer_kernel, (size, width, count)),
        out_shape=(
            jax.ShapeDtypeStruct((2, min(blocks + 1, slots), block_rows, LANES), BF16),
            jax.ShapeDtypeStruct((2, count, width), BF16),
            jax.ShapeDtypeStruct((count, width), BF16),
            jax.ShapeDtypeStruct((8, wide_vec), F32),
        ),
        in_specs=[pl.BlockSpec(memory_space=pltpu.SMEM), anywhere, inside, anywhere, anywhere, inside, inside],
        out_specs=(anywhere, anywhere, inside, inside),
        scratch_shapes=[
            vm(act),
            vm(act),
            vm((2, slots, block_rows, LANES)),
            vm((width, 3 * pair)),
            vm((pair, width)),
            vm((width, hidden)),
            vm((hidden, width)),
            vm((spans, QB), F32),
            vm((count, LANES), F32),
            vm(act),
            vm((count, pair)),
            vm((count, pair)),
            vm((count, pair)),
            vm((pair, count)),
            vm((pair, count)),
            vm((count, pair)),
            vm((8, count), F32),
            vm(act),
            vm(act),
            vm(act),
            vm(act),
            vm(act),
            vm(act),
            vm(act),
            vm(act, F32),
            vm(act),
            vm((count, hidden)),
            vm((count, hidden)),
            vm((count, pair)),
            vm((count, pair), F32),
            vm((count, pair), F32),
            vm((count, 3 * pair)),
            vm((8, 3 * pair), F32),
            vm((16, hidden), F32),
            dma(3),
            dma(4),
            dma(steps),
            dma(steps),
            dma(halves),
            dma(halves),
            dma(halves),
            dma(halves),
            dma(steps),
            dma(steps),
            dma(2),
            dma(2),
        ],
        compiler_params=pltpu.CompilerParams(collective_id=collective_id, has_side_effects=True, vmem_limit_bytes=63 * MIB),
        name="layer",
    )(table, tokens, segments, cotangent, pieces, shared, split)


SHARE = 0.72
ROW_TILE = 32


def hand_on(line, at):
    turn = lambda dest: dest + line - at if dest < at else line - dest + at
    return sorted(range(line), key=lambda dest: line if dest == at else turn(dest))


def scatter_kernel(
    dims,
    where_from,
    blocks,
    vec,
    d_in,
    total_ref,
    vec_out,
    square_out,
    d_in_other,
    stage,
    from_x_u,
    from_x_l,
    from_y_l,
    from_y_u,
    from_z,
    vec_plane,
    vec_line,
    sq_plane,
    sq_line,
    s_xu,
    r_xu,
    s_xl,
    r_xl,
    s_yl,
    r_yl,
    s_yu,
    r_yu,
    s_z,
    r_z,
    s_v,
    r_v,
    s_vz,
    r_vz,
    s_q,
    r_q,
    s_qz,
    r_qz,
    s_in,
    r_in,
):
    line, slots, upper, chips = dims
    a, b, y, c = place()
    ob, oy, oc = 1 - b, 1 - y, 1 - c
    block_rows = blocks.shape[2]
    rows = slots * block_rows
    lower = rows - upper
    count = d_in.shape[0]
    x_dev, y_dev, core_dev = device(a, ob, y, c), device(a, b, oy, c), device(a, b, y, oc)
    right = device(jnp.minimum(a + 1, line - 1), b, y, c)
    left = device(jnp.maximum(a - 1, 0), b, y, c)
    up, low = pl.ds(0, upper), pl.ds(upper, lower)

    plane = []
    for k in range(1, 8):
        fb, fy, fc = (b + k // 4) % 2, (y + (k // 2) % 2) % 2, (c + k % 2) % 2
        plane.append((k, device(a, fb, fy, fc)))
    planes = [(k, lax.rem(a + k, line)) for k in range(1, line)]
    barrier = pltpu.get_barrier_semaphore()
    for _, dev in plane:
        pl.semaphore_signal(barrier, inc=1, device_id=dev, device_id_type=MESH)
    for _, at in planes:
        pl.semaphore_signal(barrier, inc=1, device_id=device(at, b, y, c), device_id_type=MESH)

    def remote(src, dst, s, r, dev):
        return pltpu.make_async_remote_copy(src_ref=src, dst_ref=dst, send_sem=s, recv_sem=r, device_id=dev, device_id_type=MESH)

    def dest(k):
        return sum(jnp.where(a == p, hand_on(line, p)[k], 0) for p in range(line))

    def fill(at):
        def one(n, carry):
            t, bb, j = n // (PAIR * slots), lax.rem(n // slots, PAIR), lax.rem(n, slots)
            block = blocks[t, where_from[t, (at * PAIR + bb) * slots + j]]
            stage[t, at, bb, pl.ds(pl.multiple_of(j * block_rows, ROW_TILE), block_rows), :] = block
            return carry

        lax.fori_loop(0, 2 * PAIR * slots, one, 0)

    def copy_xu(at):
        return remote(stage.at[:, at, ob, up], from_x_u.at[at], s_xu.at[at], r_xu.at[at], x_dev)

    def copy_yl(at):
        return remote(stage.at[oy, at, :, low], from_y_l.at[at], s_yl.at[at], r_yl.at[at], y_dev)

    def copy_yu(at):
        return remote(stage.at[oy, at, b, up], from_y_u.at[at], s_yu.at[at], r_yu.at[at], y_dev)

    def copy_xl(at):
        return remote(stage.at[y, at, ob, low], from_x_l.at[at], s_xl.at[at], r_xl.at[at], x_dev)

    def copy_z(at, side, dev):
        return remote(stage.at[y, at, b], from_z.at[side, at], s_z.at[at], r_z.at[side, at], dev)

    def add(t, at, bb, first, size, other):
        step = 288 if size % 288 == 0 else 16

        def one(n, carry):
            start = pl.multiple_of(n * step, 16)
            mine = pl.ds(first + start, step)
            stage[t, at, bb, mine, :] = (
                stage[t, at, bb, mine, :].astype(F32) + other[pl.ds(start, step), :].astype(F32)
            ).astype(BF16)
            return carry

        lax.fori_loop(0, size // step, one, 0)

    def copy_in(k):
        part = pl.ds(pl.multiple_of(c * (count // 2) + k * (count // 2 // line), 16), count // 2 // line)
        return remote(d_in.at[part], d_in_other.at[part], s_in.at[k], r_in.at[k], y_dev)

    def first(k):
        at = dest(k)
        fill(at)
        copy_xu(at).start()
        copy_yl(at).start()
        copy_in(k).start()

    def second(k):
        at = dest(k)
        copy_xu(at).wait_recv()
        for t in range(2):
            add(t, at, b, 0, upper, from_x_u.at[at, t])
        copy_yu(at).start()
        copy_yl(at).wait_recv()
        for bb in range(PAIR):
            add(y, at, bb, upper, lower, from_y_l.at[at, bb])
        copy_xl(at).start()

    def third(k):
        at = dest(k)
        copy_yu(at).wait_recv()
        add(y, at, b, 0, upper, from_y_u.at[at])
        copy_xl(at).wait_recv()
        add(y, at, b, upper, lower, from_x_l.at[at])

    def pass_on(turn):
        down = turn - line + a

        @pl.when((down >= 0) & (down < a))
        def _():
            @pl.when(a < line - 1)
            def _():
                copy_z(down, 1, left).wait_recv()
                add(y, down, b, 0, rows, from_z.at[1, down])

            copy_z(down, 1, left).start()

        upw = line - turn + a

        @pl.when((upw > a) & (upw < line))
        def _():
            @pl.when(a > 0)
            def _():
                copy_z(upw, 0, right).wait_recv()
                add(y, upw, b, 0, rows, from_z.at[0, upw])

            copy_z(upw, 0, right).start()

    same_core = [(k, dev) for k, dev in plane if k % 2 == 0]

    def vec_copy(k, dev):
        return remote(vec, vec_plane.at[b * 2 + y], s_v.at[k], r_v.at[b * 2 + y], dev)

    def vec_copy_z(k, at):
        return remote(vec_out, vec_line.at[a], s_vz.at[k], r_vz.at[a], device(at, b, y, c))

    pl.semaphore_wait(barrier, 7 + line - 1)
    for k, dev in same_core:
        vec_copy(k, dev).start()
    vec_plane[b * 2 + y] = vec[...]

    for step in range(line + 2):
        if step < line:
            first(step)
        if step == 1 or line == 1:
            for k, _ in same_core:
                slot = ((b + k // 4) % 2) * 2 + (y + (k // 2) % 2) % 2
                remote(vec, vec_plane.at[slot], s_v.at[k], r_v.at[slot], x_dev).wait()
            vec_out[...] = vec_plane[0] + vec_plane[1] + vec_plane[2] + vec_plane[3]
            for k, at in planes:
                vec_copy_z(k, at).start()
            vec_line[a] = vec_out[...]
        if 0 <= step - 1 < line:
            second(step - 1)
        if 0 <= step - 2 < line:
            third(step - 2)
            if step - 1 < line:
                pass_on(step - 1)

    for k, at in planes:
        remote(vec_out, vec_line.at[at], s_vz.at[k], r_vz.at[at], x_dev).wait()
    vec_sum = vec_line[0]
    for p in range(1, line):
        vec_sum = vec_sum + vec_line[p]
    vec_out[...] = vec_sum

    @pl.when(a > 0)
    def _():
        copy_z(a, 0, right).wait_recv()

    @pl.when(a < line - 1)
    def _():
        copy_z(a, 1, left).wait_recv()

    def finish(n, carry):
        part = pl.ds(pl.multiple_of(n * block_rows, ROW_TILE), block_rows)
        value = stage[y, a, b, part, :].astype(F32)
        value += jnp.where(a > 0, from_z[0, a, part, :].astype(F32), 0.0)
        value += jnp.where(a < line - 1, from_z[1, a, part, :].astype(F32), 0.0)
        total_ref[part, :] = value
        return carry + jnp.sum((value * value).reshape(block_rows // 8, 8, LANES), 0)

    square = lax.fori_loop(0, slots, finish, jnp.zeros((8, LANES), F32))
    row = lax.broadcasted_iota(jnp.int32, (8, LANES), 0)
    weight = jnp.where(row < 6, 1.0 / (chips * CORES), 1.0 / chips)
    for k in range(vec_sum.shape[1] // LANES):
        piece = vec_sum[:, k * LANES : (k + 1) * LANES]
        square += weight * piece * piece
    square_out[...] = square

    def sq_copy(k, dev, slot):
        return remote(square_out, sq_plane.at[slot], s_q.at[k], r_q.at[slot], dev)

    me = b * 4 + y * 2 + c
    for k, dev in plane:
        sq_copy(k, dev, me).start()
    sq_plane[me] = square

    half = pl.ds(pl.multiple_of(c * (count // 2), 16), count // 2)
    for k in range(line):
        copy_in(k).wait_recv()
    share = remote(d_in_other.at[half], d_in_other.at[half], s_in.at[line], r_in.at[line], core_dev)
    share.start()

    for k, dev in plane:
        fb, fy, fc = (b + k // 4) % 2, (y + (k // 2) % 2) % 2, (c + k % 2) % 2
        sq_copy(k, dev, fb * 4 + fy * 2 + fc).wait()
    square = sq_plane[0]
    for k in range(1, 8):
        square = square + sq_plane[k]
    square_out[...] = square
    for k, at in planes:
        remote(square_out, sq_line.at[a], s_qz.at[k], r_qz.at[a], device(at, b, y, c)).start()
    sq_line[a] = square

    share.wait()
    for k in range(line):
        copy_in(k).wait_send()

    def sent(at, carry):
        copy_xu(at).wait_send()
        copy_yl(at).wait_send()
        copy_yu(at).wait_send()
        copy_xl(at).wait_send()

        @pl.when(at != a)
        def _():
            copy_z(at, 0, right).wait_send()

        return carry

    lax.fori_loop(0, line, sent, 0)
    for k, at in planes:
        remote(square_out, sq_line.at[at], s_qz.at[k], r_qz.at[at], x_dev).wait()
    square = sq_line[0]
    for p in range(1, line):
        square = square + sq_line[p]
    square_out[...] = square


def scatter(where_from, blocks, vec, d_in, line, slots):
    block_rows = blocks.shape[2]
    rows = slots * block_rows
    upper = int(rows * SHARE) // 16 * 16
    if slots % 2 == 0 and rows % 576 == 0:
        upper = int(rows * SHARE) // 288 * 288
    lower = rows - upper
    vm = lambda shape, kind=BF16: pltpu.VMEM(shape, kind)
    dma = lambda *n: pltpu.SemaphoreType.DMA(n)
    anywhere = pl.BlockSpec(memory_space=pl.ANY)
    inside = pl.BlockSpec(memory_space=pltpu.VMEM)
    chips = line * PAIR * 2
    return pl.pallas_call(
        functools.partial(scatter_kernel, (line, slots, upper, chips)),
        out_shape=(
            jax.ShapeDtypeStruct((rows, LANES), F32),
            jax.ShapeDtypeStruct(vec.shape, F32),
            jax.ShapeDtypeStruct((8, LANES), F32),
            jax.ShapeDtypeStruct(d_in.shape, BF16),
        ),
        in_specs=[pl.BlockSpec(memory_space=pltpu.SMEM), inside, inside, anywhere],
        out_specs=(inside, inside, inside, anywhere),
        scratch_shapes=[
            vm((2, line, PAIR, rows, LANES)),
            vm((line, 2, upper, LANES)),
            vm((line, lower, LANES)),
            vm((line, PAIR, lower, LANES)),
            vm((line, upper, LANES)),
            vm((2, line, rows, LANES)),
            vm((4,) + vec.shape, F32),
            vm((line,) + vec.shape, F32),
            vm((8, 8, LANES), F32),
            vm((line, 8, LANES), F32),
        ]
        + [dma(line)] * 8
        + [dma(line), dma(2, line)]
        + [dma(8), dma(4), dma(line), dma(line), dma(8), dma(8), dma(line), dma(line), dma(line + 1), dma(line + 1)],
        compiler_params=pltpu.CompilerParams(collective_id=3, has_side_effects=True, vmem_limit_bytes=56 * MIB),
        name="scatter",
    )(where_from, blocks, vec, d_in)


DECAY = 0.5
RATE = 0.3
RATE_VECTOR = 0.2
HIGH = lax.Precision.HIGHEST


def exact(a, b, dims):
    return lax.dot_general(a, b, (dims, ((), ())), precision=HIGH, preferred_element_type=F32)


def update_kernel(
    grad, square, vec, master, stats, roots, shared, shared_state, split, split_state,
    norm_out, clipped_out, master_out, copy_out, stats_out, shared_grad, shared_new_state, shared_new,
    split_grad, split_new_state, split_new,
):
    size = master.shape[-1]
    y = lax.axis_index("tensor") // CORES
    norm = jnp.sqrt(jnp.sum(square[...], keepdims=True))
    factor = 1.0 / jnp.maximum(norm, 1.0)
    packed = grad[0] * factor
    tail = packed[size:]
    h = LANES // 2
    clipped = jnp.concatenate([packed[:size], jnp.concatenate([tail[:, :h], tail[:, h:]], 0)], 1)
    clipped_out[0, 0] = clipped
    stats_out[0, 0, 0] = DECAY * stats[0, 0, 0] + (1.0 - DECAY) * exact(clipped, clipped, ((1,), (1,)))
    stats_out[0, 0, 1] = DECAY * stats[0, 0, 1] + (1.0 - DECAY) * exact(clipped, clipped, ((0,), (0,)))
    step = exact(exact(roots[0, 0, 0], clipped, ((1,), (0,))), roots[0, 0, 1], ((1,), (0,)))
    new = master[0, 0] - RATE * step
    master_out[0, 0] = new
    copy_out[0, 0] = new.astype(BF16)

    @pl.when(pl.program_id(0) == 0)
    def _():
        norm_out[...] = norm
        for raw, value, state, g_out, s_out, v_out in (
            (vec[0 : shared.shape[0], : shared.shape[1]], shared, shared_state, shared_grad, shared_new_state, shared_new),
            (vec[pl.ds(6 + y, 1), :][:, : split.shape[1]], split, split_state, split_grad, split_new_state, split_new),
        ):
            g = raw * factor
            moment = DECAY * state[...] + (1.0 - DECAY) * g * g
            g_out[...] = g
            s_out[...] = moment
            v_out[...] = value[...] - RATE_VECTOR * g * lax.rsqrt(moment)


def update(grad, square, vec, master, stats, roots, shared, shared_state, split, split_state):
    _, slots, size, _ = master.shape
    grad = grad.reshape(slots, -1, LANES)
    whole = lambda shape: pl.BlockSpec(shape, lambda i: (0,) * len(shape))
    one = lambda shape: pl.BlockSpec(shape, lambda i: (0, i) + (0,) * (len(shape) - 2))
    blk, two = one((1, 1, size, size)), one((1, 1, 2, size, size))
    S = jax.ShapeDtypeStruct
    vec_spec, split_spec = whole(shared.shape), whole(split.shape)
    return pl.pallas_call(
        update_kernel,
        grid=(slots,),
        out_shape=(
            S((1, 1), F32), S(master.shape, F32), S(master.shape, F32), S(master.shape, BF16), S(stats.shape, F32),
        ) + (S(shared.shape, F32),) * 3 + (S(split.shape, F32),) * 3,
        in_specs=[pl.BlockSpec((1,) + grad.shape[1:], lambda i: (i, 0, 0)), whole(square.shape), whole(vec.shape), blk, two, two,
                  vec_spec, vec_spec, split_spec, split_spec],
        out_specs=(whole((1, 1)), blk, blk, blk, two) + (vec_spec,) * 3 + (split_spec,) * 3,
        compiler_params=pltpu.CompilerParams(vmem_limit_bytes=32 * MIB),
        name="update",
    )(grad, square, vec, master, stats, roots, shared, shared_state, split, split_state)


def body(
    tokens,
    segments,
    cotangent,
    block_owner_slots,
    master_weights,
    statistics,
    inverse_roots,
    shared_vectors,
    shared_state,
    split_bias,
    split_state,
):
    _, slots, size, _ = master_weights.shape
    ranks = lax.axis_size("dp")
    line = ranks // PAIR
    blocks = block_owner_slots.shape[1]
    y = lax.axis_index("tensor") // CORES
    swap = [(t, (t + CORES) % (2 * CORES)) for t in range(2 * CORES)]

    def both(value):
        other = lax.ppermute(value, "tensor", swap)
        return jnp.where(y == 0, jnp.concatenate([value, other]), jnp.concatenate([other, value]))

    table = both(block_owner_slots)
    split = both(split_bias)
    number = jnp.arange(blocks, dtype=jnp.int32)
    hit = table[:, :, None] == jnp.arange(ranks * slots, dtype=jnp.int32)[None, None]
    where_from = jnp.sum(jnp.where(hit, number[None, :, None] - blocks, 0), 1) + blocks

    pieces = gather(master_weights[0], line)
    pieces = pieces.reshape(2, ranks * slots, packed_rows(size), LANES)
    grad_blocks, out_pair, d_in, vec = layer(table, tokens, segments, cotangent, pieces, shared_vectors, split)
    grad, vec, square, d_in_other = scatter(where_from, grad_blocks, vec, d_in, line, slots)
    updated = update(
        grad, square, vec, master_weights, statistics, inverse_roots, shared_vectors, shared_state, split_bias, split_state
    )
    output = out_pair.astype(F32)
    input_grad = jnp.where(y == 0, jnp.stack([d_in, d_in_other]), jnp.stack([d_in_other, d_in])).astype(F32)
    return (output, input_grad, updated[0].reshape(())) + tuple(updated[1:])


def solution(mesh):
    placed = (
        P("dp", None, None),
        P("dp", None),
        P("dp", None, None),
        P("tensor", None),
        P("tensor", "dp", None, None),
        P("tensor", "dp", None, None, None),
        P("tensor", "dp", None, None, None),
        P(),
        P(),
        P("tensor", None),
        P("tensor", None),
    )
    return jax.shard_map(
        body,
        mesh=mesh,
        in_specs=placed,
        out_specs=(
            P("dp", None, None),
            P("dp", None, None),
            P(),
            P("tensor", "dp", None, None),
            P("tensor", "dp", None, None),
            P("tensor", "dp", None, None),
            P("tensor", "dp", None, None, None),
            P(),
            P(),
            P(),
            P("tensor", None),
            P("tensor", None),
            P("tensor", None),
        ),
        check_vma=False,
    )
```

```python
import functools
import math

import jax
import jax.numpy as jnp
from jax import lax
from jax.sharding import PartitionSpec as P
import jax.experimental.pallas as pl
import jax.experimental.pallas.tpu as pltpu

MESH = pl.DeviceIdType.MESH
PAIR = 2
CORES = 2
LANES = 128
MIB = 2**20
HEAD = 64
EPS = 1e-05
NEG = -1000000000.0
TOP = 3.0e38
QB = 256
MLP_ROWS = 512
LN_ROWS = 128
DECAY = 0.5
RATE = 0.3
RATE_VECTOR = 0.2
F32 = jnp.float32
BF16 = jnp.bfloat16


def packed_rows(size):
    return size * size // LANES


def pack_block(block):
    half = block.shape[0] // 2
    return block[:, :LANES], jnp.concatenate([block[:half, LANES:], block[half:, LANES:]], 1)


def unpack_block(packed, size):
    tail = packed[size:]
    h = LANES // 2
    return packed[:size], jnp.concatenate([tail[:, :h], tail[:, h:]], 0)


def place():
    d = lax.axis_index("dp")
    t = lax.axis_index("tensor")
    return d // PAIR, lax.rem(d, PAIR), t // CORES, lax.rem(t, CORES)


def device(a, b, y, c):
    return (a * PAIR + b, y * CORES + c)


def remote(src, dst, s, r, dev):
    return pltpu.make_async_remote_copy(src_ref=src, dst_ref=dst, send_sem=s, recv_sem=r, device_id=dev, device_id_type=MESH)


def dot(a, b):
    return lax.dot_general(a, b, (((1,), (0,)), ((), ())), preferred_element_type=F32)


def dot_nt(a, b):
    return lax.dot_general(a, b, (((1,), (1,)), ((), ())), preferred_element_type=F32)


def dot_tn(a, b):
    return lax.dot_general(a, b, (((0,), (0,)), ((), ())), preferred_element_type=F32)


def centre_of(value):
    mean = jnp.mean(value, -1, keepdims=True)
    centred = value - mean
    spread = jnp.mean(centred * centred, -1, keepdims=True)
    return centred, lax.rsqrt(spread + EPS)


def norm_back(value, d_out, gain):
    centred, scale = centre_of(value)
    hat = centred * scale
    d_hat = d_out * gain
    back = scale * (d_hat - jnp.mean(d_hat, -1, keepdims=True) - hat * jnp.mean(d_hat * hat, -1, keepdims=True))
    return back, hat


def rows_of(start, count):
    return pl.ds(pl.multiple_of(start, count), count)


def column_sum(value):
    return jnp.sum(value, 0, keepdims=True)


def layer_kernel(
    dims,
    table,
    table_src,
    tokens,
    segments,
    cotangent,
    master,
    shared,
    split,
    split_src,
    grad_blocks,
    out_own,
    in_grad,
    vectors,
    x,
    dy,
    owned,
    held0,
    held1,
    from_x,
    from_y,
    other_table,
    other_split,
    w_qkv,
    w_out,
    w_fc,
    w_proj,
    cap,
    seg_col,
    h_one,
    q_s,
    k_s,
    v_s,
    k_t,
    v_t,
    mixed_t,
    logsum,
    send_a,
    recv_a,
    send_b,
    recv_b,
    send_c,
    recv_c,
    recv_d,
    second,
    h_two,
    gelu_s,
    d_hid,
    d_keys,
    d_vals,
    d_query_t,
    bias_qkv,
    bias_fc,
    sem_in,
    sem_out,
    s_zr,
    s_zl,
    r_z,
    s_x,
    r_x,
    s_y,
    r_y,
    s_xy,
    r_xy,
    s_yx,
    r_yx,
    s_t,
    r_t,
    sa,
    ra,
    sb,
    rb,
    sc,
    rc,
    sd,
    rd,
    smx,
    rmx,
    smy,
    rmy,
):
    size, width, count, line, slots = dims
    a, b, y, c = place()
    ob = 1 - b
    partner = device(a, b, y, 1 - c)
    x_dev, y_dev = device(a, ob, y, c), device(a, b, 1 - y, c)
    right = device(jnp.minimum(a + 1, line - 1), b, y, c)
    left = device(jnp.maximum(a - 1, 0), b, y, c)
    barrier = pltpu.get_barrier_semaphore()
    for dev in (partner, x_dev, y_dev):
        pl.semaphore_signal(barrier, inc=1, device_id=dev, device_id_type=MESH)

    @pl.when(a < line - 1)
    def _():
        pl.semaphore_signal(barrier, inc=1, device_id=right, device_id_type=MESH)

    @pl.when(a > 0)
    def _():
        pl.semaphore_signal(barrier, inc=1, device_id=left, device_id_type=MESH)

    grid = width // size
    hidden_t = split.shape[1] - 3 * size
    fold = hidden_t // size
    pair = 2 * size
    cut_a, cut_b = 3 * grid, 4 * grid
    cut_c = cut_b + grid * fold
    blocks = cut_c + grid * fold
    heads = pair // HEAD
    hidden = 2 * hidden_t
    steps = count // QB
    h = LANES // 2

    load_m = pltpu.make_async_copy(master.at[0], owned, sem_in.at[0])
    load_m.start()
    load_x = pltpu.make_async_copy(tokens.at[y], x, sem_in.at[1])
    load_x.start()
    load_dy = pltpu.make_async_copy(cotangent.at[y], dy, sem_in.at[2])
    load_dy.start()

    def piece(ref, at, bb):
        return ref.at[pl.ds((at * PAIR + bb) * slots, slots)]

    def part(ref, at, bb, upper):
        first = slots // 2
        return ref.at[pl.ds((at * PAIR + bb) * slots + (0 if upper else first), first if upper else slots - first)]

    def z_copy(at, s, dev):
        return remote(piece(held0, at, b), piece(held0, at, b), s.at[at], r_z.at[at], dev)

    def x_copy(at):
        return remote(piece(held0, at, b), piece(held0, at, b), s_x.at[at], r_x.at[at], x_dev)

    def y_copy(at):
        return remote(piece(held0, at, b), piece(held1, at, b), s_y.at[at], r_y.at[at], y_dev)

    def yx_copy(at):
        return remote(part(held0, at, ob, True), part(held1, at, ob, True), s_yx.at[at], r_yx.at[at], y_dev)

    def xy_copy(at):
        return remote(part(held1, at, b, False), part(held1, at, b, False), s_xy.at[at], r_xy.at[at], x_dev)

    load_m.wait()
    mine = (a * PAIR + b) * slots

    def pack(s, carry):
        left_part, right_part = pack_block(owned[s].astype(BF16))
        held0[mine + s, :size] = left_part
        held0[mine + s, size:] = right_part
        return carry

    lax.fori_loop(0, slots, pack, 0)
    pl.semaphore_wait(barrier, 3 + jnp.where(a < line - 1, 1, 0) + jnp.where(a > 0, 1, 0))

    @pl.when(a < line - 1)
    def _():
        z_copy(a, s_zr, right).start()

    @pl.when(a > 0)
    def _():
        z_copy(a, s_zl, left).start()

    small = [
        remote(table_src, other_table, s_t.at[0], r_t.at[0], y_dev),
        remote(split_src, other_split, s_t.at[1], r_t.at[1], y_dev),
    ]
    for copy in small:
        copy.start()
    x_copy(a).start()
    y_copy(a).start()

    vectors[...] = jnp.zeros_like(vectors)
    gain1, shift1 = shared[0:1, :], shared[1:2, :]
    gain2, shift2 = shared[2:3, :], shared[3:4, :]
    out_bias, proj_bias = shared[4:5, :], shared[5:6, :]
    load_x.wait()

    def norm_one(i, carry):
        where = rows_of(i * LN_ROWS, LN_ROWS)
        centred, scale = centre_of(x[where, :].astype(F32))
        h_one[where, :] = (centred * scale * gain1 + shift1).astype(BF16)
        return carry

    lax.fori_loop(0, count // LN_ROWS, norm_one, 0)

    def arrivals(j):
        for ok, at, s, dev, more in (
            (a - j >= 0, a - j, s_zr, right, a < line - 1),
            (a + j < line, a + j, s_zl, left, a > 0),
        ):

            @pl.when(ok)
            def _():
                z_copy(at, s, dev).wait_recv()

                @pl.when(more)
                def _():
                    z_copy(at, s, dev).start()

                x_copy(at).start()
                y_copy(at).start()

    arrivals(1)
    seg_row = segments[pl.ds(y, 1), :].astype(F32)
    seg_col[...] = jnp.transpose(jnp.broadcast_to(seg_row, (LANES, count)))
    reach = []
    at = 0
    for i in range(steps):
        first = max(0, i - 2) * QB
        wide = (i + 1) * QB - first
        reach.append((first, wide, at))
        key_seg = seg_col[first : first + wide, :]
        key_seg = jnp.concatenate([key_seg] * (QB // LANES), 1)
        key_at = lax.broadcasted_iota(jnp.int32, (wide, QB), 0) + first
        query_at = lax.broadcasted_iota(jnp.int32, (wide, QB), 1) + i * QB
        allowed = (key_seg == seg_row[:, i * QB : (i + 1) * QB]) & (key_at <= query_at)
        cap[at : at + wide, :] = jnp.where(allowed, TOP, NEG)
        at += wide
    for copy in small:
        copy.wait()
    biases = (split, other_split)
    bias_qkv[0:1, :] = jnp.concatenate([biases[u][0:1, g * size : (g + 1) * size] for g in range(3) for u in range(2)], 1)
    bias_fc[0:1, :] = jnp.concatenate([biases[u][0:1, 3 * size :] for u in range(2)], 1)
    for j in range(2, line):
        arrivals(j)

    def first_hops(at, carry):
        x_copy(at).wait_recv()
        yx_copy(at).start()
        y_copy(at).wait_recv()
        xy_copy(at).start()
        return carry

    lax.fori_loop(0, line, first_hops, 0)

    def block_at(u, block):
        ref, lookup = ((held0, table), (held1, other_table))[u]
        return unpack_block(ref[lookup[0, block]], size)

    def put_pair(ref, row, col, first, other):
        left0, right0 = first
        left1, right1 = other
        where = rows_of(row * size, size)
        ref[where, col : col + LANES] = left0
        ref[where, col + LANES : col + 2 * LANES] = jnp.concatenate([right0, left1[:, :h]], 1)
        ref[where, col + 2 * LANES : col + 3 * LANES] = jnp.concatenate([left1[:, h:], right1], 1)

    def build_attention(u):
        def one(r, carry):
            where = rows_of(r * size, size)
            for g in range(3):
                left_part, right_part = block_at(u, r * 3 + g)
                col = g * pair
                if u == 0:
                    w_qkv[where, col : col + LANES] = left_part
                    w_qkv[where, col + LANES : col + LANES + h] = right_part
                else:
                    tile = w_qkv[where, col + LANES : col + 2 * LANES]
                    w_qkv[where, col + LANES : col + 2 * LANES] = jnp.concatenate([tile[:, :h], left_part[:, :h]], 1)
                    w_qkv[where, col + 2 * LANES : col + 3 * LANES] = jnp.concatenate([left_part[:, h:], right_part], 1)
            return carry

        lax.fori_loop(0, grid, one, 0)

    def build_rest(u):
        for j in range(0, grid, 2):
            put_pair(w_out, u, j * size, block_at(u, cut_a + j), block_at(u, cut_a + j + 1))

        def fc(r, carry):
            for f in range(0, fold, 2):
                block = cut_b + r * fold + f
                put_pair(w_fc, r, u * hidden_t + f * size, block_at(u, block), block_at(u, block + 1))
            return carry

        lax.fori_loop(0, grid, fc, 0)

        def proj(f, carry):
            for r in range(0, grid, 2):
                block = cut_c + f * grid + r
                put_pair(w_proj, u * fold + f, r * size, block_at(u, block), block_at(u, block + 1))
            return carry

        lax.fori_loop(0, fold, proj, 0)

    def make_qkv(u):
        low, high = ((0, size), (LANES, pair))[u]

        def one(i, carry):
            where = rows_of(i * QB, QB)
            for g in range(3):
                cols = slice(g * pair + low, g * pair + high)
                got = dot(h_one[where, :], w_qkv[:, cols]) + bias_qkv[0:1, cols]
                if g == 0:
                    q_s[where, low:high] = (got.astype(BF16).astype(F32) * HEAD ** (-0.5)).astype(BF16)
                else:
                    row, col = ((k_s, k_t), (v_s, v_t))[g - 1]
                    row[where, low:high] = got.astype(BF16)
                    col[low:high, where] = jnp.transpose(got).astype(BF16)
            return carry

        lax.fori_loop(0, steps, one, 0)

    def head_of(value, n):
        lane = lax.broadcasted_iota(jnp.int32, value.shape, 1)
        return jnp.where((lane < HEAD) if n % 2 == 0 else (lane >= HEAD), value, jnp.zeros_like(value))

    def tile_of(n):
        return slice(n // 2 * LANES, (n // 2 + 1) * LANES)

    def attend(i, n):
        first, wide, at = reach[i]
        query_rows = slice(i * QB, (i + 1) * QB)
        keys = k_s[first : first + wide, tile_of(n)]
        query = head_of(q_s[query_rows, tile_of(n)], n)
        scores = jnp.minimum(dot_nt(keys, query), cap[at : at + wide, :])
        top = jnp.max(scores, 0, keepdims=True)
        expo = jnp.exp(scores - top)
        total = jnp.sum(expo, 0, keepdims=True)
        got = dot(v_t[n * HEAD : (n + 1) * HEAD, first : first + wide], expo.astype(BF16))
        mixed_t[n * HEAD : (n + 1) * HEAD, query_rows] = (got * (1.0 / total)).astype(BF16)
        logsum[n : n + 1, query_rows] = top + jnp.log(total)

    own_heads, other_heads = range(heads // 2), range(heads // 2, heads)
    build_attention(0)
    make_qkv(0)
    for i in range(steps):
        for n in own_heads:
            attend(i, n)
    build_rest(0)

    def second_hops(at, carry):
        yx_copy(at).wait_recv()
        xy_copy(at).wait_recv()
        return carry

    lax.fori_loop(0, line, second_hops, 0)
    build_attention(1)
    make_qkv(1)
    build_rest(1)

    def swap(send, recv, s, r, at, rows):
        where = pl.ds(at * rows, rows) if isinstance(at, int) else rows_of(at * rows, rows)
        return remote(send.at[where], recv.at[where], s.at[at], r.at[at], partner)

    for i in range(steps):
        for n in other_heads:
            attend(i, n)
        query_rows = slice(i * QB, (i + 1) * QB)
        send_a[query_rows, :] = dot_tn(mixed_t[:, query_rows], w_out[...]).astype(BF16)
        swap(send_a, recv_a, sa, ra, i, QB).start()

    load_dy.wait()

    strips = hidden // pair
    curve = math.sqrt(2.0 / math.pi)
    bias_sum = bias_fc.at[8:16]
    bias_sum[...] = jnp.zeros(bias_sum.shape, F32)

    def mlp(m, carry):
        for i in range(MLP_ROWS // QB):
            swap(send_a, recv_a, sa, ra, m * (MLP_ROWS // QB) + i, QB).wait_recv()

        def norm_two(i, inner):
            where = rows_of(m * MLP_ROWS + i * LN_ROWS, LN_ROWS)
            total = send_a[where, :].astype(F32) + recv_a[where, :].astype(F32)
            value = x[where, :].astype(F32) + total + out_bias
            second[where, :] = value
            centred, scale = centre_of(value)
            h_two[where, :] = (centred * scale * gain2 + shift2).astype(BF16)
            return inner

        lax.fori_loop(0, MLP_ROWS // LN_ROWS, norm_two, 0)
        where = rows_of(m * MLP_ROWS, MLP_ROWS)

        def strip(n, inner):
            cols = pl.ds(pl.multiple_of(n * pair, LANES), pair)
            hid = dot(h_two[where, :], w_fc[:, cols]) + bias_fc[0:1, cols]
            square = hid * hid
            bend = jnp.tanh(curve * hid * (1.0 + 0.044715 * square))
            up = 0.5 * (1.0 + bend)
            gelu_s[where, cols] = (hid * up).astype(BF16)
            slope = up + 0.5 * hid * (1.0 - bend * bend) * (curve * (1.0 + 3 * 0.044715 * square))
            back = (dot_nt(dy[where, :], w_proj[cols, :]) * slope).astype(BF16)
            d_hid[where, cols] = back
            bias_sum[0:1, cols] += column_sum(back.astype(F32))
            return inner

        lax.fori_loop(0, strips, strip, 0)
        send_c[where, :] = dot_nt(d_hid[where, :], w_fc[...]).astype(BF16)
        swap(send_c, recv_c, sc, rc, m, MLP_ROWS).start()
        send_b[where, :] = dot(gelu_s[where, :], w_proj[...]).astype(BF16)
        swap(send_b, recv_b, sb, rb, m, MLP_ROWS).start()
        return carry

    lax.fori_loop(0, count // MLP_ROWS, mlp, 0)

    def sent(at, carry):
        x_copy(at).wait_send()
        y_copy(at).wait_send()
        yx_copy(at).wait_send()
        xy_copy(at).wait_send()

        @pl.when((at <= a) & (a < line - 1))
        def _():
            z_copy(at, s_zr, right).wait_send()

        @pl.when((at >= a) & (a > 0))
        def _():
            z_copy(at, s_zl, left).wait_send()

        return carry

    lax.fori_loop(0, line, sent, 0)

    held = (held0, held1)

    def keep(ref, block, left_part, right_part):
        half = size // 2
        ref[block, :size, :] = left_part
        ref[block, size:, :] = jnp.concatenate([right_part[:half], right_part[half:]], 1)

    def keep_pair(u, tile, block):
        t0, t1, t2 = (tile[:, k * LANES : (k + 1) * LANES] for k in range(3))
        keep(held[u], block, t0, t1[:, :h])
        keep(held[u], block + 1, jnp.concatenate([t1[:, h:], t2[:, :h]], 1), t2[:, h:])

    def grad_proj(u, n):
        got = dot_tn(gelu_s[:, u * hidden_t + n * pair : u * hidden_t + (n + 1) * pair], dy[...]).astype(BF16)
        for s in range(2):
            for r in range(0, grid, 2):
                keep_pair(u, got[s * size : (s + 1) * size, r * size : (r + 2) * size], cut_c + (2 * n + s) * grid + r)

    def grad_fc(u, m):
        got = dot_tn(h_two[:, m * pair : (m + 1) * pair], d_hid[:, u * hidden_t : (u + 1) * hidden_t]).astype(BF16)
        for s in range(2):
            for f in range(0, fold, 2):
                keep_pair(u, got[s * size : (s + 1) * size, f * size : (f + 2) * size], cut_b + (2 * m + s) * fold + f)

    groups = []
    x_at = y_at = 0
    for first, number, direct in (
        (cut_c, grid * fold // 2, True),
        (cut_c + grid * fold // 2, grid * fold // 2, False),
        (cut_b, grid * fold, False),
        (cut_a, grid, False),
        (0, cut_a, False),
    ):
        moved = number if direct else number // 2
        groups.append((first, moved, direct, x_at, y_at))
        x_at += 0 if direct else moved
        y_at += moved

    def cross_x(k):
        first, moved, _, at, _ = groups[k]
        return remote(held1.at[pl.ds(first + ob * moved, moved)], from_x.at[pl.ds(at, moved)], smx.at[k], rmx.at[k], x_dev)

    def cross_y(k):
        first, moved, direct, _, at = groups[k]
        start = first if direct else first + b * moved
        return remote(held1.at[pl.ds(start, moved)], from_y.at[pl.ds(at, moved)], smy.at[k], rmy.at[k], y_dev)

    def merge(ref, start, other, at, number):
        def one(n, carry):
            ref[start + n] = (ref[start + n].astype(F32) + other[at + n].astype(F32)).astype(BF16)
            return carry

        lax.fori_loop(0, number, one, 0)

    def merge_x(k):
        first, moved, _, at, _ = groups[k]
        cross_x(k).wait_recv()
        merge(held1, first + b * moved, from_x, at, moved)
        cross_y(k).start()

    def merge_y(k):
        first, moved, direct, _, at = groups[k]
        cross_y(k).wait_recv()
        merge(held0, first if direct else first + b * moved, from_y, at, moved)

    for n in range(fold // 2):
        grad_proj(1, n)
        if n == 0:
            cross_y(0).start()
    cross_x(1).start()
    for m in range(width // pair):
        grad_fc(1, m)
    cross_x(2).start()

    for m in range(count // MLP_ROWS):
        swap(send_b, recv_b, sb, rb, m, MLP_ROWS).wait_recv()
        swap(send_c, recv_c, sc, rc, m, MLP_ROWS).wait_recv()

    def norm_two_back(i, carry):
        d_gain, d_shift, d_bias, d_proj = carry
        where = rows_of(i * LN_ROWS, LN_ROWS)
        value = second[where, :]
        total = send_b[where, :].astype(F32) + recv_b[where, :].astype(F32)
        recv_b[where, :] = (value + total + proj_bias).astype(BF16)
        d_norm = send_c[where, :].astype(F32) + recv_c[where, :].astype(F32)
        d_out = dy[where, :].astype(F32)
        back, hat = norm_back(value, d_norm, gain2)
        d_second = d_out + back
        second[where, :] = d_second
        low = d_second.astype(BF16)
        recv_c[where, :] = low
        return (
            d_gain + column_sum(d_norm * hat),
            d_shift + column_sum(d_norm),
            d_bias + column_sum(low.astype(F32)),
            d_proj + column_sum(d_out),
        )

    zero = jnp.zeros((1, width), F32)
    sums = lax.fori_loop(0, count // LN_ROWS, norm_two_back, (zero,) * 4)
    for k, row in enumerate(sums):
        vectors[2 + k : 3 + k, :width] = row
    d_low = recv_c
    keep_out = pltpu.make_async_copy(recv_b, out_own, sem_out.at[0])
    keep_out.start()
    merge_x(1)

    d_mixed = gelu_s.at[:, hidden_t : hidden_t + pair]
    d_qkv = (
        gelu_s.at[:, hidden_t + pair : hidden_t + 2 * pair],
        d_hid.at[:, hidden_t : hidden_t + pair],
        d_hid.at[:, hidden_t + pair : hidden_t + 2 * pair],
    )

    def make_d_mixed(i, carry):
        where = rows_of(i * QB, QB)
        d_mixed[where, :] = dot_nt(d_low[where, :], w_out[...]).astype(BF16)
        return carry

    lax.fori_loop(0, steps, make_d_mixed, 0)
    got = dot(mixed_t[...], d_low[...]).astype(BF16)
    for u in range(2):
        for r in range(0, grid, 2):
            keep_pair(u, got[u * size : (u + 1) * size, r * size : (r + 2) * size], cut_a + r)
    cross_x(3).start()

    d_vals[...] = jnp.zeros_like(d_vals)
    d_keys[...] = jnp.zeros_like(d_keys)

    def attend_back(i, n):
        first, wide, at = reach[i]
        query_rows = slice(i * QB, (i + 1) * QB)
        key_rows = slice(first, first + wide)
        tile = tile_of(n)
        keys = k_s[key_rows, tile]
        query = head_of(q_s[query_rows, tile], n)
        d_out = head_of(d_mixed[query_rows, tile], n)
        scores = jnp.minimum(dot_nt(keys, query), cap[at : at + wide, :])
        probs = jnp.exp(scores - logsum[n : n + 1, query_rows])
        d_probs = dot_nt(v_s[key_rows, tile], d_out)
        centre = jnp.sum(probs * d_probs, 0, keepdims=True)
        d_scores = (probs * (d_probs - centre)).astype(BF16)
        d_vals[key_rows, tile] += dot(probs.astype(BF16), d_out)
        d_keys[key_rows, tile] += dot(d_scores, query)
        got = dot(k_t[n * HEAD : (n + 1) * HEAD, key_rows], d_scores)
        d_query_t[n * HEAD : (n + 1) * HEAD, query_rows] = (got * HEAD ** (-0.5)).astype(BF16)

    def collect(u):
        low, high = ((0, size), (LANES, pair))[u]

        def one(i, carry):
            where = rows_of(i * QB, QB)
            d_qkv[0][where, low:high] = jnp.transpose(d_query_t[low:high, where].astype(F32)).astype(BF16)
            d_qkv[1][where, low:high] = d_keys[where, low:high].astype(BF16)
            d_qkv[2][where, low:high] = d_vals[where, low:high].astype(BF16)
            return carry

        lax.fori_loop(0, steps, one, 0)

    def grad_qkv(u, m):
        low, high = ((0, size), (LANES, pair))[u]
        for g in range(3):
            got = dot_tn(h_one[:, m * pair : (m + 1) * pair], d_qkv[g][:, low:high]).astype(BF16)
            for s in range(2):
                tile = got[s * size : (s + 1) * size]
                block = (2 * m + s) * 3 + g
                if u == 0:
                    keep(held0, block, tile[:, :LANES], tile[:, LANES:])
                else:
                    keep(held1, block, jnp.concatenate([tile[:, h:LANES], tile[:, LANES : LANES + h]], 1), tile[:, LANES + h :])

    d_query_t[size - h : size, :] = jnp.zeros((h, count), BF16)
    for i in range(steps):
        for n in other_heads:
            attend_back(i, n)
        if i == 1:
            merge_x(2)
    collect(1)
    for m in range(width // pair):
        grad_qkv(1, m)
    cross_x(4).start()
    merge_x(3)
    for i in range(steps):
        for n in own_heads:
            attend_back(i, n)
    merge_x(4)
    collect(0)
    for i in range(steps):
        swap(send_a, recv_a, sa, ra, i, QB).wait_send()

    def make_d_one(i, carry):
        where = rows_of(i * QB, QB)
        total = sum(dot_nt(d_qkv[g][where, :], w_qkv[:, g * pair : (g + 1) * pair]) for g in range(3))
        send_a[where, :] = total.astype(BF16)
        swap(send_a, recv_d, sd, rd, i, QB).start()
        return tuple(carry[g] + column_sum(d_qkv[g][where, :].astype(F32)) for g in range(3))

    d_bias = lax.fori_loop(0, steps, make_d_one, (jnp.zeros((1, pair), F32),) * 3)
    for u in range(2):
        row = pl.ds(6 + (y if u == 0 else 1 - y), 1)
        parts = [d_bias[g][:, u * size : (u + 1) * size] for g in range(3)] + [bias_sum[0:1, u * hidden_t : (u + 1) * hidden_t]]
        spare = vectors.shape[1] - split.shape[1]
        vectors[row, :] = jnp.concatenate(parts + [jnp.zeros((1, spare), F32)] * (spare > 0), 1)

    for m in range(width // pair):
        grad_qkv(0, m)
    for n in range(fold // 2):
        grad_proj(0, n)
    for m in range(width // pair):
        grad_fc(0, m)

    def norm_one_back(i, carry):
        d_gain, d_shift = carry
        where = rows_of(i * LN_ROWS, LN_ROWS)
        d_norm = send_a[where, :].astype(F32) + recv_d[where, :].astype(F32)
        back, hat = norm_back(x[where, :].astype(F32), d_norm, gain1)
        in_grad[where, :] = (second[where, :] + back).astype(BF16)
        return d_gain + column_sum(d_norm * hat), d_shift + column_sum(d_norm)

    for i in range(steps):
        swap(send_a, recv_d, sd, rd, i, QB).wait_recv()
    sums = lax.fori_loop(0, count // LN_ROWS, norm_one_back, (zero,) * 2)
    for k, row in enumerate(sums):
        vectors[k : k + 1, :width] = row

    for k in range(len(groups)):
        merge_y(k)
    if grad_blocks.shape[0] > blocks:
        held0[blocks] = jnp.zeros(held0.shape[1:], BF16)
    stored = grad_blocks.shape[0]
    store = pltpu.make_async_copy(held0.at[pl.ds(0, stored)], grad_blocks, sem_out.at[1])
    store.start()

    for k, (_, _, direct, _, _) in enumerate(groups):
        cross_y(k).wait_send()
        if not direct:
            cross_x(k).wait_send()
    for m in range(count // MLP_ROWS):
        swap(send_b, recv_b, sb, rb, m, MLP_ROWS).wait_send()
        swap(send_c, recv_c, sc, rc, m, MLP_ROWS).wait_send()
    for i in range(steps):
        swap(send_a, recv_d, sd, rd, i, QB).wait_send()
    keep_out.wait()
    store.wait()


def layer(table, tokens, segments, cotangent, master, shared, split, line):
    _, count, width = tokens.shape
    _, slots, size, _ = master.shape
    pair = 2 * size
    block_rows = packed_rows(size)
    total = line * PAIR * slots
    hidden = 2 * (split.shape[1] - 3 * size)
    blocks = table.shape[1]
    steps = count // QB
    halves = count // MLP_ROWS
    spans = sum((i + 1 - max(0, i - 2)) * QB for i in range(steps))
    wide_vec = -(-split.shape[1] // LANES) * LANES
    direct = width // size * (hidden // 2 // size) // 2
    x_blocks = (blocks - direct) // 2
    y_blocks = direct + x_blocks
    vm = lambda shape, kind=BF16: pltpu.VMEM(shape, kind)
    dma = lambda n: pltpu.SemaphoreType.DMA((n,))
    anywhere = pl.BlockSpec(memory_space=pltpu.HBM)
    inside = pl.BlockSpec(memory_space=pltpu.VMEM)
    act = (count, width)
    block = (block_rows, LANES)
    return pl.pallas_call(
        functools.partial(layer_kernel, (size, width, count, line, slots)),
        out_shape=(
            jax.ShapeDtypeStruct((min(blocks + 1, total),) + block, BF16),
            jax.ShapeDtypeStruct(act, BF16),
            jax.ShapeDtypeStruct(act, BF16),
            jax.ShapeDtypeStruct((8, wide_vec), F32),
        ),
        in_specs=[pl.BlockSpec(memory_space=pltpu.SMEM), anywhere, anywhere, inside, anywhere, anywhere, inside, inside, anywhere],
        out_specs=(anywhere, anywhere, inside, inside),
        scratch_shapes=[
            vm(act),
            vm(act),
            vm((slots, size, size), F32),
            vm((total,) + block),
            vm((total,) + block),
            vm((x_blocks,) + block),
            vm((y_blocks,) + block),
            pltpu.SMEM((1, blocks), jnp.int32),
            vm(split.shape, F32),
            vm((width, 3 * pair)),
            vm((pair, width)),
            vm((width, hidden)),
            vm((hidden, width)),
            vm((spans, QB), F32),
            vm((count, LANES), F32),
            vm(act),
            vm((count, pair)),
            vm((count, pair)),
            vm((count, pair)),
            vm((pair, count)),
            vm((pair, count)),
            vm((pair, count)),
            vm((8, count), F32),
            vm(act),
            vm(act),
            vm(act),
            vm(act),
            vm(act),
            vm(act),
            vm(act),
            vm(act, F32),
            vm(act),
            vm((count, hidden)),
            vm((count, hidden)),
            vm((count, pair), F32),
            vm((count, pair), F32),
            vm((pair, count)),
            vm((8, 3 * pair), F32),
            vm((16, hidden), F32),
            dma(3),
            dma(2),
        ]
        + [dma(line)] * 11
        + [dma(2), dma(2)]
        + [dma(steps), dma(steps), dma(halves), dma(halves), dma(halves), dma(halves), dma(steps), dma(steps)]
        + [dma(5)] * 4,
        compiler_params=pltpu.CompilerParams(collective_id=2, has_side_effects=True, vmem_limit_bytes=63 * MIB),
        name="layer",
    )(table, table, tokens, segments, cotangent, master, shared, split, split)


ROW_TILE = 32


def hand_on(line, at):
    turn = lambda dest: dest + line - at if dest < at else line - dest + at
    return sorted(range(line), key=lambda dest: line if dest == at else turn(dest))


def scatter_kernel(
    dims,
    where_from,
    blocks,
    vec,
    out,
    d_in,
    total_ref,
    vec_out,
    square_out,
    out_other,
    d_in_other,
    stage,
    from_x,
    from_z,
    vec_plane,
    vec_line,
    sq_plane,
    sq_line,
    s_x,
    r_x,
    s_z,
    r_z,
    s_v,
    r_v,
    s_vz,
    r_vz,
    s_q,
    r_q,
    s_qz,
    r_qz,
    s_in,
    r_in,
    s_sh,
    r_sh,
):
    line, slots, chips = dims
    a, b, y, c = place()
    ob, oy, oc = 1 - b, 1 - y, 1 - c
    block_rows = blocks.shape[1]
    rows = slots * block_rows
    count = d_in.shape[0]
    x_dev, y_dev, core_dev = device(a, ob, y, c), device(a, b, oy, c), device(a, b, y, oc)
    right = device(jnp.minimum(a + 1, line - 1), b, y, c)
    left = device(jnp.maximum(a - 1, 0), b, y, c)

    plane = []
    for k in range(1, 8):
        fb, fy, fc = lax.rem(b + k // 4, 2), lax.rem(y + k // 2 % 2, 2), lax.rem(c + k % 2, 2)
        plane.append((k, device(a, fb, fy, fc), fb * 4 + fy * 2 + fc))
    planes = [(k, lax.rem(a + k, line)) for k in range(1, line)]
    barrier = pltpu.get_barrier_semaphore()
    for _, dev, _ in plane:
        pl.semaphore_signal(barrier, inc=1, device_id=dev, device_id_type=MESH)
    for _, at in planes:
        pl.semaphore_signal(barrier, inc=1, device_id=device(at, b, y, c), device_id_type=MESH)

    def dest(k):
        return sum(jnp.where(a == p, hand_on(line, p)[k], 0) for p in range(line))

    def fill(at):
        def one(n, carry):
            bb, j = n // slots, lax.rem(n, slots)
            block = blocks[where_from[0, (at * PAIR + bb) * slots + j]]
            stage[at, bb, pl.ds(pl.multiple_of(j * block_rows, ROW_TILE), block_rows), :] = block
            return carry

        lax.fori_loop(0, PAIR * slots, one, 0)

    def copy_x(at):
        return remote(stage.at[at, ob], from_x.at[at], s_x.at[at], r_x.at[at], x_dev)

    def copy_z(at, side, dev):
        return remote(stage.at[at, b], from_z.at[at + 1 - side], s_z.at[at], r_z.at[at + 1 - side], dev)

    def add(at, other):
        def one(n, carry):
            part = pl.ds(pl.multiple_of(n * block_rows, ROW_TILE), block_rows)
            stage[at, b, part, :] = (stage[at, b, part, :].astype(F32) + other[part, :].astype(F32)).astype(BF16)
            return carry

        lax.fori_loop(0, slots, one, 0)

    half = count // 2
    own_half = pl.ds(pl.multiple_of(c * half, 16), half)

    def copy_act(k):
        src, dst = ((d_in, d_in_other), (out, out_other))[k]
        return remote(src.at[own_half], dst.at[own_half], s_in.at[k], r_in.at[k], y_dev)

    def share_act(k):
        dst = (d_in_other, out_other)[k]
        return remote(dst.at[own_half], dst.at[own_half], s_sh.at[k], r_sh.at[k], core_dev)

    def first(k):
        at = dest(k)
        fill(at)
        copy_x(at).start()

    def second(k):
        at = dest(k)
        copy_x(at).wait_recv()
        add(at, from_x.at[at])

    def pass_on(turn):
        down = turn - line + a

        @pl.when((down >= 0) & (down < a))
        def _():
            @pl.when(a < line - 1)
            def _():
                copy_z(down, 1, left).wait_recv()
                add(down, from_z.at[down])

            copy_z(down, 1, left).start()

        upw = line - turn + a

        @pl.when((upw > a) & (upw < line))
        def _():
            @pl.when(a > 0)
            def _():
                copy_z(upw, 0, right).wait_recv()
                add(upw, from_z.at[upw + 1])

            copy_z(upw, 0, right).start()

    same_core = [item for item in plane if item[0] % 2 == 0]
    here = b * 2 + y

    def vec_copy(k, dev, slot):
        return remote(vec, vec_plane.at[slot], s_v.at[k], r_v.at[slot], dev)

    def vec_copy_z(k, at, slot):
        return remote(vec_out, vec_line.at[slot], s_vz.at[k], r_vz.at[slot], device(at, b, y, c))

    first_fill = dest(0)
    fill(first_fill)
    pl.semaphore_wait(barrier, 7 + line - 1)
    copy_x(first_fill).start()
    for k, dev, _ in same_core:
        vec_copy(k, dev, here).start()
    for k in range(2):
        copy_act(k).start()
    vec_plane[here] = vec[...]

    for step in range(1, line + 1):
        if step < line:
            first(step)
        if step == 1:
            for k, dev, slot in same_core:
                vec_copy(k, dev, slot // 2).wait()
            vec_out[...] = vec_plane[0] + vec_plane[1] + vec_plane[2] + vec_plane[3]
            for k, at in planes:
                vec_copy_z(k, at, a).start()
            vec_line[a] = vec_out[...]
        second(step - 1)
        if step < line:
            pass_on(step)

    for k, at in planes:
        vec_copy_z(k, at, at).wait()
    vec_sum = vec_line[0]
    for p in range(1, line):
        vec_sum = vec_sum + vec_line[p]
    vec_out[...] = vec_sum

    @pl.when(a > 0)
    def _():
        copy_z(a, 0, right).wait_recv()

    @pl.when(a < line - 1)
    def _():
        copy_z(a, 1, left).wait_recv()

    def finish(n, carry):
        part = pl.ds(pl.multiple_of(n * block_rows, ROW_TILE), block_rows)
        value = stage[a, b, part, :].astype(F32)
        value += jnp.where(a > 0, from_z[a + 1, part, :].astype(F32), 0.0)
        value += jnp.where(a < line - 1, from_z[a, part, :].astype(F32), 0.0)
        total_ref[part, :] = value
        return carry + jnp.sum((value * value).reshape(block_rows // 8, 8, LANES), 0)

    square = lax.fori_loop(0, slots, finish, jnp.zeros((8, LANES), F32))
    row = lax.broadcasted_iota(jnp.int32, (8, LANES), 0)
    weight = jnp.where(row < 6, 1.0 / (chips * CORES), 1.0 / chips)
    for k in range(vec_sum.shape[1] // LANES):
        piece = vec_sum[:, k * LANES : (k + 1) * LANES]
        square += weight * piece * piece
    square_out[...] = square

    def sq_copy(k, dev, slot):
        return remote(square_out, sq_plane.at[slot], s_q.at[k], r_q.at[slot], dev)

    me = here * 2 + c
    for k, dev, _ in plane:
        sq_copy(k, dev, me).start()
    sq_plane[me] = square

    for k in range(2):
        copy_act(k).wait_recv()
        share_act(k).start()

    for k, dev, slot in plane:
        sq_copy(k, dev, slot).wait()
    square = sq_plane[0]
    for k in range(1, 8):
        square = square + sq_plane[k]
    square_out[...] = square

    def sq_copy_z(k, at, slot):
        return remote(square_out, sq_line.at[slot], s_qz.at[k], r_qz.at[slot], device(at, b, y, c))

    for k, at in planes:
        sq_copy_z(k, at, a).start()
    sq_line[a] = square

    for k in range(2):
        share_act(k).wait()
        copy_act(k).wait_send()

    def sent(at, carry):
        copy_x(at).wait_send()

        @pl.when(at != a)
        def _():
            copy_z(at, 0, right).wait_send()

        return carry

    lax.fori_loop(0, line, sent, 0)
    for k, at in planes:
        sq_copy_z(k, at, at).wait()
    square = sq_line[0]
    for p in range(1, line):
        square = square + sq_line[p]
    square_out[...] = square


def scatter(where_from, blocks, vec, out, d_in, line, slots):
    block_rows = blocks.shape[1]
    rows = slots * block_rows
    vm = lambda shape, kind=BF16: pltpu.VMEM(shape, kind)
    dma = lambda *n: pltpu.SemaphoreType.DMA(n)
    anywhere = pl.BlockSpec(memory_space=pltpu.HBM)
    inside = pl.BlockSpec(memory_space=pltpu.VMEM)
    chips = line * PAIR * 2
    return pl.pallas_call(
        functools.partial(scatter_kernel, (line, slots, chips)),
        out_shape=(
            jax.ShapeDtypeStruct((rows, LANES), F32),
            jax.ShapeDtypeStruct(vec.shape, F32),
            jax.ShapeDtypeStruct((8, LANES), F32),
            jax.ShapeDtypeStruct(out.shape, BF16),
            jax.ShapeDtypeStruct(d_in.shape, BF16),
        ),
        in_specs=[pl.BlockSpec(memory_space=pltpu.SMEM), inside, inside, anywhere, anywhere],
        out_specs=(inside, inside, inside, anywhere, anywhere),
        scratch_shapes=[
            vm((line, PAIR, rows, LANES)),
            vm((line, rows, LANES)),
            vm((line + 1, rows, LANES)),
            vm((4,) + vec.shape, F32),
            vm((line,) + vec.shape, F32),
            vm((8, 8, LANES), F32),
            vm((line, 8, LANES), F32),
        ]
        + [dma(line), dma(line), dma(line), dma(line + 1)]
        + [dma(8), dma(4), dma(line), dma(line), dma(8), dma(8), dma(line), dma(line), dma(2), dma(2), dma(2), dma(2)],
        compiler_params=pltpu.CompilerParams(collective_id=3, has_side_effects=True, vmem_limit_bytes=40 * MIB),
        name="scatter",
    )(where_from, blocks, vec, out, d_in)


def halves_of(value):
    high = value.astype(BF16)
    return high, (value - high.astype(F32)).astype(BF16)


def fine_dot(a, b):
    a_high, a_low = halves_of(a)
    b_high, b_low = halves_of(b)
    return dot(a_high, b_high) + (dot(a_high, b_low) + dot(a_low, b_high))


def update_kernel(
    side,
    grad,
    square,
    vec,
    master,
    stats,
    roots,
    shared,
    shared_state,
    split,
    split_state,
    out_mine,
    out_other,
    d_mine,
    d_other,
    norm_out,
    clipped_out,
    master_out,
    copy_out,
    stats_out,
    shared_grad,
    shared_new_state,
    shared_new,
    split_grad,
    split_new_state,
    split_new,
    output,
    input_grad,
):
    size = master.shape[-1]
    y = side[0]
    i = pl.program_id(0)
    slots = pl.num_programs(0) * 0 + side[1]
    mine = (i // (pl.num_programs(0) // 2)) == y
    for target, own, other in ((output, out_mine, out_other), (input_grad, d_mine, d_other)):
        target[0] = jnp.where(mine, own[...], other[...]).astype(F32)
    norm = jnp.sqrt(jnp.sum(square[...], keepdims=True))
    factor = 1.0 / jnp.maximum(norm, 1.0)

    @pl.when(i < slots)
    def _():
        clipped = jnp.concatenate(unpack_block(grad[0] * factor, size), 1)
        clipped_out[0, 0] = clipped
        low = clipped.astype(BF16)
        stats_out[0, 0, 0] = DECAY * stats[0, 0, 0] + (1.0 - DECAY) * dot_nt(low, low)
        stats_out[0, 0, 1] = DECAY * stats[0, 0, 1] + (1.0 - DECAY) * dot_tn(low, low)
        step = fine_dot(fine_dot(roots[0, 0, 0], clipped), roots[0, 0, 1])
        new = master[0, 0] - RATE * step
        master_out[0, 0] = new
        copy_out[0, 0] = new.astype(BF16)

    @pl.when(i == 0)
    def _():
        norm_out[...] = norm
        for raw, value, state, g_out, s_out, v_out in (
            (vec[0 : shared.shape[0], : shared.shape[1]], shared, shared_state, shared_grad, shared_new_state, shared_new),
            (vec[pl.ds(6 + y, 1), :][:, : split.shape[1]], split, split_state, split_grad, split_new_state, split_new),
        ):
            g = raw * factor
            moment = DECAY * state[...] + (1.0 - DECAY) * g * g
            g_out[...] = g
            s_out[...] = moment
            v_out[...] = value[...] - RATE_VECTOR * g * lax.rsqrt(moment)


def update(side, grad, square, vec, master, stats, roots, shared, shared_state, split, split_state, outs, d_ins):
    _, slots, size, _ = master.shape
    count, width = outs[0].shape
    grid = 8
    rows = 2 * count // grid
    grad = grad.reshape(slots, -1, LANES)
    whole = lambda shape: pl.BlockSpec(shape, lambda i, s: (0,) * len(shape))
    at = lambda i: jnp.minimum(i, slots - 1)
    one = lambda shape: pl.BlockSpec(shape, lambda i, s: (0, at(i)) + (0,) * (len(shape) - 2))
    blk, two = one((1, 1, size, size)), one((1, 1, 2, size, size))
    S = jax.ShapeDtypeStruct
    vec_spec, split_spec = whole(shared.shape), whole(split.shape)
    half = grid // 2
    mine = pl.BlockSpec((rows, width), lambda i, s: (jnp.where(i // half == s[0], i % half, (half - 1) * (1 - s[0])), 0))
    other = pl.BlockSpec((rows, width), lambda i, s: (jnp.where(i // half == s[0], (half - 1) * s[0], i % half), 0))
    act = pl.BlockSpec((1, rows, width), lambda i, s: (i // half, i % half, 0))
    return pl.pallas_call(
        update_kernel,
        out_shape=(S((1, 1), F32), S(master.shape, F32), S(master.shape, F32), S(master.shape, BF16), S(stats.shape, F32))
        + (S(shared.shape, F32),) * 3
        + (S(split.shape, F32),) * 3
        + (S((2, count, width), F32),) * 2,
        grid_spec=pltpu.PrefetchScalarGridSpec(
            num_scalar_prefetch=1,
            grid=(grid,),
            in_specs=[
                pl.BlockSpec((1,) + grad.shape[1:], lambda i, s: (at(i), 0, 0)),
                whole(square.shape),
                whole(vec.shape),
                blk,
                two,
                two,
                vec_spec,
                vec_spec,
                split_spec,
                split_spec,
                mine,
                other,
                mine,
                other,
            ],
            out_specs=(whole((1, 1)), blk, blk, blk, two) + (vec_spec,) * 3 + (split_spec,) * 3 + (act, act),
        ),
        compiler_params=pltpu.CompilerParams(vmem_limit_bytes=40 * MIB),
        name="update",
    )(side, grad, square, vec, master, stats, roots, shared, shared_state, split, split_state, outs[0], outs[1], d_ins[0], d_ins[1])


def body(
    tokens,
    segments,
    cotangent,
    block_owner_slots,
    master_weights,
    statistics,
    inverse_roots,
    shared_vectors,
    shared_state,
    split_bias,
    split_state,
):
    slots = master_weights.shape[1]
    ranks = lax.axis_size("dp")
    line = ranks // PAIR
    blocks = block_owner_slots.shape[1]
    number = jnp.arange(blocks, dtype=jnp.int32)
    hit = block_owner_slots[:, :, None] == jnp.arange(ranks * slots, dtype=jnp.int32)[None, None]
    where_from = jnp.sum(jnp.where(hit, number[None, :, None] - blocks, 0), 1) + blocks
    side = jnp.stack([lax.axis_index("tensor") // CORES, jnp.int32(slots)])

    grad_blocks, out, d_in, vec = layer(
        block_owner_slots, tokens, segments, cotangent, master_weights, shared_vectors, split_bias, line
    )
    grad, vec, square, out_other, d_in_other = scatter(where_from, grad_blocks, vec, out, d_in, line, slots)
    done = update(
        side,
        grad,
        square,
        vec,
        master_weights,
        statistics,
        inverse_roots,
        shared_vectors,
        shared_state,
        split_bias,
        split_state,
        (out, out_other),
        (d_in, d_in_other),
    )
    return (done[11], done[12], done[0].reshape(())) + tuple(done[1:11])


def solution(mesh):
    placed = (
        P("dp", None, None),
        P("dp", None),
        P("dp", None, None),
        P("tensor", None),
        P("tensor", "dp", None, None),
        P("tensor", "dp", None, None, None),
        P("tensor", "dp", None, None, None),
        P(),
        P(),
        P("tensor", None),
        P("tensor", None),
    )
    return jax.shard_map(
        body,
        mesh=mesh,
        in_specs=placed,
        out_specs=(
            P("dp", None, None),
            P("dp", None, None),
            P(),
            P("tensor", "dp", None, None),
            P("tensor", "dp", None, None),
            P("tensor", "dp", None, None),
            P("tensor", "dp", None, None, None),
            P(),
            P(),
            P(),
            P("tensor", None),
            P("tensor", None),
            P("tensor", None),
        ),
        check_vma=False,
    )
```

```python
import functools
import math

import jax
import jax.numpy as jnp
from jax import lax
from jax.sharding import PartitionSpec as P
import jax.experimental.pallas as pl
import jax.experimental.pallas.tpu as pltpu

MESH = pl.DeviceIdType.MESH
PAIR = 2
CORES = 2
LANES = 128
MIB = 2**20
HEAD = 64
EPS = 1e-05
NEG = -1000000000.0
TOP = 3.0e38
QB = 256
MLP_ROWS = 512
LN_ROWS = 128
DECAY = 0.5
RATE = 0.3
RATE_VECTOR = 0.2
F32 = jnp.float32
BF16 = jnp.bfloat16


def packed_rows(size):
    return size * size // LANES


def pack_block(block):
    half = block.shape[0] // 2
    return block[:, :LANES], jnp.concatenate([block[:half, LANES:], block[half:, LANES:]], 1)


def unpack_block(packed, size):
    tail = packed[size:]
    h = LANES // 2
    return packed[:size], jnp.concatenate([tail[:, :h], tail[:, h:]], 0)


def place():
    d = lax.axis_index("dp")
    t = lax.axis_index("tensor")
    return d // PAIR, lax.rem(d, PAIR), t // CORES, lax.rem(t, CORES)


def device(a, b, y, c):
    return (a * PAIR + b, y * CORES + c)


def remote(src, dst, s, r, dev):
    return pltpu.make_async_remote_copy(src_ref=src, dst_ref=dst, send_sem=s, recv_sem=r, device_id=dev, device_id_type=MESH)


def dot(a, b):
    return lax.dot_general(a, b, (((1,), (0,)), ((), ())), preferred_element_type=F32)


def dot_nt(a, b):
    return lax.dot_general(a, b, (((1,), (1,)), ((), ())), preferred_element_type=F32)


def dot_tn(a, b):
    return lax.dot_general(a, b, (((0,), (0,)), ((), ())), preferred_element_type=F32)


def centre_of(value):
    mean = jnp.mean(value, -1, keepdims=True)
    centred = value - mean
    spread = jnp.mean(centred * centred, -1, keepdims=True)
    return centred, lax.rsqrt(spread + EPS)


def norm_back(value, d_out, gain):
    centred, scale = centre_of(value)
    hat = centred * scale
    d_hat = d_out * gain
    back = scale * (d_hat - jnp.mean(d_hat, -1, keepdims=True) - hat * jnp.mean(d_hat * hat, -1, keepdims=True))
    return back, hat


def rows_of(start, count):
    return pl.ds(pl.multiple_of(start, count), count)


def column_sum(value):
    return jnp.sum(value, 0, keepdims=True)


def hand_on(line, at):
    turn = lambda dest: dest + line - at if dest < at else line - dest + at
    return sorted(range(line), key=lambda dest: line if dest == at else turn(dest))


def layer_kernel(
    dims,
    table,
    table_src,
    tokens,
    segments,
    cotangent,
    master,
    shared,
    split,
    split_src,
    where_from,
    total_out,
    vec_out,
    square_out,
    out_own,
    out_other,
    in_own,
    in_other,
    x,
    dy,
    owned,
    held0,
    held1,
    from_x,
    from_y,
    other_table,
    other_split,
    w_qkv,
    w_out,
    w_fc,
    w_proj,
    cap,
    h_one,
    q_s,
    k_s,
    v_s,
    k_t,
    v_t,
    mixed_t,
    logsum,
    send_a,
    recv_a,
    send_b,
    recv_b,
    send_c,
    recv_c,
    second,
    h_two,
    gelu_s,
    d_hid,
    d_keys,
    d_vals,
    d_query_t,
    bias_qkv,
    bias_fc,
    vectors,
    vec_plane,
    vec_line,
    sq_plane,
    sq_line,
    sem_in,
    sem_out,
    s_zr,
    s_zl,
    r_z,
    s_x,
    r_x,
    s_y,
    r_y,
    s_xy,
    r_xy,
    s_yx,
    r_yx,
    s_g,
    r_g,
    s_zgr,
    s_zgl,
    r_zg,
    s_t,
    r_t,
    sa,
    ra,
    sb,
    rb,
    sc,
    rc,
    sd,
    rd,
    smx,
    rmx,
    smy,
    rmy,
    ready,
    sfx,
    rfx,
    sfz,
    rfz,
    s_v,
    r_v,
    s_vz,
    r_vz,
    s_q,
    r_q,
    s_qz,
    r_qz,
    s_in,
    r_in,
    s_sh,
    r_sh,
):
    size, width, count, line, slots = dims
    a, b, y, c = place()
    ob = 1 - b
    partner = device(a, b, y, 1 - c)
    x_dev, y_dev = device(a, ob, y, c), device(a, b, 1 - y, c)
    right = device(jnp.minimum(a + 1, line - 1), b, y, c)
    left = device(jnp.maximum(a - 1, 0), b, y, c)
    plane = []
    for k in range(1, 8):
        fb, fy, fc = lax.rem(b + k // 4, 2), lax.rem(y + k // 2 % 2, 2), lax.rem(c + k % 2, 2)
        plane.append((k, device(a, fb, fy, fc), fb * 4 + fy * 2 + fc))
    planes = [(k, lax.rem(a + k, line)) for k in range(1, line)]
    barrier = pltpu.get_barrier_semaphore()
    for _, dev, _ in plane:
        pl.semaphore_signal(barrier, inc=1, device_id=dev, device_id_type=MESH)
    for _, at in planes:
        pl.semaphore_signal(barrier, inc=1, device_id=device(at, b, y, c), device_id_type=MESH)

    grid = width // size
    hidden_t = split.shape[1] - 3 * size
    fold = hidden_t // size
    pair = 2 * size
    cut_a, cut_b = 3 * grid, 4 * grid
    cut_c = cut_b + grid * fold
    blocks = cut_c + grid * fold
    heads = pair // HEAD
    hidden = 2 * hidden_t
    steps = count // QB
    h = LANES // 2

    load_m = pltpu.make_async_copy(master.at[0], owned, sem_in.at[0])
    load_m.start()
    load_x = pltpu.make_async_copy(tokens.at[y], x, sem_in.at[1])
    load_x.start()
    load_dy = pltpu.make_async_copy(cotangent.at[y], dy, sem_in.at[2])
    load_dy.start()

    last = slots // 3
    most = slots - last

    def span(ref, at, bb, first, number):
        return ref.at[pl.ds((at * PAIR + bb) * slots + first, number)]

    def z_copy(at, s, dev):
        return remote(span(held0, at, b, 0, slots), span(held0, at, b, 0, slots), s.at[at], r_z.at[at], dev)

    def x_copy(at):
        return remote(span(held0, at, b, 0, slots), span(held0, at, b, 0, slots), s_x.at[at], r_x.at[at], x_dev)

    def y_copy(at, number):
        return remote(span(held0, at, b, 0, number), span(held1, at, b, 0, number), s_y.at[at], r_y.at[at], y_dev)

    def y_share(at):
        return most - (1 + at % 2 if last else most // 2)

    def yx_copy(at):
        n = y_share(at)
        return remote(span(held0, at, ob, 0, n), span(held1, at, ob, 0, n), s_yx.at[at], r_yx.at[at], y_dev)

    def xy_copy(at):
        n = y_share(at)
        return remote(span(held1, at, b, n, most - n), span(held1, at, b, n, most - n), s_xy.at[at], r_xy.at[at], x_dev)

    def corner_copy():
        return remote(span(held0, a, ob, most, last), span(held1, a, ob, most, last), s_g.at[0], r_g.at[0], y_dev)

    def zg_copy(at, k, s, dev):
        where = span(held1, at, (b, ob)[k], most, last)
        return remote(where, where, s.at[k, at], r_zg.at[k, at], dev)

    load_m.wait()
    mine = (a * PAIR + b) * slots

    def pack(s, carry):
        left_part, right_part = pack_block(owned[s].astype(BF16))
        held0[mine + s, :size] = left_part
        held0[mine + s, size:] = right_part
        return carry

    lax.fori_loop(0, slots, pack, 0)
    pl.semaphore_wait(barrier, 7 + line - 1)

    @pl.when(a < line - 1)
    def _():
        z_copy(a, s_zr, right).start()

    @pl.when(a > 0)
    def _():
        z_copy(a, s_zl, left).start()

    small = [
        remote(table_src, other_table, s_t.at[0], r_t.at[0], y_dev),
        remote(split_src, other_split, s_t.at[1], r_t.at[1], y_dev),
    ]
    for copy in small:
        copy.start()
    x_copy(a).start()
    y_copy(a, slots).start()

    vectors[...] = jnp.zeros_like(vectors)
    gain1, shift1 = shared[0:1, :], shared[1:2, :]
    gain2, shift2 = shared[2:3, :], shared[3:4, :]
    out_bias, proj_bias = shared[4:5, :], shared[5:6, :]
    load_x.wait()

    def norm_one(i, carry):
        where = rows_of(i * LN_ROWS, LN_ROWS)
        centred, scale = centre_of(x[where, :].astype(F32))
        h_one[where, :] = (centred * scale * gain1 + shift1).astype(BF16)
        return carry

    lax.fori_loop(0, count // LN_ROWS, norm_one, 0)

    def arrivals(j):
        for ok, at, s, dev, more in (
            (a - j >= 0, a - j, s_zr, right, a < line - 1),
            (a + j < line, a + j, s_zl, left, a > 0),
        ):

            @pl.when(ok)
            def _():
                z_copy(at, s, dev).wait_recv()

                @pl.when(more)
                def _():
                    z_copy(at, s, dev).start()

                x_copy(at).start()
                y_copy(at, most).start()

    arrivals(1)
    seg_row = segments[pl.ds(y, 1), :].astype(F32)
    seg_col = d_keys.at[:, :LANES]
    seg_col[...] = jnp.transpose(jnp.broadcast_to(seg_row, (LANES, count)))
    reach = []
    at = 0
    for i in range(steps):
        first = max(0, i - 2) * QB
        wide = (i + 1) * QB - first
        reach.append((first, wide, at))
        key_seg = seg_col[first : first + wide, :]
        key_seg = jnp.concatenate([key_seg] * (QB // LANES), 1)
        key_at = lax.broadcasted_iota(jnp.int32, (wide, QB), 0) + first
        query_at = lax.broadcasted_iota(jnp.int32, (wide, QB), 1) + i * QB
        allowed = (key_seg == seg_row[:, i * QB : (i + 1) * QB]) & (key_at <= query_at)
        cap[at : at + wide, :] = jnp.where(allowed, TOP, NEG)
        at += wide
    x_copy(a).wait_recv()
    if last:
        corner_copy().start()
    for j in range(2, line):
        arrivals(j)
    for copy in small:
        copy.wait()
    biases = (split, other_split)
    bias_qkv[0:1, :] = jnp.concatenate([biases[u][0:1, g * size : (g + 1) * size] for g in range(3) for u in range(2)], 1)
    bias_fc[0:1, :] = jnp.concatenate([biases[u][0:1, 3 * size :] for u in range(2)], 1)

    y_copy(a, slots).wait_recv()

    def line_arrivals(j):
        for ok, at, s, dev, more in (
            (a - j >= 0, a - j, s_zgr, right, a < line - 1),
            (a + j < line, a + j, s_zgl, left, a > 0),
        ):

            @pl.when(ok)
            def _():
                for k in range(2):
                    zg_copy(at, k, s, dev).wait_recv()

                if j < line - 1:

                    @pl.when(more)
                    def _():
                        for k in range(2):
                            zg_copy(at, k, s, dev).start()

    if last:
        corner_copy().wait_recv()

        @pl.when(a < line - 1)
        def _():
            for k in range(2):
                zg_copy(a, k, s_zgr, right).start()

        @pl.when(a > 0)
        def _():
            for k in range(2):
                zg_copy(a, k, s_zgl, left).start()

        line_arrivals(1)

    for at in range(line):

        @pl.when(at != a)
        def _():
            x_copy(at).wait_recv()
            y_copy(at, most).wait_recv()

        yx_copy(at).start()
        xy_copy(at).start()
    if last:
        for j in range(2, line - 1):
            line_arrivals(j)
    def block_at(u, block):
        ref, lookup = ((held0, table), (held1, other_table))[u]
        return unpack_block(ref[lookup[0, block]], size)

    def put_pair(ref, row, col, first, other):
        left0, right0 = first
        left1, right1 = other
        where = rows_of(row * size, size)
        ref[where, col : col + LANES] = left0
        ref[where, col + LANES : col + 2 * LANES] = jnp.concatenate([right0, left1[:, :h]], 1)
        ref[where, col + 2 * LANES : col + 3 * LANES] = jnp.concatenate([left1[:, h:], right1], 1)

    def build_attention(u):
        def one(r, carry):
            where = rows_of(r * size, size)
            for g in range(3):
                left_part, right_part = block_at(u, r * 3 + g)
                col = g * pair
                if u == 0:
                    w_qkv[where, col : col + LANES] = left_part
                    w_qkv[where, col + LANES : col + LANES + h] = right_part
                else:
                    tile = w_qkv[where, col + LANES : col + 2 * LANES]
                    w_qkv[where, col + LANES : col + 2 * LANES] = jnp.concatenate([tile[:, :h], left_part[:, :h]], 1)
                    w_qkv[where, col + 2 * LANES : col + 3 * LANES] = jnp.concatenate([left_part[:, h:], right_part], 1)
            return carry

        lax.fori_loop(0, grid, one, 0)

    def build_rest(u):
        for j in range(0, grid, 2):
            put_pair(w_out, u, j * size, block_at(u, cut_a + j), block_at(u, cut_a + j + 1))

        def fc(r, carry):
            for f in range(0, fold, 2):
                block = cut_b + r * fold + f
                put_pair(w_fc, r, u * hidden_t + f * size, block_at(u, block), block_at(u, block + 1))
            return carry

        lax.fori_loop(0, grid, fc, 0)

        def proj(f, carry):
            for r in range(0, grid, 2):
                block = cut_c + f * grid + r
                put_pair(w_proj, u * fold + f, r * size, block_at(u, block), block_at(u, block + 1))
            return carry

        lax.fori_loop(0, fold, proj, 0)

    def make_qkv(u):
        low, high = ((0, size), (LANES, pair))[u]

        def one(i, carry):
            where = rows_of(i * QB, QB)
            for g in range(3):
                cols = slice(g * pair + low, g * pair + high)
                got = dot(h_one[where, :], w_qkv[:, cols]) + bias_qkv[0:1, cols]
                if g == 0:
                    q_s[where, low:high] = (got.astype(BF16).astype(F32) * HEAD ** (-0.5)).astype(BF16)
                else:
                    row, col = ((k_s, k_t), (v_s, v_t))[g - 1]
                    row[where, low:high] = got.astype(BF16)
                    if u == 0:
                        row[where, high : high + h] = jnp.zeros((QB, h), BF16)
                    col[low:high, where] = jnp.transpose(got).astype(BF16)
            return carry

        lax.fori_loop(0, steps, one, 0)

    def head_of(value, n):
        lane = lax.broadcasted_iota(jnp.int32, value.shape, 1)
        return jnp.where((lane < HEAD) if n % 2 == 0 else (lane >= HEAD), value, jnp.zeros_like(value))

    def tile_of(n):
        return slice(n // 2 * LANES, (n // 2 + 1) * LANES)

    def attend(i, n):
        first, wide, at = reach[i]
        query_rows = slice(i * QB, (i + 1) * QB)
        keys = k_s[first : first + wide, tile_of(n)]
        query = head_of(q_s[query_rows, tile_of(n)], n)
        scores = jnp.minimum(dot_nt(keys, query), cap[at : at + wide, :])
        top = jnp.max(scores, 0, keepdims=True)
        expo = jnp.exp(scores - top)
        total = jnp.sum(expo, 0, keepdims=True)
        got = dot(v_t[n * HEAD : (n + 1) * HEAD, first : first + wide], expo.astype(BF16))
        mixed_t[n * HEAD : (n + 1) * HEAD, query_rows] = (got * (1.0 / total)).astype(BF16)
        logsum[n : n + 1, query_rows] = top + jnp.log(total)

    own_heads, other_heads = range(heads // 2), range(heads // 2, heads)
    build_attention(0)
    make_qkv(0)
    for i in range(steps):
        for n in own_heads:
            attend(i, n)
    build_rest(0)

    for at in range(line):
        yx_copy(at).wait_recv()
        xy_copy(at).wait_recv()
    if last and line > 2:
        line_arrivals(line - 1)
    build_attention(1)
    make_qkv(1)
    build_rest(1)

    def swap(send, recv, s, r, at, rows):
        where = pl.ds(at * rows, rows) if isinstance(at, int) else rows_of(at * rows, rows)
        return remote(send.at[where], recv.at[where], s.at[at], r.at[at], partner)

    for i in range(steps):
        for n in other_heads:
            attend(i, n)
        query_rows = slice(i * QB, (i + 1) * QB)
        send_a[query_rows, :] = dot_tn(mixed_t[:, query_rows], w_out[...]).astype(BF16)
        swap(send_a, recv_a, sa, ra, i, QB).start()

    load_dy.wait()

    strips = hidden // pair
    curve = math.sqrt(2.0 / math.pi)
    bias_sum = bias_fc.at[8:16]
    bias_sum[...] = jnp.zeros(bias_sum.shape, F32)

    def mlp(m, carry):
        for i in range(MLP_ROWS // QB):
            swap(send_a, recv_a, sa, ra, m * (MLP_ROWS // QB) + i, QB).wait_recv()

        def norm_two(i, inner):
            where = rows_of(m * MLP_ROWS + i * LN_ROWS, LN_ROWS)
            total = send_a[where, :].astype(F32) + recv_a[where, :].astype(F32)
            value = x[where, :].astype(F32) + total + out_bias
            second[where, :] = value
            centred, scale = centre_of(value)
            h_two[where, :] = (centred * scale * gain2 + shift2).astype(BF16)
            return inner

        lax.fori_loop(0, MLP_ROWS // LN_ROWS, norm_two, 0)
        where = rows_of(m * MLP_ROWS, MLP_ROWS)

        def strip(n, inner):
            cols = pl.ds(pl.multiple_of(n * pair, LANES), pair)
            hid = dot(h_two[where, :], w_fc[:, cols]) + bias_fc[0:1, cols]
            square = hid * hid
            bend = jnp.tanh(curve * hid * (1.0 + 0.044715 * square))
            up = 0.5 * (1.0 + bend)
            gelu_s[where, cols] = (hid * up).astype(BF16)
            slope = up + 0.5 * hid * (1.0 - bend * bend) * (curve * (1.0 + 3 * 0.044715 * square))
            back = (dot_nt(dy[where, :], w_proj[cols, :]) * slope).astype(BF16)
            d_hid[where, cols] = back
            bias_sum[0:1, cols] += column_sum(back.astype(F32))
            return inner

        lax.fori_loop(0, strips, strip, 0)
        send_c[where, :] = dot_nt(d_hid[where, :], w_fc[...]).astype(BF16)
        swap(send_c, recv_c, sc, rc, m, MLP_ROWS).start()
        send_b[where, :] = dot(gelu_s[where, :], w_proj[...]).astype(BF16)
        swap(send_b, recv_b, sb, rb, m, MLP_ROWS).start()
        return carry

    lax.fori_loop(0, count // MLP_ROWS, mlp, 0)

    for at in range(line):
        x_copy(at).wait_send()
        yx_copy(at).wait_send()
        xy_copy(at).wait_send()

        @pl.when(at == a)
        def _():
            y_copy(at, slots).wait_send()

        @pl.when(at != a)
        def _():
            y_copy(at, most).wait_send()

        @pl.when((at <= a) & (a < line - 1))
        def _():
            z_copy(at, s_zr, right).wait_send()
            for k in range(2 if last else 0):
                zg_copy(at, k, s_zgr, right).wait_send()

        @pl.when((at >= a) & (a > 0))
        def _():
            z_copy(at, s_zl, left).wait_send()
            for k in range(2 if last else 0):
                zg_copy(at, k, s_zgl, left).wait_send()

    if last:
        corner_copy().wait_send()

    held = (held0, held1)

    def keep(ref, block, left_part, right_part):
        half = size // 2
        ref[block, :size, :] = left_part
        ref[block, size:, :] = jnp.concatenate([right_part[:half], right_part[half:]], 1)

    def keep_pair(u, tile, block):
        t0, t1, t2 = (tile[:, k * LANES : (k + 1) * LANES] for k in range(3))
        keep(held[u], block, t0, t1[:, :h])
        keep(held[u], block + 1, jnp.concatenate([t1[:, h:], t2[:, :h]], 1), t2[:, h:])

    def grad_proj(u, n):
        got = dot_tn(gelu_s[:, u * hidden_t + n * pair : u * hidden_t + (n + 1) * pair], dy[...]).astype(BF16)
        for s in range(2):
            for r in range(0, grid, 2):
                keep_pair(u, got[s * size : (s + 1) * size, r * size : (r + 2) * size], cut_c + (2 * n + s) * grid + r)

    def grad_fc(u, m):
        got = dot_tn(h_two[:, m * pair : (m + 1) * pair], d_hid[:, u * hidden_t : (u + 1) * hidden_t]).astype(BF16)
        for s in range(2):
            for f in range(0, fold, 2):
                keep_pair(u, got[s * size : (s + 1) * size, f * size : (f + 2) * size], cut_b + (2 * m + s) * fold + f)

    groups = []
    x_at = y_at = 0
    strip_blocks = 2 * grid
    few = strip_blocks // 2
    for first, number, direct in (
        (cut_c, few, True),
        (cut_c + few, strip_blocks - few, False),
        (cut_c + strip_blocks, strip_blocks, False),
        (cut_b, 2 * fold, False),
        (cut_b + 2 * fold, 2 * fold, False),
        (cut_a, grid, False),
        (0, 6, False),
        (6, 6, False),
    ):
        moved = number if direct else number // 2
        groups.append((first, moved, direct, x_at, y_at))
        x_at += 0 if direct else moved
        y_at += moved

    def cross_x(k):
        first, moved, _, at, _ = groups[k]
        return remote(held1.at[pl.ds(first + ob * moved, moved)], from_x.at[pl.ds(at, moved)], smx.at[k], rmx.at[k], x_dev)

    def cross_y(k):
        first, moved, direct, _, at = groups[k]
        start = first if direct else first + b * moved
        return remote(held1.at[pl.ds(start, moved)], from_y.at[pl.ds(at, moved)], smy.at[k], rmy.at[k], y_dev)

    def merge(ref, start, other, at, number):
        def one(n, carry):
            ref[start + n] = (ref[start + n].astype(F32) + other[at + n].astype(F32)).astype(BF16)
            return carry

        lax.fori_loop(0, number, one, 0)

    def merge_x(k):
        first, moved, _, at, _ = groups[k]
        cross_x(k).wait_recv()
        merge(held1, first + b * moved, from_x, at, moved)
        cross_y(k).start()

    def merge_y(k):
        first, moved, direct, _, at = groups[k]
        cross_y(k).wait_recv()
        merge(held0, first if direct else first + b * moved, from_y, at, moved)

    for n in range(fold // 2):
        grad_proj(1, n)
        if n == 0:
            cross_y(0).start()
            cross_x(1).start()
        else:
            cross_x(2).start()
    for m in range(width // pair):
        grad_fc(1, m)
        cross_x(3 + m).start()

    for m in range(count // MLP_ROWS):
        swap(send_b, recv_b, sb, rb, m, MLP_ROWS).wait_recv()
        swap(send_c, recv_c, sc, rc, m, MLP_ROWS).wait_recv()

    def norm_two_back(i, carry):
        d_gain, d_shift, d_bias, d_proj = carry
        where = rows_of(i * LN_ROWS, LN_ROWS)
        value = second[where, :]
        total = send_b[where, :].astype(F32) + recv_b[where, :].astype(F32)
        recv_b[where, :] = (value + total + proj_bias).astype(BF16)
        d_norm = send_c[where, :].astype(F32) + recv_c[where, :].astype(F32)
        d_out = dy[where, :].astype(F32)
        back, hat = norm_back(value, d_norm, gain2)
        d_second = d_out + back
        second[where, :] = d_second
        low = d_second.astype(BF16)
        recv_c[where, :] = low
        return (
            d_gain + column_sum(d_norm * hat),
            d_shift + column_sum(d_norm),
            d_bias + column_sum(low.astype(F32)),
            d_proj + column_sum(d_out),
        )

    zero = jnp.zeros((1, width), F32)
    sums = lax.fori_loop(0, count // LN_ROWS, norm_two_back, (zero,) * 4)
    for k, row in enumerate(sums):
        vectors[2 + k : 3 + k, :width] = row
    d_low = recv_c
    keep_out = pltpu.make_async_copy(recv_b, out_own, sem_out.at[0])
    keep_out.start()
    merge_x(1)

    d_mixed = gelu_s.at[:, hidden_t : hidden_t + pair]
    d_qkv = (
        gelu_s.at[:, hidden_t + pair : hidden_t + 2 * pair],
        d_hid.at[:, hidden_t : hidden_t + pair],
        d_hid.at[:, hidden_t + pair : hidden_t + 2 * pair],
    )

    def make_d_mixed(i, carry):
        where = rows_of(i * QB, QB)
        d_mixed[where, :] = dot_nt(d_low[where, :], w_out[...]).astype(BF16)
        return carry

    lax.fori_loop(0, steps, make_d_mixed, 0)
    def grad_out():
        got = dot(mixed_t[...], d_low[...]).astype(BF16)
        for u in range(2):
            for r in range(0, grid, 2):
                keep_pair(u, got[u * size : (u + 1) * size, r * size : (r + 2) * size], cut_a + r)

    d_vals[...] = jnp.zeros_like(d_vals)
    d_keys[...] = jnp.zeros_like(d_keys)

    def attend_back(i, n):
        first, wide, at = reach[i]
        query_rows = slice(i * QB, (i + 1) * QB)
        key_rows = slice(first, first + wide)
        tile = tile_of(n)
        keys = k_s[key_rows, tile]
        query = head_of(q_s[query_rows, tile], n)
        d_out = head_of(d_mixed[query_rows, tile], n)
        scores = jnp.minimum(dot_nt(keys, query), cap[at : at + wide, :])
        probs = jnp.exp(scores - logsum[n : n + 1, query_rows])
        d_probs = dot_nt(v_s[key_rows, tile], d_out)
        centre = jnp.sum(probs * d_probs, 0, keepdims=True)
        d_scores = (probs * (d_probs - centre)).astype(BF16)
        d_vals[key_rows, tile] += dot(probs.astype(BF16), d_out)
        d_keys[key_rows, tile] += dot(d_scores, query)
        got = dot(k_t[n * HEAD : (n + 1) * HEAD, key_rows], d_scores)
        d_query_t[n * HEAD : (n + 1) * HEAD, query_rows] = (got * HEAD ** (-0.5)).astype(BF16)

    def collect(u):
        low, high = ((0, size), (LANES, pair))[u]

        def one(i, carry):
            where = rows_of(i * QB, QB)
            d_qkv[0][where, low:high] = jnp.transpose(d_query_t[low:high, where].astype(F32)).astype(BF16)
            d_qkv[1][where, low:high] = d_keys[where, low:high].astype(BF16)
            d_qkv[2][where, low:high] = d_vals[where, low:high].astype(BF16)
            return carry

        lax.fori_loop(0, steps, one, 0)

    def grad_qkv(u, m):
        low, high = ((0, size), (LANES, pair))[u]
        for g in range(3):
            got = dot_tn(h_one[:, m * pair : (m + 1) * pair], d_qkv[g][:, low:high]).astype(BF16)
            for s in range(2):
                tile = got[s * size : (s + 1) * size]
                block = (2 * m + s) * 3 + g
                if u == 0:
                    keep(held0, block, tile[:, :LANES], tile[:, LANES:])
                else:
                    keep(held1, block, jnp.concatenate([tile[:, h:LANES], tile[:, LANES : LANES + h]], 1), tile[:, LANES + h :])

    d_query_t[size - h : size, :] = jnp.zeros((h, count), BF16)
    for i in range(steps):
        for n in other_heads:
            attend_back(i, n)
        if i == 1:
            merge_x(2)
    collect(1)
    for m in range(width // pair):
        grad_qkv(1, m)
        cross_x(6 + m).start()
    merge_x(3)
    grad_out()
    cross_x(5).start()
    for i in range(steps):
        for n in own_heads:
            attend_back(i, n)
        if i == 2:
            merge_x(4)
    collect(0)
    for i in range(steps):
        swap(send_a, recv_a, sa, ra, i, QB).wait_send()

    def make_d_one(i, carry):
        where = rows_of(i * QB, QB)
        total = sum(dot_nt(d_qkv[g][where, :], w_qkv[:, g * pair : (g + 1) * pair]) for g in range(3))
        send_a[where, :] = total.astype(BF16)
        swap(send_a, recv_a, sd, rd, i, QB).start()
        return tuple(carry[g] + column_sum(d_qkv[g][where, :].astype(F32)) for g in range(3))

    d_bias = lax.fori_loop(0, steps, make_d_one, (jnp.zeros((1, pair), F32),) * 3)
    for u in range(2):
        row = pl.ds(6 + (y if u == 0 else 1 - y), 1)
        parts = [d_bias[g][:, u * size : (u + 1) * size] for g in range(3)] + [bias_sum[0:1, u * hidden_t : (u + 1) * hidden_t]]
        spare = vectors.shape[1] - split.shape[1]
        vectors[row, :] = jnp.concatenate(parts + [jnp.zeros((1, spare), F32)] * (spare > 0), 1)

    for m in range(width // pair):
        grad_qkv(0, m)
    merge_x(6)
    for n in range(fold // 2):
        grad_proj(0, n)
    for m in range(width // pair):
        grad_fc(0, m)
    merge_x(7)
    merge_x(5)

    def norm_one_back(i, carry):
        d_gain, d_shift = carry
        where = rows_of(i * LN_ROWS, LN_ROWS)
        d_norm = send_a[where, :].astype(F32) + recv_a[where, :].astype(F32)
        back, hat = norm_back(x[where, :].astype(F32), d_norm, gain1)
        recv_a[where, :] = (second[where, :] + back).astype(BF16)
        return d_gain + column_sum(d_norm * hat), d_shift + column_sum(d_norm)

    for i in range(steps):
        swap(send_a, recv_a, sd, rd, i, QB).wait_recv()
    sums = lax.fori_loop(0, count // LN_ROWS, norm_one_back, (zero,) * 2)
    for k, row in enumerate(sums):
        vectors[k : k + 1, :width] = row

    keep_in = pltpu.make_async_copy(recv_a, in_own, sem_out.at[1])
    keep_in.start()

    here = b * 2 + y
    same_core = [item for item in plane if item[0] % 2 == 0]

    def vec_copy(k, dev, slot):
        return remote(vectors, vec_plane.at[slot], s_v.at[k], r_v.at[slot], dev)

    def vec_copy_z(k, at, slot):
        return remote(vec_out, vec_line.at[slot], s_vz.at[k], r_vz.at[slot], device(at, b, y, c))

    for k, dev, _ in same_core:
        vec_copy(k, dev, here).start()
    vec_plane[here] = vectors[...]

    for k in range(len(groups)):
        merge_y(k)
    if line * PAIR * slots > blocks:
        held0[blocks] = jnp.zeros(held0.shape[1:], BF16)
    for k, (_, _, direct, _, _) in enumerate(groups):
        cross_y(k).wait_send()
        if not direct:
            cross_x(k).wait_send()

    pl.semaphore_signal(ready.at[0], inc=1, device_id=x_dev, device_id_type=MESH)

    @pl.when(a < line - 1)
    def _():
        pl.semaphore_signal(ready.at[1], inc=1, device_id=right, device_id_type=MESH)

    @pl.when(a > 0)
    def _():
        pl.semaphore_signal(ready.at[2], inc=1, device_id=left, device_id_type=MESH)

    def dest(k):
        return sum(jnp.where(a == p, hand_on(line, p)[k], 0) for p in range(line))

    def fill(at):
        def one(n, carry):
            spot = at * PAIR * slots + n
            held1[spot] = held0[where_from[0, spot]]
            return carry

        lax.fori_loop(0, PAIR * slots, one, 0)

    def run(ref, at):
        return ref.at[pl.ds(at * slots, slots)]

    def copy_x(at):
        return remote(span(held1, at, ob, 0, slots), run(from_y, at), sfx.at[at], rfx.at[at], x_dev)

    def copy_z(at, side, dev):
        return remote(span(held1, at, b, 0, slots), run(from_x, at + 1 - side), sfz.at[at], rfz.at[at + 1 - side], dev)

    def add(at, other, spot):
        merge(held1, (at * PAIR + b) * slots, other, spot * slots, slots)

    half = count // 2
    own_half = rows_of(c * half, half)

    def copy_act(k):
        src, dst = ((recv_b, out_other), (recv_a, in_other))[k]
        return remote(src.at[own_half], dst.at[own_half], s_in.at[k], r_in.at[k], y_dev)

    def share_act(k):
        dst = (out_other, in_other)[k]
        return remote(dst.at[own_half], dst.at[own_half], s_sh.at[k], r_sh.at[k], partner)

    def first_step(k):
        at = dest(k)
        fill(at)
        if k == 0:
            pl.semaphore_wait(ready.at[0], 1)
        copy_x(at).start()

    def second_step(k):
        at = dest(k)
        copy_x(at).wait_recv()
        add(at, from_y, at)

    def pass_on(turn):
        down = turn - line + a

        @pl.when((down >= 0) & (down < a))
        def _():
            @pl.when(a < line - 1)
            def _():
                copy_z(down, 1, left).wait_recv()
                add(down, from_x, down)

            copy_z(down, 1, left).start()

        upw = line - turn + a

        @pl.when((upw > a) & (upw < line))
        def _():
            @pl.when(a > 0)
            def _():
                copy_z(upw, 0, right).wait_recv()
                add(upw, from_x, upw + 1)

            copy_z(upw, 0, right).start()

    first_step(0)
    for k in range(2):
        copy_act(k).start()

    @pl.when(a > 0)
    def _():
        pl.semaphore_wait(ready.at[1], 1)

    @pl.when(a < line - 1)
    def _():
        pl.semaphore_wait(ready.at[2], 1)

    for step in range(1, line + 1):
        if step < line:
            first_step(step)
        if step == 1:
            for k, dev, slot in same_core:
                vec_copy(k, dev, slot // 2).wait()
            vec_out[...] = vec_plane[0] + vec_plane[1] + vec_plane[2] + vec_plane[3]
            for k, at in planes:
                vec_copy_z(k, at, a).start()
            vec_line[a] = vec_out[...]
        second_step(step - 1)
        if step < line:
            pass_on(step)

    for k, at in planes:
        vec_copy_z(k, at, at).wait()
    vec_sum = vec_line[0]
    for p in range(1, line):
        vec_sum = vec_sum + vec_line[p]
    vec_out[...] = vec_sum

    @pl.when(a > 0)
    def _():
        copy_z(a, 0, right).wait_recv()

    @pl.when(a < line - 1)
    def _():
        copy_z(a, 1, left).wait_recv()

    def finish(n, carry):
        value = held1[(a * PAIR + b) * slots + n].astype(F32)
        value += jnp.where(a > 0, from_x[(a + 1) * slots + n].astype(F32), 0.0)
        value += jnp.where(a < line - 1, from_x[a * slots + n].astype(F32), 0.0)
        total_out[n] = value
        return carry + jnp.sum((value * value).reshape(-1, 8, LANES), 0)

    square = lax.fori_loop(0, slots, finish, jnp.zeros((8, LANES), F32))
    chips = line * PAIR * 2
    row = lax.broadcasted_iota(jnp.int32, (8, LANES), 0)
    weight = jnp.where(row < 6, 1.0 / (chips * CORES), 1.0 / chips)
    for k in range(vec_sum.shape[1] // LANES):
        tile = vec_sum[:, k * LANES : (k + 1) * LANES]
        square += weight * tile * tile
    square_out[...] = square

    def sq_copy(k, dev, slot):
        return remote(square_out, sq_plane.at[slot], s_q.at[k], r_q.at[slot], dev)

    me = here * 2 + c
    for k, dev, _ in plane:
        sq_copy(k, dev, me).start()
    sq_plane[me] = square

    for k in range(2):
        copy_act(k).wait_recv()
        share_act(k).start()

    for k, dev, slot in plane:
        sq_copy(k, dev, slot).wait()
    square = sq_plane[0]
    for k in range(1, 8):
        square = square + sq_plane[k]
    square_out[...] = square

    def sq_copy_z(k, at, slot):
        return remote(square_out, sq_line.at[slot], s_qz.at[k], r_qz.at[slot], device(at, b, y, c))

    for k, at in planes:
        sq_copy_z(k, at, a).start()
    sq_line[a] = square

    for k in range(2):
        share_act(k).wait()
        copy_act(k).wait_send()
    for m in range(count // MLP_ROWS):
        swap(send_b, recv_b, sb, rb, m, MLP_ROWS).wait_send()
        swap(send_c, recv_c, sc, rc, m, MLP_ROWS).wait_send()
    for i in range(steps):
        swap(send_a, recv_a, sd, rd, i, QB).wait_send()
    keep_out.wait()
    keep_in.wait()

    def gone(at, carry):
        copy_x(at).wait_send()

        @pl.when(at != a)
        def _():
            copy_z(at, 0, right).wait_send()

        return carry

    lax.fori_loop(0, line, gone, 0)
    for k, at in planes:
        sq_copy_z(k, at, at).wait()
    square = sq_line[0]
    for p in range(1, line):
        square = square + sq_line[p]
    square_out[...] = square


def layer(table, where_from, tokens, segments, cotangent, master, shared, split, line):
    _, count, width = tokens.shape
    _, slots, size, _ = master.shape
    pair = 2 * size
    total = line * PAIR * slots
    hidden = 2 * (split.shape[1] - 3 * size)
    blocks = table.shape[1]
    steps = count // QB
    halves = count // MLP_ROWS
    spans = sum((i + 1 - max(0, i - 2)) * QB for i in range(steps))
    wide_vec = -(-split.shape[1] // LANES) * LANES
    direct = width // size
    x_blocks = (blocks - direct) // 2
    y_blocks = direct + x_blocks
    vm = lambda shape, kind=BF16: pltpu.VMEM(shape, kind)
    dma = lambda *n: pltpu.SemaphoreType.DMA(n)
    anywhere = pl.BlockSpec(memory_space=pl.ANY)
    inside = pl.BlockSpec(memory_space=pltpu.VMEM)
    scalars = pl.BlockSpec(memory_space=pltpu.SMEM)
    act = (count, width)
    block = (packed_rows(size), LANES)
    vec = (8, wide_vec)
    S = jax.ShapeDtypeStruct
    return pl.pallas_call(
        functools.partial(layer_kernel, (size, width, count, line, slots)),
        out_shape=(S((slots,) + block, F32), S(vec, F32), S((8, LANES), F32)) + (S(act, BF16),) * 4,
        in_specs=[scalars, anywhere, anywhere, inside, anywhere, anywhere, inside, inside, anywhere, scalars],
        out_specs=(inside, inside, inside) + (anywhere,) * 4,
        scratch_shapes=[
            vm(act),
            vm(act),
            vm((slots, size, size), F32),
            vm((total,) + block),
            vm((total,) + block),
            vm((max(x_blocks, (line + 1) * slots),) + block),
            vm((max(y_blocks, line * slots),) + block),
            pltpu.SMEM((1, blocks), jnp.int32),
            vm(split.shape, F32),
            vm((width, 3 * pair)),
            vm((pair, width)),
            vm((width, hidden)),
            vm((hidden, width)),
            vm((spans, QB), F32),
            vm(act),
            vm((count, pair)),
            vm((count, pair)),
            vm((count, pair)),
            vm((pair, count)),
            vm((pair, count)),
            vm((pair, count)),
            vm((8, count), F32),
            vm(act),
            vm(act),
            vm(act),
            vm(act),
            vm(act),
            vm(act),
            vm(act, F32),
            vm(act),
            vm((count, hidden)),
            vm((count, hidden)),
            vm((count, pair), F32),
            vm((count, pair), F32),
            vm((pair, count)),
            vm((8, 3 * pair), F32),
            vm((16, hidden), F32),
            vm(vec, F32),
            vm((4,) + vec, F32),
            vm((line,) + vec, F32),
            vm((8, 8, LANES), F32),
            vm((line, 8, LANES), F32),
            dma(3),
            dma(2),
        ]
        + [dma(line)] * 11
        + [dma(1), dma(1)]
        + [dma(2, line)] * 3
        + [dma(2), dma(2)]
        + [dma(steps), dma(steps), dma(halves), dma(halves), dma(halves), dma(halves), dma(steps), dma(steps)]
        + [dma(8)] * 4
        + [pltpu.SemaphoreType.REGULAR((3,)), dma(line), dma(line), dma(line), dma(line + 1)]
        + [dma(8), dma(4), dma(line), dma(line), dma(8), dma(8), dma(line), dma(line), dma(2), dma(2), dma(2), dma(2)],
        compiler_params=pltpu.CompilerParams(collective_id=2, has_side_effects=True, vmem_limit_bytes=63 * MIB),
        name="layer",
    )(table, table, tokens, segments, cotangent, master, shared, split, split, where_from)


def halves_of(value):
    high = value.astype(BF16)
    return high, (value - high.astype(F32)).astype(BF16)


def fine_dot(a, b):
    a_high, a_low = halves_of(a)
    b_high, b_low = halves_of(b)
    return dot(a_high, b_high) + (dot(a_high, b_low) + dot(a_low, b_high))


def update_kernel(
    grad,
    square,
    vec,
    master,
    stats,
    roots,
    shared,
    shared_state,
    split,
    split_state,
    out_mine,
    out_theirs,
    in_mine,
    in_theirs,
    norm_out,
    clipped_out,
    master_out,
    copy_out,
    stats_out,
    shared_grad,
    shared_new_state,
    shared_new,
    split_grad,
    split_new_state,
    split_new,
    output,
    input_grad,
    acts,
    wide,
    grad_v,
    master_v,
    stats_v,
    roots_v,
    clipped_v,
    copy_v,
    sem_act,
    sem_wide,
    sem_in,
    sem_out,
):
    slots, size = master.shape[1], master.shape[2]
    y = lax.axis_index("tensor") // CORES
    _, count, _ = acts.shape
    chunk = count // 4
    fetch = []
    for k, ref in enumerate((out_mine, out_theirs, in_mine, in_theirs)):
        fetch.append(pltpu.make_async_copy(ref, acts.at[k], sem_act.at[k]))

    def slot_loads(n):
        return [
            pltpu.make_async_copy(src.at[n], dst.at[n], sem_in.at[k, n])
            for k, (src, dst) in enumerate(
                ((grad, grad_v), (roots.at[0], roots_v), (stats.at[0], stats_v), (master.at[0], master_v))
            )
        ]

    for n in range(slots):
        for copy in slot_loads(n):
            copy.start()
    for copy in fetch:
        copy.start()

    def wide_copy(k, n):
        target = (output, output, input_grad, input_grad)[k]
        seq = y if k % 2 == 0 else 1 - y
        rows = rows_of(n * chunk, chunk)
        return pltpu.make_async_copy(wide.at[k, rows], target.at[seq, rows], sem_wide.at[k, n])

    def widen(k):
        fetch[k].wait()

        def one(n, carry):
            rows = rows_of(n * chunk, chunk)
            wide[k, rows, :] = acts[k, rows, :].astype(F32)
            wide_copy(k, n).start()
            return carry

        lax.fori_loop(0, 4, one, 0)

    norm = jnp.sqrt(jnp.sum(square[...], keepdims=True))
    factor = 1.0 / jnp.maximum(norm, 1.0)
    norm_out[...] = norm
    def slot_copies(n):
        return [
            pltpu.make_async_copy(src.at[n], dst.at[0, n], sem_out.at[k, n])
            for k, (src, dst) in enumerate(
                ((clipped_v, clipped_out), (master_v, master_out), (copy_v, copy_out), (stats_v, stats_out))
            )
        ]

    def slot(n, carry):
        for copy in slot_loads(n):
            copy.wait()
        clipped = jnp.concatenate(unpack_block(grad_v[n] * factor, size), 1)
        clipped_v[n] = clipped
        low = clipped.astype(BF16)
        stats_v[n, 0] = DECAY * stats_v[n, 0] + (1.0 - DECAY) * dot_nt(low, low)
        stats_v[n, 1] = DECAY * stats_v[n, 1] + (1.0 - DECAY) * dot_tn(low, low)
        step = fine_dot(fine_dot(roots_v[n, 0], clipped), roots_v[n, 1])
        new = master_v[n] - RATE * step
        master_v[n] = new
        copy_v[n] = new.astype(BF16)
        for copy in slot_copies(n):
            copy.start()
        return carry

    early = slots // 2
    lax.fori_loop(0, early, slot, 0, unroll=True)
    widen(0)
    widen(1)
    lax.fori_loop(early, slots, slot, 0, unroll=True)
    for k in range(2, 4):
        widen(k)
    for raw, value, state, g_out, s_out, v_out in (
        (vec[0 : shared.shape[0], : shared.shape[1]], shared, shared_state, shared_grad, shared_new_state, shared_new),
        (vec[pl.ds(6 + y, 1), :][:, : split.shape[1]], split, split_state, split_grad, split_new_state, split_new),
    ):
        g = raw * factor
        moment = DECAY * state[...] + (1.0 - DECAY) * g * g
        g_out[...] = g
        s_out[...] = moment
        v_out[...] = value[...] - RATE_VECTOR * g * lax.rsqrt(moment)

    def done(n, carry):
        for copy in slot_copies(n):
            copy.wait()
        return carry

    lax.fori_loop(0, slots, done, 0)
    for k in range(4):
        for n in range(4):
            wide_copy(k, n).wait()


def update(grad, square, vec, master, stats, roots, shared, shared_state, split, split_state, acts):
    _, slots, size, _ = master.shape
    count, width = acts[0].shape
    anywhere = pl.BlockSpec(memory_space=pl.ANY)
    inside = pl.BlockSpec(memory_space=pltpu.VMEM)
    S = jax.ShapeDtypeStruct
    vm = lambda shape, kind=F32: pltpu.VMEM(shape, kind)
    dma = lambda *n: pltpu.SemaphoreType.DMA(n)
    return pl.pallas_call(
        update_kernel,
        out_shape=(S((1, 1), F32), S(master.shape, F32), S(master.shape, F32), S(master.shape, BF16), S(stats.shape, F32))
        + (S(shared.shape, F32),) * 3
        + (S(split.shape, F32),) * 3
        + (S((2, count, width), F32),) * 2,
        in_specs=[anywhere, inside, inside] + [anywhere] * 3 + [inside] * 4 + [anywhere] * 4,
        out_specs=(inside,) + (anywhere,) * 4 + (inside,) * 6 + (anywhere,) * 2,
        scratch_shapes=[
            vm((4, count, width), BF16),
            vm((4, count, width)),
            vm(grad.shape),
            vm((slots, size, size)),
            vm((slots, 2, size, size)),
            vm((slots, 2, size, size)),
            vm((slots, size, size)),
            vm((slots, size, size), BF16),
            dma(4),
            dma(4, 4),
            dma(4, slots),
            dma(4, slots),
        ],
        compiler_params=pltpu.CompilerParams(vmem_limit_bytes=63 * MIB),
        name="update",
    )(grad, square, vec, master, stats, roots, shared, shared_state, split, split_state, *acts)


def body(
    tokens,
    segments,
    cotangent,
    block_owner_slots,
    master_weights,
    statistics,
    inverse_roots,
    shared_vectors,
    shared_state,
    split_bias,
    split_state,
):
    slots = master_weights.shape[1]
    ranks = lax.axis_size("dp")
    line = ranks // PAIR
    blocks = block_owner_slots.shape[1]
    number = jnp.arange(blocks, dtype=jnp.int32)
    hit = block_owner_slots[:, :, None] == jnp.arange(ranks * slots, dtype=jnp.int32)[None, None]
    where_from = jnp.sum(jnp.where(hit, number[None, :, None] - blocks, 0), 1) + blocks

    grad, vec, square, out, out_other, d_in, d_in_other = layer(
        block_owner_slots, where_from, tokens, segments, cotangent, master_weights, shared_vectors, split_bias, line
    )
    done = update(
        grad,
        square,
        vec,
        master_weights,
        statistics,
        inverse_roots,
        shared_vectors,
        shared_state,
        split_bias,
        split_state,
        (out, out_other, d_in, d_in_other),
    )
    return (done[11], done[12], done[0].reshape(())) + tuple(done[1:11])


def solution(mesh):
    placed = (
        P("dp", None, None),
        P("dp", None),
        P("dp", None, None),
        P("tensor", None),
        P("tensor", "dp", None, None),
        P("tensor", "dp", None, None, None),
        P("tensor", "dp", None, None, None),
        P(),
        P(),
        P("tensor", None),
        P("tensor", None),
    )
    return jax.shard_map(
        body,
        mesh=mesh,
        in_specs=placed,
        out_specs=(
            P("dp", None, None),
            P("dp", None, None),
            P(),
            P("tensor", "dp", None, None),
            P("tensor", "dp", None, None),
            P("tensor", "dp", None, None),
            P("tensor", "dp", None, None, None),
            P(),
            P(),
            P(),
            P("tensor", None),
            P("tensor", None),
            P("tensor", None),
        ),
        check_vma=False,
    )
```

```python
import functools
import math

import jax
import jax.numpy as jnp
from jax import lax
from jax.sharding import PartitionSpec as P
import jax.experimental.pallas as pl
import jax.experimental.pallas.tpu as pltpu

MESH = pl.DeviceIdType.MESH
PAIR = 2
CORES = 2
LANES = 128
MIB = 2**20
HEAD = 64
EPS = 1e-05
NEG = -1000000000.0
TOP = 3.0e38
QB = 256
MLP_ROWS = 512
LN_ROWS = 128
DECAY = 0.5
RATE = 0.3
RATE_VECTOR = 0.2
F32 = jnp.float32
BF16 = jnp.bfloat16


def packed_rows(size):
    return size * size // LANES


def pack_block(block):
    half = block.shape[0] // 2
    return block[:, :LANES], jnp.concatenate([block[:half, LANES:], block[half:, LANES:]], 1)


def unpack_block(packed, size):
    tail = packed[size:]
    h = LANES // 2
    return packed[:size], jnp.concatenate([tail[:, :h], tail[:, h:]], 0)


def place():
    d = lax.axis_index("dp")
    t = lax.axis_index("tensor")
    return d // PAIR, lax.rem(d, PAIR), t // CORES, lax.rem(t, CORES)


def device(a, b, y, c):
    return (a * PAIR + b, y * CORES + c)


def remote(src, dst, s, r, dev):
    return pltpu.make_async_remote_copy(src_ref=src, dst_ref=dst, send_sem=s, recv_sem=r, device_id=dev, device_id_type=MESH)


def dot(a, b):
    return lax.dot_general(a, b, (((1,), (0,)), ((), ())), preferred_element_type=F32)


def dot_nt(a, b):
    return lax.dot_general(a, b, (((1,), (1,)), ((), ())), preferred_element_type=F32)


def dot_tn(a, b):
    return lax.dot_general(a, b, (((0,), (0,)), ((), ())), preferred_element_type=F32)


def centre_of(value):
    mean = jnp.mean(value, -1, keepdims=True)
    centred = value - mean
    spread = jnp.mean(centred * centred, -1, keepdims=True)
    return centred, lax.rsqrt(spread + EPS)


def norm_back(value, d_out, gain):
    centred, scale = centre_of(value)
    hat = centred * scale
    d_hat = d_out * gain
    back = scale * (d_hat - jnp.mean(d_hat, -1, keepdims=True) - hat * jnp.mean(d_hat * hat, -1, keepdims=True))
    return back, hat


def rows_of(start, count):
    return pl.ds(pl.multiple_of(start, count), count)


def column_sum(value):
    return jnp.sum(value, 0, keepdims=True)


def hand_on(line, at):
    turn = lambda dest: dest + line - at if dest < at else line - dest + at
    return sorted(range(line), key=lambda dest: line if dest == at else turn(dest))


def layer_kernel(
    dims,
    table,
    table_src,
    tokens,
    segments,
    cotangent,
    master,
    shared,
    split,
    split_src,
    table_row,
    total_out,
    vec_out,
    square_out,
    out_own,
    out_other,
    in_own,
    in_other,
    x,
    dy,
    owned,
    held0,
    held1,
    from_x,
    from_y,
    other_table,
    other_split,
    inverse,
    where_from,
    w_qkv,
    w_out,
    w_fc,
    w_proj,
    cap,
    h_one,
    q_s,
    k_s,
    v_s,
    k_t,
    v_t,
    mixed_t,
    logsum,
    send_a,
    recv_a,
    send_b,
    recv_b,
    send_c,
    recv_c,
    second,
    h_two,
    gelu_s,
    d_hid,
    d_keys,
    d_vals,
    d_query_t,
    bias_qkv,
    bias_fc,
    vectors,
    vec_plane,
    vec_line,
    sq_plane,
    sq_line,
    sem_in,
    sem_out,
    s_zr,
    s_zl,
    r_z,
    s_x,
    r_x,
    s_y,
    r_y,
    s_xy,
    r_xy,
    s_yx,
    r_yx,
    s_g,
    r_g,
    s_zgr,
    s_zgl,
    r_zg,
    s_t,
    r_t,
    sa,
    ra,
    sb,
    rb,
    sc,
    rc,
    sd,
    rd,
    smx,
    rmx,
    smy,
    rmy,
    ready,
    sfx,
    rfx,
    sfz,
    rfz,
    s_v,
    r_v,
    s_vz,
    r_vz,
    s_q,
    r_q,
    s_qz,
    r_qz,
    s_in,
    r_in,
    s_sh,
    r_sh,
):
    size, width, count, line, slots = dims
    a, b, y, c = place()
    ob = 1 - b
    partner = device(a, b, y, 1 - c)
    x_dev, y_dev = device(a, ob, y, c), device(a, b, 1 - y, c)
    right = device(jnp.minimum(a + 1, line - 1), b, y, c)
    left = device(jnp.maximum(a - 1, 0), b, y, c)
    plane = []
    for k in range(1, 8):
        fb, fy, fc = lax.rem(b + k // 4, 2), lax.rem(y + k // 2 % 2, 2), lax.rem(c + k % 2, 2)
        plane.append((k, device(a, fb, fy, fc), fb * 4 + fy * 2 + fc))
    planes = [(k, lax.rem(a + k, line)) for k in range(1, line)]
    barrier = pltpu.get_barrier_semaphore()
    for _, dev, _ in plane:
        pl.semaphore_signal(barrier, inc=1, device_id=dev, device_id_type=MESH)
    for _, at in planes:
        pl.semaphore_signal(barrier, inc=1, device_id=device(at, b, y, c), device_id_type=MESH)

    grid = width // size
    hidden_t = split.shape[1] - 3 * size
    fold = hidden_t // size
    pair = 2 * size
    cut_a, cut_b = 3 * grid, 4 * grid
    cut_c = cut_b + grid * fold
    blocks = cut_c + grid * fold
    heads = pair // HEAD
    hidden = 2 * hidden_t
    steps = count // QB
    h = LANES // 2

    load_m = pltpu.make_async_copy(master.at[0], owned, sem_in.at[0])
    load_m.start()
    load_x = pltpu.make_async_copy(tokens.at[y], x, sem_in.at[1])
    load_x.start()
    load_dy = pltpu.make_async_copy(cotangent.at[y], dy, sem_in.at[2])
    load_dy.start()

    last = slots // 3
    most = slots - last

    def span(ref, at, bb, first, number):
        return ref.at[pl.ds((at * PAIR + bb) * slots + first, number)]

    def z_copy(at, s, dev):
        return remote(span(held0, at, b, 0, slots), span(held0, at, b, 0, slots), s.at[at], r_z.at[at], dev)

    def x_copy(at):
        return remote(span(held0, at, b, 0, slots), span(held0, at, b, 0, slots), s_x.at[at], r_x.at[at], x_dev)

    def y_copy(at, number):
        return remote(span(held0, at, b, 0, number), span(held1, at, b, 0, number), s_y.at[at], r_y.at[at], y_dev)

    def y_share(at):
        return most - (1 + at % 2 if last else most // 2)

    def yx_copy(at):
        n = y_share(at)
        return remote(span(held0, at, ob, 0, n), span(held1, at, ob, 0, n), s_yx.at[at], r_yx.at[at], y_dev)

    def xy_copy(at):
        n = y_share(at)
        return remote(span(held1, at, b, n, most - n), span(held1, at, b, n, most - n), s_xy.at[at], r_xy.at[at], x_dev)

    def corner_copy():
        return remote(span(held0, a, ob, most, last), span(held1, a, ob, most, last), s_g.at[0], r_g.at[0], y_dev)

    def zg_copy(at, k, s, dev):
        where = span(held1, at, (b, ob)[k], most, last)
        return remote(where, where, s.at[k, at], r_zg.at[k, at], dev)

    load_m.wait()
    mine = (a * PAIR + b) * slots

    def pack(s, carry):
        left_part, right_part = pack_block(owned[s].astype(BF16))
        held0[mine + s, :size] = left_part
        held0[mine + s, size:] = right_part
        return carry

    lax.fori_loop(0, slots, pack, 0)
    pl.semaphore_wait(barrier, 7 + line - 1)

    @pl.when(a < line - 1)
    def _():
        z_copy(a, s_zr, right).start()

    @pl.when(a > 0)
    def _():
        z_copy(a, s_zl, left).start()

    small = [
        remote(table_src, other_table, s_t.at[0], r_t.at[0], y_dev),
        remote(split_src, other_split, s_t.at[1], r_t.at[1], y_dev),
    ]
    for copy in small:
        copy.start()
    x_copy(a).start()
    y_copy(a, slots).start()

    vectors[...] = jnp.zeros_like(vectors)
    gain1, shift1 = shared[0:1, :], shared[1:2, :]
    gain2, shift2 = shared[2:3, :], shared[3:4, :]
    out_bias, proj_bias = shared[4:5, :], shared[5:6, :]
    load_x.wait()

    def norm_one(i, carry):
        where = rows_of(i * LN_ROWS, LN_ROWS)
        centred, scale = centre_of(x[where, :].astype(F32))
        h_one[where, :] = (centred * scale * gain1 + shift1).astype(BF16)
        return carry

    lax.fori_loop(0, count // LN_ROWS, norm_one, 0)

    def arrivals(j):
        for ok, at, s, dev, more in (
            (a - j >= 0, a - j, s_zr, right, a < line - 1),
            (a + j < line, a + j, s_zl, left, a > 0),
        ):

            @pl.when(ok)
            def _():
                z_copy(at, s, dev).wait_recv()

                @pl.when(more)
                def _():
                    z_copy(at, s, dev).start()

                x_copy(at).start()
                y_copy(at, most).start()

    arrivals(1)
    seg_row = segments[pl.ds(y, 1), :].astype(F32)
    seg_col = d_keys.at[:, :LANES]
    seg_col[...] = jnp.transpose(jnp.broadcast_to(seg_row, (LANES, count)))
    reach = []
    at = 0
    for i in range(steps):
        first = max(0, i - 2) * QB
        wide = (i + 1) * QB - first
        reach.append((first, wide, at))
        key_seg = seg_col[first : first + wide, :]
        key_seg = jnp.concatenate([key_seg] * (QB // LANES), 1)
        key_at = lax.broadcasted_iota(jnp.int32, (wide, QB), 0) + first
        query_at = lax.broadcasted_iota(jnp.int32, (wide, QB), 1) + i * QB
        allowed = (key_seg == seg_row[:, i * QB : (i + 1) * QB]) & (key_at <= query_at)
        cap[at : at + wide, :] = jnp.where(allowed, TOP, NEG)
        at += wide
    x_copy(a).wait_recv()
    if last:
        corner_copy().start()
    for j in range(2, line):
        arrivals(j)
    spots = line * PAIR * slots
    hit = lax.broadcasted_iota(jnp.int32, (spots, blocks), 0) == table_row[0:1, :]
    number = lax.broadcasted_iota(jnp.int32, (spots, blocks), 1)
    found = jnp.sum(jnp.where(hit, number - blocks, 0), 1, keepdims=True) + blocks
    inverse[...] = jnp.broadcast_to(jnp.clip(found, 0, spots - 1), inverse.shape)
    load_inverse = pltpu.make_async_copy(inverse, where_from, sem_in.at[3])
    load_inverse.start()
    for copy in small:
        copy.wait()
    biases = (split, other_split)
    bias_qkv[0:1, :] = jnp.concatenate([biases[u][0:1, g * size : (g + 1) * size] for g in range(3) for u in range(2)], 1)
    bias_fc[0:1, :] = jnp.concatenate([biases[u][0:1, 3 * size :] for u in range(2)], 1)

    y_copy(a, slots).wait_recv()

    def line_arrivals(j):
        for ok, at, s, dev, more in (
            (a - j >= 0, a - j, s_zgr, right, a < line - 1),
            (a + j < line, a + j, s_zgl, left, a > 0),
        ):

            @pl.when(ok)
            def _():
                for k in range(2):
                    zg_copy(at, k, s, dev).wait_recv()

                if j < line - 1:

                    @pl.when(more)
                    def _():
                        for k in range(2):
                            zg_copy(at, k, s, dev).start()

    if last:
        corner_copy().wait_recv()

        @pl.when(a < line - 1)
        def _():
            for k in range(2):
                zg_copy(a, k, s_zgr, right).start()

        @pl.when(a > 0)
        def _():
            for k in range(2):
                zg_copy(a, k, s_zgl, left).start()

        line_arrivals(1)

    for at in range(line):

        @pl.when(at != a)
        def _():
            x_copy(at).wait_recv()
            y_copy(at, most).wait_recv()

        yx_copy(at).start()
        xy_copy(at).start()
    if last:
        for j in range(2, line - 1):
            line_arrivals(j)
    def block_at(u, block):
        ref, lookup = ((held0, table), (held1, other_table))[u]
        return unpack_block(ref[lookup[0, block]], size)

    def put_pair(ref, row, col, first, other):
        left0, right0 = first
        left1, right1 = other
        where = rows_of(row * size, size)
        ref[where, col : col + LANES] = left0
        ref[where, col + LANES : col + 2 * LANES] = jnp.concatenate([right0, left1[:, :h]], 1)
        ref[where, col + 2 * LANES : col + 3 * LANES] = jnp.concatenate([left1[:, h:], right1], 1)

    def build_attention(u):
        def one(r, carry):
            where = rows_of(r * size, size)
            for g in range(3):
                left_part, right_part = block_at(u, r * 3 + g)
                col = g * pair
                if u == 0:
                    w_qkv[where, col : col + LANES] = left_part
                    w_qkv[where, col + LANES : col + LANES + h] = right_part
                else:
                    tile = w_qkv[where, col + LANES : col + 2 * LANES]
                    w_qkv[where, col + LANES : col + 2 * LANES] = jnp.concatenate([tile[:, :h], left_part[:, :h]], 1)
                    w_qkv[where, col + 2 * LANES : col + 3 * LANES] = jnp.concatenate([left_part[:, h:], right_part], 1)
            return carry

        lax.fori_loop(0, grid, one, 0)

    def build_rest(u):
        for j in range(0, grid, 2):
            put_pair(w_out, u, j * size, block_at(u, cut_a + j), block_at(u, cut_a + j + 1))

        def fc(r, carry):
            for f in range(0, fold, 2):
                block = cut_b + r * fold + f
                put_pair(w_fc, r, u * hidden_t + f * size, block_at(u, block), block_at(u, block + 1))
            return carry

        lax.fori_loop(0, grid, fc, 0)

        def proj(f, carry):
            for r in range(0, grid, 2):
                block = cut_c + f * grid + r
                put_pair(w_proj, u * fold + f, r * size, block_at(u, block), block_at(u, block + 1))
            return carry

        lax.fori_loop(0, fold, proj, 0)

    def make_qkv(u):
        low, high = ((0, size), (LANES, pair))[u]

        def one(i, carry):
            where = rows_of(i * QB, QB)
            for g in range(3):
                cols = slice(g * pair + low, g * pair + high)
                got = dot(h_one[where, :], w_qkv[:, cols]) + bias_qkv[0:1, cols]
                if g == 0:
                    q_s[where, low:high] = (got.astype(BF16).astype(F32) * HEAD ** (-0.5)).astype(BF16)
                else:
                    row, col = ((k_s, k_t), (v_s, v_t))[g - 1]
                    row[where, low:high] = got.astype(BF16)
                    if u == 0:
                        row[where, high : high + h] = jnp.zeros((QB, h), BF16)
                    col[low:high, where] = jnp.transpose(got).astype(BF16)
            return carry

        lax.fori_loop(0, steps, one, 0)

    def head_of(value, n):
        lane = lax.broadcasted_iota(jnp.int32, value.shape, 1)
        return jnp.where((lane < HEAD) if n % 2 == 0 else (lane >= HEAD), value, jnp.zeros_like(value))

    def tile_of(n):
        return slice(n // 2 * LANES, (n // 2 + 1) * LANES)

    def attend(i, n):
        first, wide, at = reach[i]
        query_rows = slice(i * QB, (i + 1) * QB)
        keys = k_s[first : first + wide, tile_of(n)]
        query = head_of(q_s[query_rows, tile_of(n)], n)
        scores = jnp.minimum(dot_nt(keys, query), cap[at : at + wide, :])
        top = jnp.max(scores, 0, keepdims=True)
        expo = jnp.exp(scores - top)
        total = jnp.sum(expo, 0, keepdims=True)
        got = dot(v_t[n * HEAD : (n + 1) * HEAD, first : first + wide], expo.astype(BF16))
        mixed_t[n * HEAD : (n + 1) * HEAD, query_rows] = (got * (1.0 / total)).astype(BF16)
        logsum[n : n + 1, query_rows] = top + jnp.log(total)

    own_heads, other_heads = range(heads // 2), range(heads // 2, heads)
    build_attention(0)
    make_qkv(0)
    for i in range(steps):
        for n in own_heads:
            attend(i, n)
    build_rest(0)

    for at in range(line):
        yx_copy(at).wait_recv()
        xy_copy(at).wait_recv()
    if last and line > 2:
        line_arrivals(line - 1)
    build_attention(1)
    make_qkv(1)
    build_rest(1)

    def swap(send, recv, s, r, at, rows):
        where = pl.ds(at * rows, rows) if isinstance(at, int) else rows_of(at * rows, rows)
        return remote(send.at[where], recv.at[where], s.at[at], r.at[at], partner)

    for i in range(steps):
        for n in other_heads:
            attend(i, n)
        query_rows = slice(i * QB, (i + 1) * QB)
        send_a[query_rows, :] = dot_tn(mixed_t[:, query_rows], w_out[...]).astype(BF16)
        swap(send_a, recv_a, sa, ra, i, QB).start()

    load_dy.wait()
    load_inverse.wait()

    strips = hidden // pair
    curve = math.sqrt(2.0 / math.pi)
    bias_sum = bias_fc.at[8:16]
    bias_sum[...] = jnp.zeros(bias_sum.shape, F32)

    def mlp(m, carry):
        for i in range(MLP_ROWS // QB):
            swap(send_a, recv_a, sa, ra, m * (MLP_ROWS // QB) + i, QB).wait_recv()

        def norm_two(i, inner):
            where = rows_of(m * MLP_ROWS + i * LN_ROWS, LN_ROWS)
            total = send_a[where, :].astype(F32) + recv_a[where, :].astype(F32)
            value = x[where, :].astype(F32) + total + out_bias
            second[where, :] = value
            centred, scale = centre_of(value)
            h_two[where, :] = (centred * scale * gain2 + shift2).astype(BF16)
            return inner

        lax.fori_loop(0, MLP_ROWS // LN_ROWS, norm_two, 0)
        where = rows_of(m * MLP_ROWS, MLP_ROWS)

        def strip(n, inner):
            cols = pl.ds(pl.multiple_of(n * pair, LANES), pair)
            hid = dot(h_two[where, :], w_fc[:, cols]) + bias_fc[0:1, cols]
            square = hid * hid
            bend = jnp.tanh(curve * hid * (1.0 + 0.044715 * square))
            up = 0.5 * (1.0 + bend)
            gelu_s[where, cols] = (hid * up).astype(BF16)
            slope = up + 0.5 * hid * (1.0 - bend * bend) * (curve * (1.0 + 3 * 0.044715 * square))
            d_hid[where, cols] = slope.astype(BF16)
            return inner

        lax.fori_loop(0, strips, strip, 0, unroll=True)
        send_b[where, :] = dot(gelu_s[where, :], w_proj[...]).astype(BF16)
        swap(send_b, recv_b, sb, rb, m, MLP_ROWS).start()
        return carry

    lax.fori_loop(0, count // MLP_ROWS, mlp, 0)

    def mlp_back(m, carry):
        where = rows_of(m * MLP_ROWS, MLP_ROWS)

        def strip(n, inner):
            cols = pl.ds(pl.multiple_of(n * pair, LANES), pair)
            back = (dot_nt(dy[where, :], w_proj[cols, :]) * d_hid[where, cols].astype(F32)).astype(BF16)
            d_hid[where, cols] = back
            bias_sum[0:1, cols] += column_sum(back.astype(F32))
            return inner

        lax.fori_loop(0, strips, strip, 0, unroll=True)
        send_c[where, :] = dot_nt(d_hid[where, :], w_fc[...]).astype(BF16)
        swap(send_c, recv_c, sc, rc, m, MLP_ROWS).start()
        return carry

    for at in range(line):
        x_copy(at).wait_send()
        yx_copy(at).wait_send()
        xy_copy(at).wait_send()

        @pl.when(at == a)
        def _():
            y_copy(at, slots).wait_send()

        @pl.when(at != a)
        def _():
            y_copy(at, most).wait_send()

        @pl.when((at <= a) & (a < line - 1))
        def _():
            z_copy(at, s_zr, right).wait_send()
            for k in range(2 if last else 0):
                zg_copy(at, k, s_zgr, right).wait_send()

        @pl.when((at >= a) & (a > 0))
        def _():
            z_copy(at, s_zl, left).wait_send()
            for k in range(2 if last else 0):
                zg_copy(at, k, s_zgl, left).wait_send()

    if last:
        corner_copy().wait_send()

    held = (held0, held1)

    def keep(ref, block, left_part, right_part):
        half = size // 2
        ref[block, :size, :] = left_part
        ref[block, size:, :] = jnp.concatenate([right_part[:half], right_part[half:]], 1)

    def keep_pair(u, tile, block):
        t0, t1, t2 = (tile[:, k * LANES : (k + 1) * LANES] for k in range(3))
        keep(held[u], block, t0, t1[:, :h])
        keep(held[u], block + 1, jnp.concatenate([t1[:, h:], t2[:, :h]], 1), t2[:, h:])

    def grad_proj(u, n):
        got = dot_tn(gelu_s[:, u * hidden_t + n * pair : u * hidden_t + (n + 1) * pair], dy[...]).astype(BF16)
        for s in range(2):
            for r in range(0, grid, 2):
                keep_pair(u, got[s * size : (s + 1) * size, r * size : (r + 2) * size], cut_c + (2 * n + s) * grid + r)

    def grad_fc(u, m):
        got = dot_tn(h_two[:, m * pair : (m + 1) * pair], d_hid[:, u * hidden_t : (u + 1) * hidden_t]).astype(BF16)
        for s in range(2):
            for f in range(0, fold, 2):
                keep_pair(u, got[s * size : (s + 1) * size, f * size : (f + 2) * size], cut_b + (2 * m + s) * fold + f)

    strip_blocks = 2 * grid
    few = strip_blocks // 2
    groups = []
    at_x = at_y = 0
    for first, number, kind in (
        (cut_c, few, 0),
        (cut_c + few, strip_blocks - few, 1),
        (cut_c + strip_blocks, strip_blocks, 1),
        (cut_b, 2 * fold, 1),
        (cut_b + 2 * fold, 2 * fold, 1),
        (cut_a, grid, 1),
        (0, 6, 1),
        (6, 6, 1),
    ):
        moved = number >> kind
        groups.append((kind, first, moved, at_x, at_y))
        at_x += moved * kind
        at_y += moved

    def cross_x(k):
        _, first, moved, at, _ = groups[k]
        return remote(held1.at[pl.ds(first + ob * moved, moved)], from_x.at[pl.ds(at, moved)], smx.at[k], rmx.at[k], x_dev)

    def kept(k):
        kind, first, moved, _, _ = groups[k]
        return first + b * moved * kind

    def cross_y(k):
        _, _, moved, _, at = groups[k]
        return remote(held1.at[pl.ds(kept(k), moved)], from_y.at[pl.ds(at, moved)], smy.at[k], rmy.at[k], y_dev)

    def merge(ref, start, other, at, number):
        def one(n, carry):
            ref[start + n] = (ref[start + n].astype(F32) + other[at + n].astype(F32)).astype(BF16)
            return carry

        lax.fori_loop(0, number, one, 0)

    def merge_x(k):
        _, _, moved, at, _ = groups[k]
        cross_x(k).wait_recv()
        merge(held1, kept(k), from_x, at, moved)
        cross_y(k).start()

    def merge_y(k):
        _, _, moved, _, at = groups[k]
        cross_y(k).wait_recv()
        merge(held0, kept(k), from_y, at, moved)

    for n in range(fold // 2):
        grad_proj(1, n)
        if n == 0:
            cross_y(0).start()
            cross_x(1).start()
        else:
            cross_x(2).start()
    lax.fori_loop(0, count // MLP_ROWS, mlp_back, 0)
    grad_fc(1, 0)
    cross_x(3).start()
    merge_x(1)
    grad_fc(1, 1)

    for m in range(count // MLP_ROWS):
        swap(send_b, recv_b, sb, rb, m, MLP_ROWS).wait_recv()
        swap(send_c, recv_c, sc, rc, m, MLP_ROWS).wait_recv()

    def norm_two_back(i, carry):
        d_gain, d_shift, d_bias, d_proj = carry
        where = rows_of(i * LN_ROWS, LN_ROWS)
        value = second[where, :]
        total = send_b[where, :].astype(F32) + recv_b[where, :].astype(F32)
        recv_b[where, :] = (value + total + proj_bias).astype(BF16)
        d_norm = send_c[where, :].astype(F32) + recv_c[where, :].astype(F32)
        d_out = dy[where, :].astype(F32)
        back, hat = norm_back(value, d_norm, gain2)
        d_second = d_out + back
        second[where, :] = d_second
        low = d_second.astype(BF16)
        recv_c[where, :] = low
        return (
            d_gain + column_sum(d_norm * hat),
            d_shift + column_sum(d_norm),
            d_bias + column_sum(low.astype(F32)),
            d_proj + column_sum(d_out),
        )

    zero = jnp.zeros((1, width), F32)
    sums = lax.fori_loop(0, count // LN_ROWS, norm_two_back, (zero,) * 4)
    for k, row in enumerate(sums):
        vectors[2 + k : 3 + k, :width] = row
    d_low = recv_c
    keep_out = pltpu.make_async_copy(recv_b, out_own, sem_out.at[0])
    keep_out.start()
    merge_x(2)

    d_mixed = gelu_s.at[:, hidden_t : hidden_t + pair]
    d_qkv = (
        gelu_s.at[:, hidden_t + pair : hidden_t + 2 * pair],
        d_hid.at[:, hidden_t : hidden_t + pair],
        d_hid.at[:, hidden_t + pair : hidden_t + 2 * pair],
    )

    def make_d_mixed(i, carry):
        where = rows_of(i * QB, QB)
        d_mixed[where, :] = dot_nt(d_low[where, :], w_out[...]).astype(BF16)
        return carry

    lax.fori_loop(0, steps, make_d_mixed, 0)
    cross_x(4).start()
    def grad_out():
        got = dot(mixed_t[...], d_low[...]).astype(BF16)
        for u in range(2):
            for r in range(0, grid, 2):
                keep_pair(u, got[u * size : (u + 1) * size, r * size : (r + 2) * size], cut_a + r)

    d_vals[...] = jnp.zeros_like(d_vals)
    d_keys[...] = jnp.zeros_like(d_keys)

    def attend_back(i, n):
        first, wide, at = reach[i]
        query_rows = slice(i * QB, (i + 1) * QB)
        key_rows = slice(first, first + wide)
        tile = tile_of(n)
        keys = k_s[key_rows, tile]
        query = head_of(q_s[query_rows, tile], n)
        d_out = head_of(d_mixed[query_rows, tile], n)
        scores = jnp.minimum(dot_nt(keys, query), cap[at : at + wide, :])
        probs = jnp.exp(scores - logsum[n : n + 1, query_rows])
        d_probs = dot_nt(v_s[key_rows, tile], d_out)
        centre = jnp.sum(probs * d_probs, 0, keepdims=True)
        d_scores = (probs * (d_probs - centre)).astype(BF16)
        d_vals[key_rows, tile] += dot(probs.astype(BF16), d_out)
        d_keys[key_rows, tile] += dot(d_scores, query)
        got = dot(k_t[n * HEAD : (n + 1) * HEAD, key_rows], d_scores)
        d_query_t[n * HEAD : (n + 1) * HEAD, query_rows] = (got * HEAD ** (-0.5)).astype(BF16)

    def collect(u):
        low, high = ((0, size), (LANES, pair))[u]

        def one(i, carry):
            where = rows_of(i * QB, QB)
            d_qkv[0][where, low:high] = jnp.transpose(d_query_t[low:high, where].astype(F32)).astype(BF16)
            d_qkv[1][where, low:high] = d_keys[where, low:high].astype(BF16)
            d_qkv[2][where, low:high] = d_vals[where, low:high].astype(BF16)
            return carry

        lax.fori_loop(0, steps, one, 0)

    def grad_qkv(u, m):
        low, high = ((0, size), (LANES, pair))[u]
        for g in range(3):
            got = dot_tn(h_one[:, m * pair : (m + 1) * pair], d_qkv[g][:, low:high]).astype(BF16)
            for s in range(2):
                tile = got[s * size : (s + 1) * size]
                block = (2 * m + s) * 3 + g
                if u == 0:
                    keep(held0, block, tile[:, :LANES], tile[:, LANES:])
                else:
                    keep(held1, block, jnp.concatenate([tile[:, h:LANES], tile[:, LANES : LANES + h]], 1), tile[:, LANES + h :])

    d_query_t[size - h : size, :] = jnp.zeros((h, count), BF16)
    for i in range(steps):
        for n in other_heads:
            attend_back(i, n)
        if i == 1:
            merge_x(3)
    collect(1)
    for m in range(width // pair):
        grad_qkv(1, m)
        if m == 0:
            cross_x(6).start()
    grad_out()
    merge_x(4)
    cross_x(7).start()
    for i in range(steps):
        for n in own_heads:
            attend_back(i, n)
        if i == 1:
            cross_x(5).start()
        if i == 2:
            merge_x(6)
    merge_x(7)
    collect(0)
    for i in range(steps):
        swap(send_a, recv_a, sa, ra, i, QB).wait_send()

    def make_d_one(i, carry):
        where = rows_of(i * QB, QB)
        total = sum(dot_nt(d_qkv[g][where, :], w_qkv[:, g * pair : (g + 1) * pair]) for g in range(3))
        send_a[where, :] = total.astype(BF16)
        swap(send_a, recv_a, sd, rd, i, QB).start()
        return tuple(carry[g] + column_sum(d_qkv[g][where, :].astype(F32)) for g in range(3))

    d_bias = lax.fori_loop(0, steps, make_d_one, (jnp.zeros((1, pair), F32),) * 3)
    merge_x(5)
    for u in range(2):
        row = pl.ds(6 + (y if u == 0 else 1 - y), 1)
        parts = [d_bias[g][:, u * size : (u + 1) * size] for g in range(3)] + [bias_sum[0:1, u * hidden_t : (u + 1) * hidden_t]]
        spare = vectors.shape[1] - split.shape[1]
        vectors[row, :] = jnp.concatenate(parts + [jnp.zeros((1, spare), F32)] * (spare > 0), 1)

    for m in range(width // pair):
        grad_qkv(0, m)
    for n in range(fold // 2):
        grad_proj(0, n)
    for m in range(width // pair):
        grad_fc(0, m)

    def norm_one_back(i, carry):
        d_gain, d_shift = carry
        where = rows_of(i * LN_ROWS, LN_ROWS)
        d_norm = send_a[where, :].astype(F32) + recv_a[where, :].astype(F32)
        back, hat = norm_back(x[where, :].astype(F32), d_norm, gain1)
        recv_a[where, :] = (second[where, :] + back).astype(BF16)
        return d_gain + column_sum(d_norm * hat), d_shift + column_sum(d_norm)

    for i in range(steps):
        swap(send_a, recv_a, sd, rd, i, QB).wait_recv()
    sums = lax.fori_loop(0, count // LN_ROWS, norm_one_back, (zero,) * 2)
    for k, row in enumerate(sums):
        vectors[k : k + 1, :width] = row

    keep_in = pltpu.make_async_copy(recv_a, in_own, sem_out.at[1])
    keep_in.start()

    here = b * 2 + y
    same_core = [item for item in plane if item[0] % 2 == 0]

    def vec_copy(k, dev, slot):
        return remote(vectors, vec_plane.at[slot], s_v.at[k], r_v.at[slot], dev)

    def vec_copy_z(k, at, slot):
        return remote(vec_out, vec_line.at[slot], s_vz.at[k], r_vz.at[slot], device(at, b, y, c))

    for k, dev, _ in same_core:
        vec_copy(k, dev, here).start()
    vec_plane[here] = vectors[...]

    for k in range(len(groups)):
        merge_y(k)
    if line * PAIR * slots > blocks:
        held0[blocks] = jnp.zeros(held0.shape[1:], BF16)
    for k, group in enumerate(groups):
        cross_y(k).wait_send()
        if group[0] > 0:
            cross_x(k).wait_send()

    pl.semaphore_signal(ready.at[0], inc=1, device_id=x_dev, device_id_type=MESH)

    @pl.when(a < line - 1)
    def _():
        pl.semaphore_signal(ready.at[1], inc=1, device_id=right, device_id_type=MESH)

    @pl.when(a > 0)
    def _():
        pl.semaphore_signal(ready.at[2], inc=1, device_id=left, device_id_type=MESH)

    def dest(k):
        return sum(jnp.where(a == p, hand_on(line, p)[k], 0) for p in range(line))

    def fill(at):
        def one(n, carry):
            spot = at * PAIR * slots + n
            held1[spot] = held0[where_from[spot, 0]]
            return carry

        lax.fori_loop(0, PAIR * slots, one, 0)

    def run(ref, at):
        return ref.at[pl.ds(at * slots, slots)]

    def copy_x(at):
        return remote(span(held1, at, ob, 0, slots), run(from_y, at), sfx.at[at], rfx.at[at], x_dev)

    def copy_z(at, side, dev):
        return remote(span(held1, at, b, 0, slots), run(from_x, at + 1 - side), sfz.at[at], rfz.at[at + 1 - side], dev)

    def add(at, other, spot):
        merge(held1, (at * PAIR + b) * slots, other, spot * slots, slots)

    half = count // 2
    own_half = rows_of(c * half, half)

    def copy_act(k):
        src, dst = ((recv_b, out_other), (recv_a, in_other))[k]
        return remote(src.at[own_half], dst.at[own_half], s_in.at[k], r_in.at[k], y_dev)

    def share_act(k):
        dst = (out_other, in_other)[k]
        return remote(dst.at[own_half], dst.at[own_half], s_sh.at[k], r_sh.at[k], partner)

    def first_step(k):
        at = dest(k)
        fill(at)
        if k == 0:
            pl.semaphore_wait(ready.at[0], 1)
        copy_x(at).start()

    def second_step(k):
        at = dest(k)
        copy_x(at).wait_recv()
        add(at, from_y, at)

    def pass_on(turn):
        down = turn - line + a

        @pl.when((down >= 0) & (down < a))
        def _():
            @pl.when(a < line - 1)
            def _():
                copy_z(down, 1, left).wait_recv()
                add(down, from_x, down)

            copy_z(down, 1, left).start()

        upw = line - turn + a

        @pl.when((upw > a) & (upw < line))
        def _():
            @pl.when(a > 0)
            def _():
                copy_z(upw, 0, right).wait_recv()
                add(upw, from_x, upw + 1)

            copy_z(upw, 0, right).start()

    first_step(0)
    for k in range(2):
        copy_act(k).start()

    @pl.when(a > 0)
    def _():
        pl.semaphore_wait(ready.at[1], 1)

    @pl.when(a < line - 1)
    def _():
        pl.semaphore_wait(ready.at[2], 1)

    for step in range(1, line + 1):
        if step < line:
            first_step(step)
        if step == 1:
            for k, dev, slot in same_core:
                vec_copy(k, dev, slot // 2).wait()
            vec_out[...] = vec_plane[0] + vec_plane[1] + vec_plane[2] + vec_plane[3]
            for k, at in planes:
                vec_copy_z(k, at, a).start()
            vec_line[a] = vec_out[...]
        second_step(step - 1)
        if step < line:
            pass_on(step)

    for k, at in planes:
        vec_copy_z(k, at, at).wait()
    vec_sum = vec_line[0]
    for p in range(1, line):
        vec_sum = vec_sum + vec_line[p]
    vec_out[...] = vec_sum

    @pl.when(a > 0)
    def _():
        copy_z(a, 0, right).wait_recv()

    @pl.when(a < line - 1)
    def _():
        copy_z(a, 1, left).wait_recv()

    def finish(n, carry):
        value = held1[(a * PAIR + b) * slots + n].astype(F32)
        value += jnp.where(a > 0, from_x[(a + 1) * slots + n].astype(F32), 0.0)
        value += jnp.where(a < line - 1, from_x[a * slots + n].astype(F32), 0.0)
        total_out[n] = value
        return carry + jnp.sum((value * value).reshape(-1, 8, LANES), 0)

    square = lax.fori_loop(0, slots, finish, jnp.zeros((8, LANES), F32))
    chips = line * PAIR * 2
    row = lax.broadcasted_iota(jnp.int32, (8, LANES), 0)
    weight = jnp.where(row < 6, 1.0 / (chips * CORES), 1.0 / chips)
    for k in range(vec_sum.shape[1] // LANES):
        tile = vec_sum[:, k * LANES : (k + 1) * LANES]
        square += weight * tile * tile
    square_out[...] = square

    def sq_copy(k, dev, slot):
        return remote(square_out, sq_plane.at[slot], s_q.at[k], r_q.at[slot], dev)

    me = here * 2 + c
    for k, dev, _ in plane:
        sq_copy(k, dev, me).start()
    sq_plane[me] = square

    for k in range(2):
        copy_act(k).wait_recv()
        share_act(k).start()

    for k, dev, slot in plane:
        sq_copy(k, dev, slot).wait()
    square = sq_plane[0]
    for k in range(1, 8):
        square = square + sq_plane[k]
    square_out[...] = square

    def sq_copy_z(k, at, slot):
        return remote(square_out, sq_line.at[slot], s_qz.at[k], r_qz.at[slot], device(at, b, y, c))

    for k, at in planes:
        sq_copy_z(k, at, a).start()
    sq_line[a] = square

    for k in range(2):
        share_act(k).wait()
        copy_act(k).wait_send()
    for m in range(count // MLP_ROWS):
        swap(send_b, recv_b, sb, rb, m, MLP_ROWS).wait_send()
        swap(send_c, recv_c, sc, rc, m, MLP_ROWS).wait_send()
    for i in range(steps):
        swap(send_a, recv_a, sd, rd, i, QB).wait_send()
    keep_out.wait()
    keep_in.wait()

    def gone(at, carry):
        copy_x(at).wait_send()

        @pl.when(at != a)
        def _():
            copy_z(at, 0, right).wait_send()

        return carry

    lax.fori_loop(0, line, gone, 0)
    for k, at in planes:
        sq_copy_z(k, at, at).wait()
    square = sq_line[0]
    for p in range(1, line):
        square = square + sq_line[p]
    square_out[...] = square


def layer(table, tokens, segments, cotangent, master, shared, split, line):
    _, count, width = tokens.shape
    _, slots, size, _ = master.shape
    pair = 2 * size
    total = line * PAIR * slots
    hidden = 2 * (split.shape[1] - 3 * size)
    blocks = table.shape[1]
    steps = count // QB
    halves = count // MLP_ROWS
    spans = sum((i + 1 - max(0, i - 2)) * QB for i in range(steps))
    wide_vec = -(-split.shape[1] // LANES) * LANES
    direct = width // size
    x_blocks = (blocks - direct) // 2
    y_blocks = direct + x_blocks
    vm = lambda shape, kind=BF16: pltpu.VMEM(shape, kind)
    dma = lambda *n: pltpu.SemaphoreType.DMA(n)
    anywhere = pl.BlockSpec(memory_space=pl.ANY)
    inside = pl.BlockSpec(memory_space=pltpu.VMEM)
    scalars = pl.BlockSpec(memory_space=pltpu.SMEM)
    act = (count, width)
    block = (packed_rows(size), LANES)
    vec = (8, wide_vec)
    S = jax.ShapeDtypeStruct
    return pl.pallas_call(
        functools.partial(layer_kernel, (size, width, count, line, slots)),
        out_shape=(S((slots,) + block, F32), S(vec, F32), S((8, LANES), F32)) + (S(act, BF16),) * 4,
        in_specs=[scalars, anywhere, anywhere, inside, anywhere, anywhere, inside, inside, anywhere, inside],
        out_specs=(inside, inside, inside) + (anywhere,) * 4,
        scratch_shapes=[
            vm(act),
            vm(act),
            vm((slots, size, size), F32),
            vm((total,) + block),
            vm((total,) + block),
            vm((max(x_blocks, (line + 1) * slots),) + block),
            vm((max(y_blocks, line * slots),) + block),
            pltpu.SMEM((1, blocks), jnp.int32),
            vm(split.shape, F32),
            vm((total, LANES), jnp.int32),
            pltpu.SMEM((total, LANES), jnp.int32),
            vm((width, 3 * pair)),
            vm((pair, width)),
            vm((width, hidden)),
            vm((hidden, width)),
            vm((spans, QB), F32),
            vm(act),
            vm((count, pair)),
            vm((count, pair)),
            vm((count, pair)),
            vm((pair, count)),
            vm((pair, count)),
            vm((pair, count)),
            vm((8, count), F32),
            vm(act),
            vm(act),
            vm(act),
            vm(act),
            vm(act),
            vm(act),
            vm(act, F32),
            vm(act),
            vm((count, hidden)),
            vm((count, hidden)),
            vm((count, pair), F32),
            vm((count, pair), F32),
            vm((pair, count)),
            vm((8, 3 * pair), F32),
            vm((16, hidden), F32),
            vm(vec, F32),
            vm((4,) + vec, F32),
            vm((line,) + vec, F32),
            vm((8, 8, LANES), F32),
            vm((line, 8, LANES), F32),
            dma(4),
            dma(2),
        ]
        + [dma(line)] * 11
        + [dma(1), dma(1)]
        + [dma(2, line)] * 3
        + [dma(2), dma(2)]
        + [dma(steps), dma(steps), dma(halves), dma(halves), dma(halves), dma(halves), dma(steps), dma(steps)]
        + [dma(8)] * 4
        + [pltpu.SemaphoreType.REGULAR((3,)), dma(line), dma(line), dma(line), dma(line + 1)]
        + [dma(8), dma(4), dma(line), dma(line), dma(8), dma(8), dma(line), dma(line), dma(2), dma(2), dma(2), dma(2)],
        compiler_params=pltpu.CompilerParams(collective_id=2, has_side_effects=True, vmem_limit_bytes=63 * MIB),
        name="layer",
    )(table, table, tokens, segments, cotangent, master, shared, split, split, table)


def halves_of(value):
    high = value.astype(BF16)
    return high, (value - high.astype(F32)).astype(BF16)


def fine_dot(a, b):
    a_high, a_low = halves_of(a)
    b_high, b_low = halves_of(b)
    return dot(a_high, b_high) + (dot(a_high, b_low) + dot(a_low, b_high))


def update_kernel(
    grad,
    square,
    vec,
    master,
    stats,
    roots,
    shared,
    shared_state,
    split,
    split_state,
    out_mine,
    out_theirs,
    in_mine,
    in_theirs,
    norm_out,
    clipped_out,
    master_out,
    copy_out,
    stats_out,
    shared_grad,
    shared_new_state,
    shared_new,
    split_grad,
    split_new_state,
    split_new,
    output,
    input_grad,
    acts,
    wide,
    grad_v,
    master_v,
    stats_v,
    roots_v,
    clipped_v,
    copy_v,
    sem_act,
    sem_wide,
    sem_in,
    sem_out,
):
    slots, size = master.shape[1], master.shape[2]
    y = lax.axis_index("tensor") // CORES
    _, count, _ = acts.shape
    chunk = count // 4
    fetch = []
    for k, ref in enumerate((out_mine, out_theirs, in_mine, in_theirs)):
        fetch.append(pltpu.make_async_copy(ref, acts.at[k], sem_act.at[k]))

    def slot_loads(n):
        return [
            pltpu.make_async_copy(src.at[n], dst.at[n], sem_in.at[k, n])
            for k, (src, dst) in enumerate(
                ((grad, grad_v), (roots.at[0], roots_v), (stats.at[0], stats_v), (master.at[0], master_v))
            )
        ]

    for n in range(slots):
        for copy in slot_loads(n):
            copy.start()
    for copy in fetch:
        copy.start()

    def wide_copy(k, n):
        target = (output, output, input_grad, input_grad)[k]
        seq = y if k % 2 == 0 else 1 - y
        rows = rows_of(n * chunk, chunk)
        return pltpu.make_async_copy(wide.at[k, rows], target.at[seq, rows], sem_wide.at[k, n])

    def widen(k):
        fetch[k].wait()

        def one(n, carry):
            rows = rows_of(n * chunk, chunk)
            wide[k, rows, :] = acts[k, rows, :].astype(F32)
            wide_copy(k, n).start()
            return carry

        lax.fori_loop(0, 4, one, 0)

    norm = jnp.sqrt(jnp.sum(square[...], keepdims=True))
    factor = 1.0 / jnp.maximum(norm, 1.0)
    norm_out[...] = norm
    def slot_copies(n):
        return [
            pltpu.make_async_copy(src.at[n], dst.at[0, n], sem_out.at[k, n])
            for k, (src, dst) in enumerate(
                ((clipped_v, clipped_out), (master_v, master_out), (copy_v, copy_out), (stats_v, stats_out))
            )
        ]

    def slot(n, carry):
        for copy in slot_loads(n):
            copy.wait()
        clipped = jnp.concatenate(unpack_block(grad_v[n] * factor, size), 1)
        clipped_v[n] = clipped
        low = clipped.astype(BF16)
        stats_v[n, 0] = DECAY * stats_v[n, 0] + (1.0 - DECAY) * dot_nt(low, low)
        stats_v[n, 1] = DECAY * stats_v[n, 1] + (1.0 - DECAY) * dot_tn(low, low)
        step = fine_dot(fine_dot(roots_v[n, 0], clipped), roots_v[n, 1])
        new = master_v[n] - RATE * step
        master_v[n] = new
        copy_v[n] = new.astype(BF16)
        for copy in slot_copies(n):
            copy.start()
        return carry

    early = slots // 2
    lax.fori_loop(0, early, slot, 0, unroll=True)
    widen(0)
    widen(1)
    lax.fori_loop(early, slots, slot, 0, unroll=True)
    for k in range(2, 4):
        widen(k)
    for raw, value, state, g_out, s_out, v_out in (
        (vec[0 : shared.shape[0], : shared.shape[1]], shared, shared_state, shared_grad, shared_new_state, shared_new),
        (vec[pl.ds(6 + y, 1), :][:, : split.shape[1]], split, split_state, split_grad, split_new_state, split_new),
    ):
        g = raw * factor
        moment = DECAY * state[...] + (1.0 - DECAY) * g * g
        g_out[...] = g
        s_out[...] = moment
        v_out[...] = value[...] - RATE_VECTOR * g * lax.rsqrt(moment)

    def done(n, carry):
        for copy in slot_copies(n):
            copy.wait()
        return carry

    lax.fori_loop(0, slots, done, 0)
    for k in range(4):
        for n in range(4):
            wide_copy(k, n).wait()


def update(grad, square, vec, master, stats, roots, shared, shared_state, split, split_state, acts):
    _, slots, size, _ = master.shape
    count, width = acts[0].shape
    anywhere = pl.BlockSpec(memory_space=pl.ANY)
    inside = pl.BlockSpec(memory_space=pltpu.VMEM)
    S = jax.ShapeDtypeStruct
    vm = lambda shape, kind=F32: pltpu.VMEM(shape, kind)
    dma = lambda *n: pltpu.SemaphoreType.DMA(n)
    return pl.pallas_call(
        update_kernel,
        out_shape=(S((1, 1), F32), S(master.shape, F32), S(master.shape, F32), S(master.shape, BF16), S(stats.shape, F32))
        + (S(shared.shape, F32),) * 3
        + (S(split.shape, F32),) * 3
        + (S((2, count, width), F32),) * 2,
        in_specs=[anywhere, inside, inside] + [anywhere] * 3 + [inside] * 4 + [anywhere] * 4,
        out_specs=(inside,) + (anywhere,) * 4 + (inside,) * 6 + (anywhere,) * 2,
        scratch_shapes=[
            vm((4, count, width), BF16),
            vm((4, count, width)),
            vm(grad.shape),
            vm((slots, size, size)),
            vm((slots, 2, size, size)),
            vm((slots, 2, size, size)),
            vm((slots, size, size)),
            vm((slots, size, size), BF16),
            dma(4),
            dma(4, 4),
            dma(4, slots),
            dma(4, slots),
        ],
        compiler_params=pltpu.CompilerParams(vmem_limit_bytes=63 * MIB),
        name="update",
    )(grad, square, vec, master, stats, roots, shared, shared_state, split, split_state, *acts)


def body(
    tokens,
    segments,
    cotangent,
    block_owner_slots,
    master_weights,
    statistics,
    inverse_roots,
    shared_vectors,
    shared_state,
    split_bias,
    split_state,
):
    line = lax.axis_size("dp") // PAIR
    grad, vec, square, out, out_other, d_in, d_in_other = layer(
        block_owner_slots, tokens, segments, cotangent, master_weights, shared_vectors, split_bias, line
    )
    done = update(
        grad,
        square,
        vec,
        master_weights,
        statistics,
        inverse_roots,
        shared_vectors,
        shared_state,
        split_bias,
        split_state,
        (out, out_other, d_in, d_in_other),
    )
    return (done[11], done[12], done[0].reshape(())) + tuple(done[1:11])


def solution(mesh):
    placed = (
        P("dp", None, None),
        P("dp", None),
        P("dp", None, None),
        P("tensor", None),
        P("tensor", "dp", None, None),
        P("tensor", "dp", None, None, None),
        P("tensor", "dp", None, None, None),
        P(),
        P(),
        P("tensor", None),
        P("tensor", None),
    )
    return jax.shard_map(
        body,
        mesh=mesh,
        in_specs=placed,
        out_specs=(
            P("dp", None, None),
            P("dp", None, None),
            P(),
            P("tensor", "dp", None, None),
            P("tensor", "dp", None, None),
            P("tensor", "dp", None, None),
            P("tensor", "dp", None, None, None),
            P(),
            P(),
            P(),
            P("tensor", None),
            P("tensor", None),
            P("tensor", None),
        ),
        check_vma=False,
    )
```

```python
import functools
import math

import jax
import jax.numpy as jnp
from jax import lax
from jax.sharding import PartitionSpec as P
import jax.experimental.pallas as pl
import jax.experimental.pallas.tpu as pltpu

MESH = pl.DeviceIdType.MESH
PAIR = 2
CORES = 2
LANES = 128
MIB = 2**20
HEAD = 64
EPS = 1e-05
NEG = -1000000000.0
TOP = 3.0e38
QB = 256
MLP_ROWS = 512
LN_ROWS = 256
DECAY = 0.5
RATE = 0.3
RATE_VECTOR = 0.2
F32 = jnp.float32
BF16 = jnp.bfloat16


def packed_rows(size):
    return size * size // LANES


def pack_block(block):
    half = block.shape[0] // 2
    return block[:, :LANES], jnp.concatenate([block[:half, LANES:], block[half:, LANES:]], 1)


def unpack_block(packed, size):
    tail = packed[size:]
    h = LANES // 2
    return packed[:size], jnp.concatenate([tail[:, :h], tail[:, h:]], 0)


def place():
    d = lax.axis_index("dp")
    t = lax.axis_index("tensor")
    return d // PAIR, lax.rem(d, PAIR), t // CORES, lax.rem(t, CORES)


def device(a, b, y, c):
    return (a * PAIR + b, y * CORES + c)


def remote(src, dst, s, r, dev):
    return pltpu.make_async_remote_copy(src_ref=src, dst_ref=dst, send_sem=s, recv_sem=r, device_id=dev, device_id_type=MESH)


def dot(a, b):
    return lax.dot_general(a, b, (((1,), (0,)), ((), ())), preferred_element_type=F32)


def dot_nt(a, b):
    return lax.dot_general(a, b, (((1,), (1,)), ((), ())), preferred_element_type=F32)


def dot_tn(a, b):
    return lax.dot_general(a, b, (((0,), (0,)), ((), ())), preferred_element_type=F32)


def centre_of(value):
    mean = jnp.mean(value, -1, keepdims=True)
    centred = value - mean
    spread = jnp.mean(centred * centred, -1, keepdims=True)
    return centred, lax.rsqrt(spread + EPS)


def norm_back(value, d_out, gain):
    centred, scale = centre_of(value)
    hat = centred * scale
    d_hat = d_out * gain
    back = scale * (d_hat - jnp.mean(d_hat, -1, keepdims=True) - hat * jnp.mean(d_hat * hat, -1, keepdims=True))
    return back, hat


def rows_of(start, count):
    return pl.ds(pl.multiple_of(start, count), count)


def column_sum(value):
    return jnp.sum(value, 0, keepdims=True)


def hand_on(line, at):
    turn = lambda dest: dest + line - at if dest < at else line - dest + at
    return sorted(range(line), key=lambda dest: line if dest == at else turn(dest))


def layer_kernel(
    dims,
    table,
    table_src,
    tokens,
    segments,
    cotangent,
    master,
    shared,
    split,
    split_src,
    table_row,
    total_out,
    vec_out,
    square_out,
    out_own,
    out_other,
    in_own,
    in_other,
    x,
    dy,
    owned,
    held0,
    held1,
    from_x,
    from_y,
    other_table,
    other_split,
    inverse,
    where_from,
    w_qkv,
    w_out,
    w_fc,
    w_proj,
    cap,
    h_one,
    q_s,
    k_s,
    v_s,
    k_t,
    v_t,
    mixed_t,
    logsum,
    send_a,
    recv_a,
    send_b,
    recv_b,
    send_c,
    recv_c,
    second,
    h_two,
    gelu_s,
    d_hid,
    d_keys,
    d_vals,
    d_query_t,
    bias_qkv,
    bias_fc,
    vectors,
    vec_plane,
    vec_line,
    sq_plane,
    sq_line,
    sem_in,
    sem_out,
    s_zr,
    s_zl,
    r_z,
    s_x,
    r_x,
    s_y,
    r_y,
    s_xy,
    r_xy,
    s_yx,
    r_yx,
    s_g,
    r_g,
    s_zgr,
    s_zgl,
    r_zg,
    s_t,
    r_t,
    sa,
    ra,
    sb,
    rb,
    sc,
    rc,
    sd,
    rd,
    smx,
    rmx,
    smy,
    rmy,
    ready,
    sfx,
    rfx,
    sfz,
    rfz,
    s_v,
    r_v,
    s_vz,
    r_vz,
    s_q,
    r_q,
    s_qz,
    r_qz,
    s_in,
    r_in,
    s_sh,
    r_sh,
):
    size, width, count, line, slots = dims
    a, b, y, c = place()
    ob = 1 - b
    partner = device(a, b, y, 1 - c)
    x_dev, y_dev = device(a, ob, y, c), device(a, b, 1 - y, c)
    right = device(jnp.minimum(a + 1, line - 1), b, y, c)
    left = device(jnp.maximum(a - 1, 0), b, y, c)
    plane = []
    for k in range(1, 8):
        fb, fy, fc = lax.rem(b + k // 4, 2), lax.rem(y + k // 2 % 2, 2), lax.rem(c + k % 2, 2)
        plane.append((k, device(a, fb, fy, fc), fb * 4 + fy * 2 + fc))
    planes = [(k, lax.rem(a + k, line)) for k in range(1, line)]
    barrier = pltpu.get_barrier_semaphore()
    for _, dev, _ in plane:
        pl.semaphore_signal(barrier, inc=1, device_id=dev, device_id_type=MESH)
    for _, at in planes:
        pl.semaphore_signal(barrier, inc=1, device_id=device(at, b, y, c), device_id_type=MESH)

    grid = width // size
    hidden_t = split.shape[1] - 3 * size
    fold = hidden_t // size
    pair = 2 * size
    cut_a, cut_b = 3 * grid, 4 * grid
    cut_c = cut_b + grid * fold
    blocks = cut_c + grid * fold
    heads = pair // HEAD
    hidden = 2 * hidden_t
    steps = count // QB
    h = LANES // 2

    load_m = pltpu.make_async_copy(master.at[0], owned, sem_in.at[0])
    load_m.start()
    load_x = pltpu.make_async_copy(tokens.at[y], x, sem_in.at[1])
    load_x.start()
    load_dy = pltpu.make_async_copy(cotangent.at[y], dy, sem_in.at[2])
    load_dy.start()

    last = slots // 3
    most = slots - last

    def span(ref, at, bb, first, number):
        return ref.at[pl.ds((at * PAIR + bb) * slots + first, number)]

    def z_copy(at, s, dev):
        return remote(span(held0, at, b, 0, slots), span(held0, at, b, 0, slots), s.at[at], r_z.at[at], dev)

    def x_copy(at):
        return remote(span(held0, at, b, 0, slots), span(held0, at, b, 0, slots), s_x.at[at], r_x.at[at], x_dev)

    def y_copy(at, number):
        return remote(span(held0, at, b, 0, number), span(held1, at, b, 0, number), s_y.at[at], r_y.at[at], y_dev)

    def y_share(at):
        return most - (1 + at % 2 if last else most // 2)

    def yx_copy(at):
        n = y_share(at)
        return remote(span(held0, at, ob, 0, n), span(held1, at, ob, 0, n), s_yx.at[at], r_yx.at[at], y_dev)

    def xy_copy(at):
        n = y_share(at)
        return remote(span(held1, at, b, n, most - n), span(held1, at, b, n, most - n), s_xy.at[at], r_xy.at[at], x_dev)

    def corner_copy():
        return remote(span(held0, a, ob, most, last), span(held1, a, ob, most, last), s_g.at[0], r_g.at[0], y_dev)

    def zg_copy(at, k, s, dev):
        where = span(held1, at, (b, ob)[k], most, last)
        return remote(where, where, s.at[k, at], r_zg.at[k, at], dev)

    load_m.wait()
    mine = (a * PAIR + b) * slots

    def pack(s, carry):
        left_part, right_part = pack_block(owned[s].astype(BF16))
        held0[mine + s, :size] = left_part
        held0[mine + s, size:] = right_part
        return carry

    lax.fori_loop(0, slots, pack, 0)
    pl.semaphore_wait(barrier, 7 + line - 1)

    @pl.when(a < line - 1)
    def _():
        z_copy(a, s_zr, right).start()

    @pl.when(a > 0)
    def _():
        z_copy(a, s_zl, left).start()

    small = [
        remote(table_src, other_table, s_t.at[0], r_t.at[0], y_dev),
        remote(split_src, other_split, s_t.at[1], r_t.at[1], y_dev),
    ]
    for copy in small:
        copy.start()
    x_copy(a).start()
    y_copy(a, slots).start()

    vectors[...] = jnp.zeros_like(vectors)
    gain1, shift1 = shared[0:1, :], shared[1:2, :]
    gain2, shift2 = shared[2:3, :], shared[3:4, :]
    out_bias, proj_bias = shared[4:5, :], shared[5:6, :]
    load_x.wait()

    def norm_one(i, carry):
        where = rows_of(i * LN_ROWS, LN_ROWS)
        centred, scale = centre_of(x[where, :].astype(F32))
        h_one[where, :] = (centred * scale * gain1 + shift1).astype(BF16)
        return carry

    lax.fori_loop(0, count // LN_ROWS, norm_one, 0)

    def arrivals(j):
        for ok, at, s, dev, more in (
            (a - j >= 0, a - j, s_zr, right, a < line - 1),
            (a + j < line, a + j, s_zl, left, a > 0),
        ):

            @pl.when(ok)
            def _():
                z_copy(at, s, dev).wait_recv()

                @pl.when(more)
                def _():
                    z_copy(at, s, dev).start()

                x_copy(at).start()
                y_copy(at, most).start()

    arrivals(1)
    seg_row = segments[pl.ds(y, 1), :].astype(F32)
    seg_col = d_keys.at[:, :LANES]
    seg_col[...] = jnp.transpose(jnp.broadcast_to(seg_row, (LANES, count)))
    reach = []
    at = 0
    for i in range(steps):
        first = max(0, i - 2) * QB
        wide = (i + 1) * QB - first
        reach.append((first, wide, at))
        key_seg = seg_col[first : first + wide, :]
        key_seg = jnp.concatenate([key_seg] * (QB // LANES), 1)
        key_at = lax.broadcasted_iota(jnp.int32, (wide, QB), 0) + first
        query_at = lax.broadcasted_iota(jnp.int32, (wide, QB), 1) + i * QB
        allowed = (key_seg == seg_row[:, i * QB : (i + 1) * QB]) & (key_at <= query_at)
        cap[at : at + wide, :] = jnp.where(allowed, TOP, NEG)
        at += wide
    x_copy(a).wait_recv()
    if last:
        corner_copy().start()
    d_vals[...] = jnp.zeros_like(d_vals)
    d_keys[...] = jnp.zeros_like(d_keys)
    d_query_t[size - h : size, :] = jnp.zeros((h, count), BF16)
    for j in range(2, line):
        arrivals(j)
    spots = line * PAIR * slots
    hit = lax.broadcasted_iota(jnp.int32, (spots, blocks), 0) == table_row[0:1, :]
    number = lax.broadcasted_iota(jnp.int32, (spots, blocks), 1)
    found = jnp.sum(jnp.where(hit, number - blocks, 0), 1, keepdims=True) + blocks
    inverse[...] = jnp.broadcast_to(jnp.clip(found, 0, spots - 1), inverse.shape)
    load_inverse = pltpu.make_async_copy(inverse, where_from, sem_in.at[3])
    load_inverse.start()
    for copy in small:
        copy.wait()
    biases = (split, other_split)
    bias_qkv[0:1, :] = jnp.concatenate([biases[u][0:1, g * size : (g + 1) * size] for g in range(3) for u in range(2)], 1)
    bias_fc[0:1, :] = jnp.concatenate([biases[u][0:1, 3 * size :] for u in range(2)], 1)

    y_copy(a, slots).wait_recv()

    def line_arrivals(j):
        for ok, at, s, dev, more in (
            (a - j >= 0, a - j, s_zgr, right, a < line - 1),
            (a + j < line, a + j, s_zgl, left, a > 0),
        ):

            @pl.when(ok)
            def _():
                for k in range(2):
                    zg_copy(at, k, s, dev).wait_recv()

                if j < line - 1:

                    @pl.when(more)
                    def _():
                        for k in range(2):
                            zg_copy(at, k, s, dev).start()

    if last:
        corner_copy().wait_recv()

        @pl.when(a < line - 1)
        def _():
            for k in range(2):
                zg_copy(a, k, s_zgr, right).start()

        @pl.when(a > 0)
        def _():
            for k in range(2):
                zg_copy(a, k, s_zgl, left).start()

        line_arrivals(1)

    for at in range(line):

        @pl.when(at != a)
        def _():
            x_copy(at).wait_recv()
            y_copy(at, most).wait_recv()

        yx_copy(at).start()
        xy_copy(at).start()
    if last:
        for j in range(2, line - 1):
            line_arrivals(j)
    def block_at(u, block):
        ref, lookup = ((held0, table), (held1, other_table))[u]
        return unpack_block(ref[lookup[0, block]], size)

    def put_pair(ref, row, col, first, other):
        left0, right0 = first
        left1, right1 = other
        where = rows_of(row * size, size)
        ref[where, col : col + LANES] = left0
        ref[where, col + LANES : col + 2 * LANES] = jnp.concatenate([right0, left1[:, :h]], 1)
        ref[where, col + 2 * LANES : col + 3 * LANES] = jnp.concatenate([left1[:, h:], right1], 1)

    def build_attention(u):
        def one(r, carry):
            where = rows_of(r * size, size)
            for g in range(3):
                left_part, right_part = block_at(u, r * 3 + g)
                col = g * pair
                if u == 0:
                    w_qkv[where, col : col + LANES] = left_part
                    w_qkv[where, col + LANES : col + LANES + h] = right_part
                else:
                    tile = w_qkv[where, col + LANES : col + 2 * LANES]
                    w_qkv[where, col + LANES : col + 2 * LANES] = jnp.concatenate([tile[:, :h], left_part[:, :h]], 1)
                    w_qkv[where, col + 2 * LANES : col + 3 * LANES] = jnp.concatenate([left_part[:, h:], right_part], 1)
            return carry

        lax.fori_loop(0, grid, one, 0)

    def build_rest(u):
        for j in range(0, grid, 2):
            put_pair(w_out, u, j * size, block_at(u, cut_a + j), block_at(u, cut_a + j + 1))

        def fc(r, carry):
            for f in range(0, fold, 2):
                block = cut_b + r * fold + f
                put_pair(w_fc, r, u * hidden_t + f * size, block_at(u, block), block_at(u, block + 1))
            return carry

        lax.fori_loop(0, grid, fc, 0)

        def proj(f, carry):
            for r in range(0, grid, 2):
                block = cut_c + f * grid + r
                put_pair(w_proj, u * fold + f, r * size, block_at(u, block), block_at(u, block + 1))
            return carry

        lax.fori_loop(0, fold, proj, 0)

    def make_qkv(u):
        low, high = ((0, size), (LANES, pair))[u]

        def one(i, carry):
            where = rows_of(i * QB, QB)
            for g in range(3):
                cols = slice(g * pair + low, g * pair + high)
                got = dot(h_one[where, :], w_qkv[:, cols]) + bias_qkv[0:1, cols]
                if g == 0:
                    q_s[where, low:high] = (got.astype(BF16).astype(F32) * HEAD ** (-0.5)).astype(BF16)
                else:
                    row, col = ((k_s, k_t), (v_s, v_t))[g - 1]
                    row[where, low:high] = got.astype(BF16)
                    if u == 0:
                        row[where, high : high + h] = jnp.zeros((QB, h), BF16)
                    col[low:high, where] = jnp.transpose(got).astype(BF16)
            return carry

        lax.fori_loop(0, steps, one, 0)

    def head_of(value, n):
        lane = lax.broadcasted_iota(jnp.int32, value.shape, 1)
        return jnp.where((lane < HEAD) if n % 2 == 0 else (lane >= HEAD), value, jnp.zeros_like(value))

    def tile_of(n):
        return slice(n // 2 * LANES, (n // 2 + 1) * LANES)

    def attend(i, n):
        first, wide, at = reach[i]
        query_rows = slice(i * QB, (i + 1) * QB)
        keys = k_s[first : first + wide, tile_of(n)]
        query = head_of(q_s[query_rows, tile_of(n)], n)
        scores = jnp.minimum(dot_nt(keys, query), cap[at : at + wide, :])
        top = jnp.max(scores, 0, keepdims=True)
        expo = jnp.exp(scores - top)
        total = jnp.sum(expo, 0, keepdims=True)
        got = dot(v_t[n * HEAD : (n + 1) * HEAD, first : first + wide], expo.astype(BF16))
        mixed_t[n * HEAD : (n + 1) * HEAD, query_rows] = (got * (1.0 / total)).astype(BF16)
        logsum[n : n + 1, query_rows] = top + jnp.log(total)

    own_heads, other_heads = range(heads // 2), range(heads // 2, heads)
    build_attention(0)
    make_qkv(0)
    for i in range(steps):
        for n in own_heads:
            attend(i, n)
    build_rest(0)

    for at in range(line):
        yx_copy(at).wait_recv()
        xy_copy(at).wait_recv()
    if last and line > 2:
        line_arrivals(line - 1)
    build_attention(1)
    make_qkv(1)
    build_rest(1)

    def swap(send, recv, s, r, at, rows):
        where = pl.ds(at * rows, rows) if isinstance(at, int) else rows_of(at * rows, rows)
        return remote(send.at[where], recv.at[where], s.at[at], r.at[at], partner)

    for i in range(steps):
        for n in other_heads:
            attend(i, n)
        query_rows = slice(i * QB, (i + 1) * QB)
        send_a[query_rows, :] = dot_tn(mixed_t[:, query_rows], w_out[...]).astype(BF16)
        swap(send_a, recv_a, sa, ra, i, QB).start()

    load_dy.wait()
    load_inverse.wait()

    strips = hidden // pair
    curve = math.sqrt(2.0 / math.pi)
    bias_sum = bias_fc.at[8:16]
    bias_sum[...] = jnp.zeros(bias_sum.shape, F32)

    def mlp(m, carry):
        for i in range(MLP_ROWS // QB):
            swap(send_a, recv_a, sa, ra, m * (MLP_ROWS // QB) + i, QB).wait_recv()

        def norm_two(i, inner):
            where = rows_of(m * MLP_ROWS + i * LN_ROWS, LN_ROWS)
            total = send_a[where, :].astype(F32) + recv_a[where, :].astype(F32)
            value = x[where, :].astype(F32) + total + out_bias
            second[where, :] = value
            centred, scale = centre_of(value)
            h_two[where, :] = (centred * scale * gain2 + shift2).astype(BF16)
            return inner

        lax.fori_loop(0, MLP_ROWS // LN_ROWS, norm_two, 0)
        where = rows_of(m * MLP_ROWS, MLP_ROWS)

        def strip(n, inner):
            cols = pl.ds(pl.multiple_of(n * pair, LANES), pair)
            hid = dot(h_two[where, :], w_fc[:, cols]) + bias_fc[0:1, cols]
            square = hid * hid
            bend = jnp.tanh(curve * hid * (1.0 + 0.044715 * square))
            up = 0.5 * (1.0 + bend)
            gelu_s[where, cols] = (hid * up).astype(BF16)
            slope = up + 0.5 * hid * (1.0 - bend * bend) * (curve * (1.0 + 3 * 0.044715 * square))
            d_hid[where, cols] = slope.astype(BF16)
            return inner

        lax.fori_loop(0, strips, strip, 0, unroll=True)
        send_b[where, :] = dot(gelu_s[where, :], w_proj[...]).astype(BF16)
        swap(send_b, recv_b, sb, rb, m, MLP_ROWS).start()
        return carry

    lax.fori_loop(0, count // MLP_ROWS, mlp, 0)

    def mlp_back(m, carry):
        where = rows_of(m * MLP_ROWS, MLP_ROWS)

        def strip(n, inner):
            cols = pl.ds(pl.multiple_of(n * pair, LANES), pair)
            back = (dot_nt(dy[where, :], w_proj[cols, :]) * d_hid[where, cols].astype(F32)).astype(BF16)
            d_hid[where, cols] = back
            bias_sum[0:1, cols] += column_sum(back.astype(F32))
            return inner

        lax.fori_loop(0, strips, strip, 0, unroll=True)
        send_c[where, :] = dot_nt(d_hid[where, :], w_fc[...]).astype(BF16)
        swap(send_c, recv_c, sc, rc, m, MLP_ROWS).start()
        return carry

    for at in range(line):
        x_copy(at).wait_send()
        yx_copy(at).wait_send()
        xy_copy(at).wait_send()

        @pl.when(at == a)
        def _():
            y_copy(at, slots).wait_send()

        @pl.when(at != a)
        def _():
            y_copy(at, most).wait_send()

        @pl.when((at <= a) & (a < line - 1))
        def _():
            z_copy(at, s_zr, right).wait_send()
            for k in range(2 if last else 0):
                zg_copy(at, k, s_zgr, right).wait_send()

        @pl.when((at >= a) & (a > 0))
        def _():
            z_copy(at, s_zl, left).wait_send()
            for k in range(2 if last else 0):
                zg_copy(at, k, s_zgl, left).wait_send()

    if last:
        corner_copy().wait_send()

    held = (held0, held1)

    def keep(ref, block, left_part, right_part):
        half = size // 2
        ref[block, :size, :] = left_part
        ref[block, size:, :] = jnp.concatenate([right_part[:half], right_part[half:]], 1)

    def keep_pair(u, tile, block):
        t0, t1, t2 = (tile[:, k * LANES : (k + 1) * LANES] for k in range(3))
        keep(held[u], block, t0, t1[:, :h])
        keep(held[u], block + 1, jnp.concatenate([t1[:, h:], t2[:, :h]], 1), t2[:, h:])

    def grad_proj(u, n):
        got = dot_tn(gelu_s[:, u * hidden_t + n * pair : u * hidden_t + (n + 1) * pair], dy[...]).astype(BF16)
        for s in range(2):
            for r in range(0, grid, 2):
                keep_pair(u, got[s * size : (s + 1) * size, r * size : (r + 2) * size], cut_c + (2 * n + s) * grid + r)

    def grad_fc(u, m):
        got = dot_tn(h_two[:, m * pair : (m + 1) * pair], d_hid[:, u * hidden_t : (u + 1) * hidden_t]).astype(BF16)
        for s in range(2):
            for f in range(0, fold, 2):
                keep_pair(u, got[s * size : (s + 1) * size, f * size : (f + 2) * size], cut_b + (2 * m + s) * fold + f)

    strip_blocks = 2 * grid
    few = strip_blocks // 2
    groups = []
    at_x = at_y = 0
    for first, number, kind in (
        (cut_c, few, 0),
        (cut_c + few, strip_blocks - few, 1),
        (cut_c + strip_blocks, strip_blocks, 1),
        (cut_b, 2 * fold, 1),
        (cut_b + 2 * fold, 2 * fold, 1),
        (cut_a, grid, 1),
        (0, 6, 1),
        (6, 6, 1),
    ):
        moved = number >> kind
        groups.append((kind, first, moved, at_x, at_y))
        at_x += moved * kind
        at_y += moved

    def cross_x(k):
        _, first, moved, at, _ = groups[k]
        return remote(held1.at[pl.ds(first + ob * moved, moved)], from_x.at[pl.ds(at, moved)], smx.at[k], rmx.at[k], x_dev)

    def kept(k):
        kind, first, moved, _, _ = groups[k]
        return first + b * moved * kind

    def cross_y(k):
        _, _, moved, _, at = groups[k]
        return remote(held1.at[pl.ds(kept(k), moved)], from_y.at[pl.ds(at, moved)], smy.at[k], rmy.at[k], y_dev)

    def merge(ref, start, other, at, number):
        def one(n, carry):
            ref[start + n] = (ref[start + n].astype(F32) + other[at + n].astype(F32)).astype(BF16)
            return carry

        lax.fori_loop(0, number, one, 0)

    def merge_x(k):
        _, _, moved, at, _ = groups[k]
        cross_x(k).wait_recv()
        merge(held1, kept(k), from_x, at, moved)
        cross_y(k).start()

    def merge_y(k):
        _, _, moved, _, at = groups[k]
        cross_y(k).wait_recv()
        merge(held0, kept(k), from_y, at, moved)

    for n in range(fold // 2):
        grad_proj(1, n)
        if n == 0:
            cross_y(0).start()
            cross_x(1).start()
        else:
            cross_x(2).start()
    lax.fori_loop(0, count // MLP_ROWS, mlp_back, 0)
    grad_fc(1, 0)
    cross_x(3).start()
    merge_x(1)
    grad_fc(1, 1)

    for m in range(count // MLP_ROWS):
        swap(send_b, recv_b, sb, rb, m, MLP_ROWS).wait_recv()
        swap(send_c, recv_c, sc, rc, m, MLP_ROWS).wait_recv()

    def norm_two_back(i, carry):
        d_gain, d_shift, d_bias, d_proj = carry
        where = rows_of(i * LN_ROWS, LN_ROWS)
        value = second[where, :]
        total = send_b[where, :].astype(F32) + recv_b[where, :].astype(F32)
        recv_b[where, :] = (value + total + proj_bias).astype(BF16)
        d_norm = send_c[where, :].astype(F32) + recv_c[where, :].astype(F32)
        d_out = dy[where, :].astype(F32)
        back, hat = norm_back(value, d_norm, gain2)
        d_second = d_out + back
        second[where, :] = d_second
        low = d_second.astype(BF16)
        recv_c[where, :] = low
        return (
            d_gain + column_sum(d_norm * hat),
            d_shift + column_sum(d_norm),
            d_bias + column_sum(low.astype(F32)),
            d_proj + column_sum(d_out),
        )

    zero = jnp.zeros((1, width), F32)
    sums = lax.fori_loop(0, count // LN_ROWS, norm_two_back, (zero,) * 4)
    for k, row in enumerate(sums):
        vectors[2 + k : 3 + k, :width] = row
    d_low = recv_c
    keep_out = pltpu.make_async_copy(recv_b, out_own, sem_out.at[0])
    keep_out.start()
    merge_x(2)

    d_mixed = gelu_s.at[:, hidden_t : hidden_t + pair]
    d_qkv = (
        gelu_s.at[:, hidden_t + pair : hidden_t + 2 * pair],
        d_hid.at[:, hidden_t : hidden_t + pair],
        d_hid.at[:, hidden_t + pair : hidden_t + 2 * pair],
    )

    def make_d_mixed(i, carry):
        where = rows_of(i * QB, QB)
        d_mixed[where, :] = dot_nt(d_low[where, :], w_out[...]).astype(BF16)
        return carry

    lax.fori_loop(0, steps, make_d_mixed, 0)
    cross_x(4).start()
    def grad_out():
        got = dot(mixed_t[...], d_low[...]).astype(BF16)
        for u in range(2):
            for r in range(0, grid, 2):
                keep_pair(u, got[u * size : (u + 1) * size, r * size : (r + 2) * size], cut_a + r)


    def attend_back(i, n):
        first, wide, at = reach[i]
        query_rows = slice(i * QB, (i + 1) * QB)
        key_rows = slice(first, first + wide)
        tile = tile_of(n)
        keys = k_s[key_rows, tile]
        query = head_of(q_s[query_rows, tile], n)
        d_out = head_of(d_mixed[query_rows, tile], n)
        scores = jnp.minimum(dot_nt(keys, query), cap[at : at + wide, :])
        probs = jnp.exp(scores - logsum[n : n + 1, query_rows])
        d_probs = dot_nt(v_s[key_rows, tile], d_out)
        centre = jnp.sum(probs * d_probs, 0, keepdims=True)
        d_scores = (probs * (d_probs - centre)).astype(BF16)
        d_vals[key_rows, tile] += dot(probs.astype(BF16), d_out)
        d_keys[key_rows, tile] += dot(d_scores, query)
        got = dot(k_t[n * HEAD : (n + 1) * HEAD, key_rows], d_scores)
        d_query_t[n * HEAD : (n + 1) * HEAD, query_rows] = (got * HEAD ** (-0.5)).astype(BF16)

    def collect(u):
        low, high = ((0, size), (LANES, pair))[u]

        def one(i, carry):
            where = rows_of(i * QB, QB)
            d_qkv[0][where, low:high] = jnp.transpose(d_query_t[low:high, where].astype(F32)).astype(BF16)
            d_qkv[1][where, low:high] = d_keys[where, low:high].astype(BF16)
            d_qkv[2][where, low:high] = d_vals[where, low:high].astype(BF16)
            return carry

        lax.fori_loop(0, steps, one, 0)

    def grad_qkv(u, m):
        low, high = ((0, size), (LANES, pair))[u]
        for g in range(3):
            got = dot_tn(h_one[:, m * pair : (m + 1) * pair], d_qkv[g][:, low:high]).astype(BF16)
            for s in range(2):
                tile = got[s * size : (s + 1) * size]
                block = (2 * m + s) * 3 + g
                if u == 0:
                    keep(held0, block, tile[:, :LANES], tile[:, LANES:])
                else:
                    keep(held1, block, jnp.concatenate([tile[:, h:LANES], tile[:, LANES : LANES + h]], 1), tile[:, LANES + h :])

    for i in range(steps):
        for n in other_heads:
            attend_back(i, n)
        if i == 1:
            merge_x(3)
    collect(1)
    for m in range(width // pair):
        grad_qkv(1, m)
        if m == 0:
            cross_x(6).start()
    grad_out()
    merge_x(4)
    cross_x(7).start()
    for i in range(steps):
        for n in own_heads:
            attend_back(i, n)
        if i == 1:
            cross_x(5).start()
        if i == 2:
            merge_x(6)
    merge_x(7)
    collect(0)
    for i in range(steps):
        swap(send_a, recv_a, sa, ra, i, QB).wait_send()

    def make_d_one(i, carry):
        where = rows_of(i * QB, QB)
        total = sum(dot_nt(d_qkv[g][where, :], w_qkv[:, g * pair : (g + 1) * pair]) for g in range(3))
        send_a[where, :] = total.astype(BF16)
        swap(send_a, recv_a, sd, rd, i, QB).start()
        return tuple(carry[g] + column_sum(d_qkv[g][where, :].astype(F32)) for g in range(3))

    d_bias = lax.fori_loop(0, steps, make_d_one, (jnp.zeros((1, pair), F32),) * 3)
    merge_x(5)
    for u in range(2):
        row = pl.ds(6 + (y if u == 0 else 1 - y), 1)
        parts = [d_bias[g][:, u * size : (u + 1) * size] for g in range(3)] + [bias_sum[0:1, u * hidden_t : (u + 1) * hidden_t]]
        spare = vectors.shape[1] - split.shape[1]
        vectors[row, :] = jnp.concatenate(parts + [jnp.zeros((1, spare), F32)] * (spare > 0), 1)

    for m in range(width // pair):
        grad_qkv(0, m)
    for n in range(fold // 2):
        grad_proj(0, n)
    for m in range(width // pair):
        grad_fc(0, m)

    def norm_one_back(i, carry):
        d_gain, d_shift = carry
        where = rows_of(i * LN_ROWS, LN_ROWS)
        d_norm = send_a[where, :].astype(F32) + recv_a[where, :].astype(F32)
        back, hat = norm_back(x[where, :].astype(F32), d_norm, gain1)
        recv_a[where, :] = (second[where, :] + back).astype(BF16)
        return d_gain + column_sum(d_norm * hat), d_shift + column_sum(d_norm)

    for i in range(steps):
        swap(send_a, recv_a, sd, rd, i, QB).wait_recv()
    sums = lax.fori_loop(0, count // LN_ROWS, norm_one_back, (zero,) * 2)
    for k, row in enumerate(sums):
        vectors[k : k + 1, :width] = row

    keep_in = pltpu.make_async_copy(recv_a, in_own, sem_out.at[1])
    keep_in.start()

    here = b * 2 + y
    same_core = [item for item in plane if item[0] % 2 == 0]

    def vec_copy(k, dev, slot):
        return remote(vectors, vec_plane.at[slot], s_v.at[k], r_v.at[slot], dev)

    def vec_copy_z(k, at, slot):
        return remote(vec_out, vec_line.at[slot], s_vz.at[k], r_vz.at[slot], device(at, b, y, c))

    for k, dev, _ in same_core:
        vec_copy(k, dev, here).start()
    vec_plane[here] = vectors[...]

    for k in range(len(groups)):
        merge_y(k)
    if line * PAIR * slots > blocks:
        held0[blocks] = jnp.zeros(held0.shape[1:], BF16)
    for k, group in enumerate(groups):
        cross_y(k).wait_send()
        if group[0] > 0:
            cross_x(k).wait_send()

    pl.semaphore_signal(ready.at[0], inc=1, device_id=x_dev, device_id_type=MESH)

    @pl.when(a < line - 1)
    def _():
        pl.semaphore_signal(ready.at[1], inc=1, device_id=right, device_id_type=MESH)

    @pl.when(a > 0)
    def _():
        pl.semaphore_signal(ready.at[2], inc=1, device_id=left, device_id_type=MESH)

    def dest(k):
        return sum(jnp.where(a == p, hand_on(line, p)[k], 0) for p in range(line))

    def fill(at):
        def one(n, carry):
            spot = at * PAIR * slots + n
            held1[spot] = held0[where_from[spot, 0]]
            return carry

        lax.fori_loop(0, PAIR * slots, one, 0)

    def run(ref, at):
        return ref.at[pl.ds(at * slots, slots)]

    def copy_x(at):
        return remote(span(held1, at, ob, 0, slots), run(from_y, at), sfx.at[at], rfx.at[at], x_dev)

    def copy_z(at, side, dev):
        return remote(span(held1, at, b, 0, slots), run(from_x, at + 1 - side), sfz.at[at], rfz.at[at + 1 - side], dev)

    def add(at, other, spot):
        merge(held1, (at * PAIR + b) * slots, other, spot * slots, slots)

    half = count // 2
    own_half = rows_of(c * half, half)

    def copy_act(k):
        src, dst = ((recv_b, out_other), (recv_a, in_other))[k]
        return remote(src.at[own_half], dst.at[own_half], s_in.at[k], r_in.at[k], y_dev)

    def share_act(k):
        dst = (out_other, in_other)[k]
        return remote(dst.at[own_half], dst.at[own_half], s_sh.at[k], r_sh.at[k], partner)

    def first_step(k):
        at = dest(k)
        fill(at)
        if k == 0:
            pl.semaphore_wait(ready.at[0], 1)
        copy_x(at).start()

    def second_step(k):
        at = dest(k)
        copy_x(at).wait_recv()
        add(at, from_y, at)

    def pass_on(turn):
        down = turn - line + a

        @pl.when((down >= 0) & (down < a))
        def _():
            @pl.when(a < line - 1)
            def _():
                copy_z(down, 1, left).wait_recv()
                add(down, from_x, down)

            copy_z(down, 1, left).start()

        upw = line - turn + a

        @pl.when((upw > a) & (upw < line))
        def _():
            @pl.when(a > 0)
            def _():
                copy_z(upw, 0, right).wait_recv()
                add(upw, from_x, upw + 1)

            copy_z(upw, 0, right).start()

    first_step(0)
    for k in range(2):
        copy_act(k).start()

    @pl.when(a > 0)
    def _():
        pl.semaphore_wait(ready.at[1], 1)

    @pl.when(a < line - 1)
    def _():
        pl.semaphore_wait(ready.at[2], 1)

    for step in range(1, line + 1):
        if step < line:
            first_step(step)
        if step == 1:
            for k, dev, slot in same_core:
                vec_copy(k, dev, slot // 2).wait()
            vec_out[...] = vec_plane[0] + vec_plane[1] + vec_plane[2] + vec_plane[3]
            for k, at in planes:
                vec_copy_z(k, at, a).start()
            vec_line[a] = vec_out[...]
        second_step(step - 1)
        if step < line:
            pass_on(step)

    for k, at in planes:
        vec_copy_z(k, at, at).wait()
    vec_sum = vec_line[0]
    for p in range(1, line):
        vec_sum = vec_sum + vec_line[p]
    vec_out[...] = vec_sum

    @pl.when(a > 0)
    def _():
        copy_z(a, 0, right).wait_recv()

    @pl.when(a < line - 1)
    def _():
        copy_z(a, 1, left).wait_recv()

    def finish(n, carry):
        value = held1[(a * PAIR + b) * slots + n].astype(F32)
        value += jnp.where(a > 0, from_x[(a + 1) * slots + n].astype(F32), 0.0)
        value += jnp.where(a < line - 1, from_x[a * slots + n].astype(F32), 0.0)
        total_out[n] = value
        return carry + jnp.sum((value * value).reshape(-1, 8, LANES), 0)

    square = lax.fori_loop(0, slots, finish, jnp.zeros((8, LANES), F32))
    chips = line * PAIR * 2
    row = lax.broadcasted_iota(jnp.int32, (8, LANES), 0)
    weight = jnp.where(row < 6, 1.0 / (chips * CORES), 1.0 / chips)
    for k in range(vec_sum.shape[1] // LANES):
        tile = vec_sum[:, k * LANES : (k + 1) * LANES]
        square += weight * tile * tile
    square_out[...] = square

    def sq_copy(k, dev, slot):
        return remote(square_out, sq_plane.at[slot], s_q.at[k], r_q.at[slot], dev)

    me = here * 2 + c
    for k, dev, _ in plane:
        sq_copy(k, dev, me).start()
    sq_plane[me] = square

    for k in range(2):
        copy_act(k).wait_recv()
        share_act(k).start()

    for k, dev, slot in plane:
        sq_copy(k, dev, slot).wait()
    square = sq_plane[0]
    for k in range(1, 8):
        square = square + sq_plane[k]
    square_out[...] = square

    def sq_copy_z(k, at, slot):
        return remote(square_out, sq_line.at[slot], s_qz.at[k], r_qz.at[slot], device(at, b, y, c))

    for k, at in planes:
        sq_copy_z(k, at, a).start()
    sq_line[a] = square

    for k in range(2):
        share_act(k).wait()
        copy_act(k).wait_send()
    for m in range(count // MLP_ROWS):
        swap(send_b, recv_b, sb, rb, m, MLP_ROWS).wait_send()
        swap(send_c, recv_c, sc, rc, m, MLP_ROWS).wait_send()
    for i in range(steps):
        swap(send_a, recv_a, sd, rd, i, QB).wait_send()
    keep_out.wait()
    keep_in.wait()

    def gone(at, carry):
        copy_x(at).wait_send()

        @pl.when(at != a)
        def _():
            copy_z(at, 0, right).wait_send()

        return carry

    lax.fori_loop(0, line, gone, 0)
    for k, at in planes:
        sq_copy_z(k, at, at).wait()
    square = sq_line[0]
    for p in range(1, line):
        square = square + sq_line[p]
    square_out[...] = square


def layer(table, tokens, segments, cotangent, master, shared, split, line):
    _, count, width = tokens.shape
    _, slots, size, _ = master.shape
    pair = 2 * size
    total = line * PAIR * slots
    hidden = 2 * (split.shape[1] - 3 * size)
    blocks = table.shape[1]
    steps = count // QB
    halves = count // MLP_ROWS
    spans = sum((i + 1 - max(0, i - 2)) * QB for i in range(steps))
    wide_vec = -(-split.shape[1] // LANES) * LANES
    direct = width // size
    x_blocks = (blocks - direct) // 2
    y_blocks = direct + x_blocks
    vm = lambda shape, kind=BF16: pltpu.VMEM(shape, kind)
    dma = lambda *n: pltpu.SemaphoreType.DMA(n)
    anywhere = pl.BlockSpec(memory_space=pl.ANY)
    inside = pl.BlockSpec(memory_space=pltpu.VMEM)
    scalars = pl.BlockSpec(memory_space=pltpu.SMEM)
    act = (count, width)
    block = (packed_rows(size), LANES)
    vec = (8, wide_vec)
    S = jax.ShapeDtypeStruct
    return pl.pallas_call(
        functools.partial(layer_kernel, (size, width, count, line, slots)),
        out_shape=(S((slots,) + block, F32), S(vec, F32), S((8, LANES), F32)) + (S(act, BF16),) * 4,
        in_specs=[scalars, anywhere, anywhere, inside, anywhere, anywhere, inside, inside, anywhere, inside],
        out_specs=(inside, inside, inside) + (anywhere,) * 4,
        scratch_shapes=[
            vm(act),
            vm(act),
            vm((slots, size, size), F32),
            vm((total,) + block),
            vm((total,) + block),
            vm((max(x_blocks, (line + 1) * slots),) + block),
            vm((max(y_blocks, line * slots),) + block),
            pltpu.SMEM((1, blocks), jnp.int32),
            vm(split.shape, F32),
            vm((total, LANES), jnp.int32),
            pltpu.SMEM((total, LANES), jnp.int32),
            vm((width, 3 * pair)),
            vm((pair, width)),
            vm((width, hidden)),
            vm((hidden, width)),
            vm((spans, QB), F32),
            vm(act),
            vm((count, pair)),
            vm((count, pair)),
            vm((count, pair)),
            vm((pair, count)),
            vm((pair, count)),
            vm((pair, count)),
            vm((8, count), F32),
            vm(act),
            vm(act),
            vm(act),
            vm(act),
            vm(act),
            vm(act),
            vm(act, F32),
            vm(act),
            vm((count, hidden)),
            vm((count, hidden)),
            vm((count, pair), F32),
            vm((count, pair), F32),
            vm((pair, count)),
            vm((8, 3 * pair), F32),
            vm((16, hidden), F32),
            vm(vec, F32),
            vm((4,) + vec, F32),
            vm((line,) + vec, F32),
            vm((8, 8, LANES), F32),
            vm((line, 8, LANES), F32),
            dma(4),
            dma(2),
        ]
        + [dma(line)] * 11
        + [dma(1), dma(1)]
        + [dma(2, line)] * 3
        + [dma(2), dma(2)]
        + [dma(steps), dma(steps), dma(halves), dma(halves), dma(halves), dma(halves), dma(steps), dma(steps)]
        + [dma(8)] * 4
        + [pltpu.SemaphoreType.REGULAR((3,)), dma(line), dma(line), dma(line), dma(line + 1)]
        + [dma(8), dma(4), dma(line), dma(line), dma(8), dma(8), dma(line), dma(line), dma(2), dma(2), dma(2), dma(2)],
        compiler_params=pltpu.CompilerParams(collective_id=2, has_side_effects=True, vmem_limit_bytes=63 * MIB),
        name="layer",
    )(table, table, tokens, segments, cotangent, master, shared, split, split, table)


def halves_of(value):
    high = value.astype(BF16)
    return high, (value - high.astype(F32)).astype(BF16)


def fine_dot(a, b):
    a_high, a_low = halves_of(a)
    b_high, b_low = halves_of(b)
    return dot(a_high, b_high) + (dot(a_high, b_low) + dot(a_low, b_high))


def update_kernel(
    grad,
    square,
    vec,
    master,
    stats,
    roots,
    shared,
    shared_state,
    split,
    split_state,
    out_mine,
    out_theirs,
    in_mine,
    in_theirs,
    norm_out,
    clipped_out,
    master_out,
    copy_out,
    stats_out,
    shared_grad,
    shared_new_state,
    shared_new,
    split_grad,
    split_new_state,
    split_new,
    output,
    input_grad,
    acts,
    wide,
    grad_v,
    master_v,
    stats_v,
    roots_v,
    clipped_v,
    copy_v,
    sem_act,
    sem_wide,
    sem_in,
    sem_out,
):
    slots, size = master.shape[1], master.shape[2]
    y = lax.axis_index("tensor") // CORES
    _, count, _ = acts.shape
    chunk = count // 4
    fetch = []
    for k, ref in enumerate((out_mine, out_theirs, in_mine, in_theirs)):
        fetch.append(pltpu.make_async_copy(ref, acts.at[k], sem_act.at[k]))

    def slot_loads(n):
        return [
            pltpu.make_async_copy(src.at[n], dst.at[n], sem_in.at[k, n])
            for k, (src, dst) in enumerate(
                ((grad, grad_v), (roots.at[0], roots_v), (stats.at[0], stats_v), (master.at[0], master_v))
            )
        ]

    for n in range(slots):
        for copy in slot_loads(n):
            copy.start()
    for copy in fetch:
        copy.start()

    def wide_copy(k, n):
        target = (output, output, input_grad, input_grad)[k]
        seq = y if k % 2 == 0 else 1 - y
        rows = rows_of(n * chunk, chunk)
        return pltpu.make_async_copy(wide.at[k, rows], target.at[seq, rows], sem_wide.at[k, n])

    def widen(k):
        fetch[k].wait()

        def one(n, carry):
            rows = rows_of(n * chunk, chunk)
            wide[k, rows, :] = acts[k, rows, :].astype(F32)
            wide_copy(k, n).start()
            return carry

        lax.fori_loop(0, 4, one, 0)

    norm = jnp.sqrt(jnp.sum(square[...], keepdims=True))
    factor = 1.0 / jnp.maximum(norm, 1.0)
    norm_out[...] = norm
    def slot_copies(n):
        return [
            pltpu.make_async_copy(src.at[n], dst.at[0, n], sem_out.at[k, n])
            for k, (src, dst) in enumerate(
                ((clipped_v, clipped_out), (master_v, master_out), (copy_v, copy_out), (stats_v, stats_out))
            )
        ]

    def slot(n, carry):
        for copy in slot_loads(n):
            copy.wait()
        clipped = jnp.concatenate(unpack_block(grad_v[n] * factor, size), 1)
        clipped_v[n] = clipped
        low = clipped.astype(BF16)
        stats_v[n, 0] = DECAY * stats_v[n, 0] + (1.0 - DECAY) * dot_nt(low, low)
        stats_v[n, 1] = DECAY * stats_v[n, 1] + (1.0 - DECAY) * dot_tn(low, low)
        step = fine_dot(fine_dot(roots_v[n, 0], clipped), roots_v[n, 1])
        new = master_v[n] - RATE * step
        master_v[n] = new
        copy_v[n] = new.astype(BF16)
        for copy in slot_copies(n):
            copy.start()
        return carry

    early = slots // 2
    lax.fori_loop(0, early, slot, 0, unroll=True)
    widen(0)
    widen(1)
    lax.fori_loop(early, slots, slot, 0, unroll=True)
    for k in range(2, 4):
        widen(k)
    for raw, value, state, g_out, s_out, v_out in (
        (vec[0 : shared.shape[0], : shared.shape[1]], shared, shared_state, shared_grad, shared_new_state, shared_new),
        (vec[pl.ds(6 + y, 1), :][:, : split.shape[1]], split, split_state, split_grad, split_new_state, split_new),
    ):
        g = raw * factor
        moment = DECAY * state[...] + (1.0 - DECAY) * g * g
        g_out[...] = g
        s_out[...] = moment
        v_out[...] = value[...] - RATE_VECTOR * g * lax.rsqrt(moment)

    def done(n, carry):
        for copy in slot_copies(n):
            copy.wait()
        return carry

    lax.fori_loop(0, slots, done, 0)
    for k in range(4):
        for n in range(4):
            wide_copy(k, n).wait()


def update(grad, square, vec, master, stats, roots, shared, shared_state, split, split_state, acts):
    _, slots, size, _ = master.shape
    count, width = acts[0].shape
    anywhere = pl.BlockSpec(memory_space=pl.ANY)
    inside = pl.BlockSpec(memory_space=pltpu.VMEM)
    S = jax.ShapeDtypeStruct
    vm = lambda shape, kind=F32: pltpu.VMEM(shape, kind)
    dma = lambda *n: pltpu.SemaphoreType.DMA(n)
    return pl.pallas_call(
        update_kernel,
        out_shape=(S((1, 1), F32), S(master.shape, F32), S(master.shape, F32), S(master.shape, BF16), S(stats.shape, F32))
        + (S(shared.shape, F32),) * 3
        + (S(split.shape, F32),) * 3
        + (S((2, count, width), F32),) * 2,
        in_specs=[anywhere, inside, inside] + [anywhere] * 3 + [inside] * 4 + [anywhere] * 4,
        out_specs=(inside,) + (anywhere,) * 4 + (inside,) * 6 + (anywhere,) * 2,
        scratch_shapes=[
            vm((4, count, width), BF16),
            vm((4, count, width)),
            vm(grad.shape),
            vm((slots, size, size)),
            vm((slots, 2, size, size)),
            vm((slots, 2, size, size)),
            vm((slots, size, size)),
            vm((slots, size, size), BF16),
            dma(4),
            dma(4, 4),
            dma(4, slots),
            dma(4, slots),
        ],
        compiler_params=pltpu.CompilerParams(vmem_limit_bytes=63 * MIB),
        name="update",
    )(grad, square, vec, master, stats, roots, shared, shared_state, split, split_state, *acts)


def body(
    tokens,
    segments,
    cotangent,
    block_owner_slots,
    master_weights,
    statistics,
    inverse_roots,
    shared_vectors,
    shared_state,
    split_bias,
    split_state,
):
    line = lax.axis_size("dp") // PAIR
    grad, vec, square, out, out_other, d_in, d_in_other = layer(
        block_owner_slots, tokens, segments, cotangent, master_weights, shared_vectors, split_bias, line
    )
    done = update(
        grad,
        square,
        vec,
        master_weights,
        statistics,
        inverse_roots,
        shared_vectors,
        shared_state,
        split_bias,
        split_state,
        (out, out_other, d_in, d_in_other),
    )
    return (done[11], done[12], done[0].reshape(())) + tuple(done[1:11])


def solution(mesh):
    placed = (
        P("dp", None, None),
        P("dp", None),
        P("dp", None, None),
        P("tensor", None),
        P("tensor", "dp", None, None),
        P("tensor", "dp", None, None, None),
        P("tensor", "dp", None, None, None),
        P(),
        P(),
        P("tensor", None),
        P("tensor", None),
    )
    return jax.shard_map(
        body,
        mesh=mesh,
        in_specs=placed,
        out_specs=(
            P("dp", None, None),
            P("dp", None, None),
            P(),
            P("tensor", "dp", None, None),
            P("tensor", "dp", None, None),
            P("tensor", "dp", None, None),
            P("tensor", "dp", None, None, None),
            P(),
            P(),
            P(),
            P("tensor", None),
            P("tensor", None),
            P("tensor", None),
        ),
        check_vma=False,
    )
```
